32 devices in a mesh: seq: 4 (over y, x), fsdp: 8 (over z, core).
Axes of the slice: x: 2, y: 2, z: 4, core: 2. Of those that a mesh axis runs over, the one named last changes fastest.
Arguments:
- tokens: bfloat16 [8, 1536, 2048], P('fsdp', 'seq'), may hold values from -6 to 6
- lengths: int32 [8, 3], P('fsdp'), may hold values from 1 to 1536, as said below
- routes: int32 [8, 1536, 8], P('fsdp', 'seq'), may hold values from 0 to 31, all different within a row; in each aligned block of 384 rows (0 to 383, 384 to 767, ..., all dimensions but the last counted through in order) at most 130 rows name the same one
- gates: float32 [8, 1536, 8], P('fsdp', 'seq'), may hold values from 0.06 to 0.25
- gain_attn: bfloat16 [2048], P('fsdp'), may hold values from 0.5 to 1.5
- gain_moe: bfloat16 [2048], P('fsdp'), may hold values from 0.5 to 1.5
- w_qkv: bfloat16 [2048, 6144], P('fsdp'), may hold values from -0.1875 to 0.1875
- w_out: bfloat16 [2048, 2048], P('fsdp'), may hold values from -0.5 to 0.5
- w_gate_up: bfloat16 [32, 2048, 2, 1024], P('seq', 'fsdp'), may hold values from -0.125 to 0.125
- w_down: bfloat16 [32, 1024, 2048], P('seq', None, 'fsdp'), may hold values from -0.75 to 0.75
- cotangent: bfloat16 [8, 1536, 2048], P('fsdp', 'seq'), may hold values from -6 to 6
Outputs:
- mixed: bfloat16 [8, 1536, 2048], P('fsdp', 'seq')
- grad_tokens: bfloat16 [8, 1536, 2048], P('fsdp', 'seq')
- grad_gain_attn: float32 [2048], P('fsdp')
- grad_gain_moe: float32 [2048], P('fsdp')
- grad_qkv: float32 [2048, 6144], P('fsdp')
- grad_out: float32 [2048, 2048], P('fsdp')
- grad_gate_up: float32 [32, 2048, 2, 1024], P('seq', 'fsdp')
- grad_down: float32 [32, 1024, 2048], P('seq', None, 'fsdp')
The draws below stay inside these ranges and needn't reach their ends.
Inputs may be any that keep to these rules, and one draw needn't show every extreme that they name: `routes`: in the positions of one device no expert is named by more than 130 rows; the 8 experts of a position differ. Each group's lengths sum to 1536 or less; the first sequence of each group is packed first and has at least 1392 positions; the rest of the group is padding.
All inputs are finite; a program needn't handle non-finite values.
Results may differ from the reference program's by a relative error of at most 0.022.
Values may be sent and summed in bfloat16 or wider, within the bound.
A program may use at most 448 MiB of HBM per device.

```python
import math
import jax
import jax.numpy as jnp
import numpy as np
from jax import lax

D = 2048
HEADS = 16
HEAD = 128
FFE = 1024
TOP = 8
SEQS = 3
EXPERTS = 32
SEQ_TOK = 1536
ROWS = 384
GROUPS = 8
CAP = 130
N_SEQ = 4


def draw_lengths(key, part):
    key = jax.random.fold_in(key, 11)
    key_short, key_pad = jax.random.split(key)
    unit_len = max(1, SEQ_TOK // 32)
    shorter = jax.random.randint(key_short, (GROUPS, SEQS - 1), 1, unit_len + 1)
    padding = jax.random.randint(key_pad, (GROUPS, 1), 0, unit_len + 1)
    longest = SEQ_TOK - padding - jnp.sum(shorter, axis=1, keepdims=True)
    return jnp.concatenate([longest, shorter], axis=1).astype(jnp.int32)


def level_of(own_key, shape, cuts, smallest, largest):
    factor_of = 1.0
    for dim, shards_of in cuts:
        steps = jax.random.uniform(jax.random.fold_in(jax.random.fold_in(own_key, 6), dim), (shards_of,), jnp.float32, smallest / len(cuts), largest / len(cuts))
        factor_of = factor_of * jnp.repeat(jnp.exp(steps), shape[dim] // shards_of).reshape((-1,) + (1,) * (len(shape) - 1 - dim))
    return factor_of


def assign_block(rng, own, number, rows, count, top, bound, skew):
    ranking = jax.random.permutation(rng, count)
    crowded, common = portions_of(count, rows * top, bound, skew, True), portions_of(count, rows * top, bound, skew, False)
    places = jnp.arange(count)

    def named(tallies, rotation):
        used = int((tallies > 0).sum())
        fixed = max(1, used // 4)
        moved = fixed + (places - fixed + rotation * (used - fixed)) % max(1, count - fixed)
        return jnp.zeros((count,), jnp.int32).at[ranking[jnp.where(places < fixed, places, moved)]].set(jnp.asarray(tallies, jnp.int32))

    tallies = jnp.where(number % 4 == 0, named(crowded, number // 4), named(common, number - number // 4 - 1))
    mixed = jax.random.permutation(jax.random.fold_in(own, 3), count)
    donor, receiver = mixed[0:count // 2 * 2:2], mixed[1:count // 2 * 2:2]
    slack = jnp.minimum(tallies[donor] - 1, bound - tallies[receiver]) // 2
    slack = jnp.where((donor == ranking[0]) | (receiver == ranking[0]) | (tallies[receiver] == 0), 0, jnp.maximum(slack, 0))
    moved = jax.random.randint(jax.random.fold_in(own, 4), (count // 2,), 0, 1 << 20) % (slack + 1)
    tallies = tallies.at[donor].add(-moved).at[receiver].add(moved)
    labels = jnp.searchsorted(jnp.cumsum(tallies), jnp.arange(rows * top), side="right").astype(jnp.int32)
    table = labels.reshape(top, rows).T
    table = table[jax.random.permutation(jax.random.fold_in(own, 1), rows)]
    rotation = jax.random.randint(jax.random.fold_in(own, 2), (rows, 1), 0, top)
    return jnp.take_along_axis(table, (jnp.arange(top)[None, :] + rotation) % top, axis=1)


def portions_of(count, total, reach, lean, full):
    weights = [(1 << 20) // math.isqrt(grade ** lean) + 1 for grade in range(1, count + 1)]
    largest = reach if full else min(reach, max(-(-total // count), total * weights[0] // sum(weights)))
    least = 1 if total - largest >= count - 1 else 0
    counts, surplus = [largest] + [least] * (count - 1), total - largest - least * (count - 1)
    while surplus > 0:
        candidates = [i for i in range(1, count) if counts[i] < largest] or [i for i in range(1, count) if counts[i] < reach]
        whole, left = sum([weights[i] for i in candidates]), surplus
        for i in candidates:
            extra = min(reach - counts[i], max(1, left * weights[i] // whole), surplus)
            counts[i] = counts[i] + extra
            surplus = surplus - extra
    return np.array(counts)


def centred(stream_key, extent, spread, bound, cuts=(), held_as=jnp.bfloat16):
    array = spread * jax.random.normal(stream_key, extent, jnp.float32)
    if cuts:
        array = array * level_of(stream_key, extent, cuts, -0.22, 0.18)
    return jnp.clip(array, -bound, bound).astype(held_as)


def setup_inputs(seed: int = 0) -> dict:
    keys = jax.random.split(jax.random.key(seed), 12)
    tokens = centred(keys[0], (GROUPS, SEQ_TOK, D), 1.0, 6.0, ((0, 8), (1, 4)))
    lengths = draw_lengths(jax.random.fold_in(keys[11], 71), 0)
    routes_keys = jax.random.split(jax.random.fold_in(keys[2], 1), GROUPS * SEQ_TOK // ROWS)
    routes_turns = jax.random.permutation(jax.random.fold_in(keys[2], 3), GROUPS * SEQ_TOK // ROWS)
    routes = jax.vmap(lambda own, number: assign_block(jax.random.fold_in(keys[2], 2), own, number, ROWS, EXPERTS, TOP, CAP, 1))(routes_keys, routes_turns).reshape((GROUPS, SEQ_TOK, TOP))
    gates = jnp.clip(jnp.exp(math.log(0.25) - 1.4271164 * jax.random.uniform(keys[3], (GROUPS, SEQ_TOK, TOP), jnp.float32) ** level_of(keys[3], (GROUPS, SEQ_TOK, TOP), ((0, 8), (1, 4)), -0.2, 0.2)), 0.06, 0.25)
    gain_attn = jnp.clip(1.0 + 0.1 * jax.random.normal(keys[4], (D,), jnp.float32), 0.5, 1.5).astype(jnp.bfloat16)
    gain_moe = jnp.clip(1.0 + 0.1 * jax.random.normal(keys[5], (D,), jnp.float32), 0.5, 1.5).astype(jnp.bfloat16)
    w_qkv = centred(keys[6], (D, 3 * D), (D // 2) ** -0.5, 0.1875, ((0, 8),))
    w_out = centred(keys[7], (D, D), (D // 16) ** -0.5, 0.5, ((0, 8),))
    w_gate_up = centred(keys[8], (EXPERTS, D, 2, FFE), D ** -0.5, 0.125, ((0, 4), (1, 8)))
    w_down = centred(keys[9], (EXPERTS, FFE, D), (FFE // 16) ** -0.5, 0.75, ((0, 4), (2, 8)))
    cotangent = centred(keys[10], (GROUPS, SEQ_TOK, D), 1.0, 6.0, ((0, 8), (1, 4)))
    return dict(tokens=tokens, lengths=lengths, routes=routes, gates=gates, gain_attn=gain_attn, gain_moe=gain_moe, w_qkv=w_qkv, w_out=w_out, w_gate_up=w_gate_up, w_down=w_down, cotangent=cotangent)


@jax.custom_vjp
def low(v):
    return lax.optimization_barrier(v.astype(jnp.bfloat16)).astype(jnp.float32)

@jax.custom_vjp
def low_back(v):
    return v

def low_keep(v):
    return (low(v), None)

def low_pass(kept, grad):
    return (grad,)

def back_keep(v):
    return (v, None)

def back_low(kept, grad):
    return (low(grad),)
low.defvjp(low_keep, low_pass)
low_back.defvjp(back_keep, back_low)
epsilon = 1e-06
highest = lax.Precision.HIGHEST

def norm_rows(values, gain):
    return values * lax.rsqrt(lax.optimization_barrier(jnp.mean(values * values, axis=-1, keepdims=True)) + epsilon) * gain

def slot_table(routing, weight):
    flat_route = routing.reshape(-1)
    onehot = (flat_route[:, None] == jnp.arange(EXPERTS, dtype=jnp.int32)[None, :]).astype(jnp.int32)
    slot_rank = lax.optimization_barrier(jnp.sum((jnp.cumsum(onehot, axis=0) - onehot) * onehot, axis=1)).astype(jnp.int32)
    owner = (jnp.arange(flat_route.shape[0], dtype=jnp.int32) // TOP).astype(jnp.int32)
    depth = N_SEQ * CAP
    table = jnp.zeros((EXPERTS, depth), jnp.int32).at[flat_route, slot_rank].set(owner)
    share = jnp.zeros((EXPERTS, depth), jnp.float32).at[flat_route, slot_rank].set(weight.reshape(-1))
    return (table, share)

def group_forward(params, inputs):
    gain_a, gain_m, w_qkv, w_out, w_gate_up, w_down = params
    x_group, segment, table, share = inputs
    span_len = x_group.shape[0]
    normed_a = low(norm_rows(x_group, gain_a))
    qkv = low_back(low(jnp.dot(normed_a, w_qkv, precision=highest)))
    qkv = qkv.reshape(span_len, 3, HEADS, HEAD)
    scores = jnp.einsum('qhd,khd->hqk', qkv[:, 0], qkv[:, 1], precision=highest)
    scores = low_back(scores * HEAD ** (-0.5))
    scores = jnp.where(segment[None, :, None] == segment[None, None, :], scores, -1e+30)
    prob_b = low(jax.nn.softmax(scores, axis=-1))
    heads_now = jnp.einsum('hqk,khd->qhd', prob_b, qkv[:, 2], precision=highest)
    heads_now = low_back(low(heads_now)).reshape(span_len, D)
    resid = x_group + low_back(jnp.dot(heads_now, w_out, precision=highest))
    normed_m = low(norm_rows(resid, gain_m))

    def expert(inputs_e):
        index_rows, gate_up, down_proj = inputs_e
        x_slots = low_back(normed_m[index_rows])
        proj = low_back(jnp.dot(x_slots, gate_up.reshape(D, 2 * FFE), precision=highest)).reshape(-1, 2, FFE)
        act = low(jax.nn.silu(proj[:, 0]) * proj[:, 1])
        return low_back(low(jnp.dot(act, down_proj, precision=highest)))
    produced = lax.map(jax.checkpoint(expert), (table, w_gate_up, w_down))
    moe = jnp.zeros((span_len, D), jnp.float32).at[table.reshape(-1)].add((share[:, :, None] * produced).reshape(-1, D))
    return resid + moe

def reference(tokens, lengths, routes, gates, gain_attn, gain_moe, w_qkv, w_out, w_gate_up, w_down, cotangent):
    ends = jnp.cumsum(lengths, axis=1).astype(jnp.int32)
    places = jnp.arange(SEQ_TOK, dtype=jnp.int32)
    segment = lax.optimization_barrier(jnp.sum((places[None, :, None] >= ends[:, None, :]).astype(jnp.int32), axis=-1)).astype(jnp.int32)
    table, share = jax.vmap(slot_table)(routes, gates)
    params = (gain_attn.astype(jnp.float32), gain_moe.astype(jnp.float32), w_qkv.astype(jnp.float32), w_out.astype(jnp.float32), w_gate_up.astype(jnp.float32), w_down.astype(jnp.float32))

    def whole(x_all, weights):

        def one_group(inputs):
            return group_forward(weights, inputs)
        return lax.map(jax.checkpoint(one_group), (x_all, segment, table, share))
    result, pullback = jax.vjp(whole, tokens.astype(jnp.float32), params)
    grad_x, grads = pullback(cotangent.astype(jnp.float32))
    return (result.astype(jnp.bfloat16), grad_x.astype(jnp.bfloat16), grads[0], grads[1], grads[2], grads[3], grads[4], grads[5])
```

```python
import jax
import jax.numpy as jnp
from jax import lax
from jax.sharding import PartitionSpec as P

D = 2048
HEADS = 16
HEAD = 128
FFE = 1024
TOP = 8

epsilon = 1e-06
f32 = jnp.float32
bf16 = jnp.bfloat16


def swap(value, axis, bit):
    size = lax.axis_size(axis)
    return lax.ppermute(value, axis, [(i, i ^ bit) for i in range(size)])


def dot(a, b, contract, batch=((), ())):
    return lax.dot_general(a, b, (contract, batch), preferred_element_type=f32)


def segment_ids(length_row, span_len):
    ends = jnp.cumsum(length_row)
    places = lax.iota(jnp.int32, span_len)
    return jnp.sum((places[:, None] >= ends[None, :]).astype(jnp.int32), axis=1)


def attend_forward(queries, key_rows, values, segment, block_len):
    span_len, heads_now, head_dim = queries.shape
    score_scale = head_dim ** (-0.5)

    def one_block(row_start):
        q_block = lax.dynamic_slice_in_dim(queries, row_start, block_len, 0)
        seg_block = lax.dynamic_slice_in_dim(segment, row_start, block_len, 0)
        scores = (
            jnp.einsum("qhd,khd->hqk", q_block, key_rows, preferred_element_type=f32)
            * score_scale
        )
        scores = jnp.where(seg_block[None, :, None] == segment[None, None, :], scores, -1e30)
        row_max = jnp.max(scores, axis=2, keepdims=True)
        exp_part = jnp.exp(scores - row_max)
        row_sum = jnp.sum(exp_part, axis=2, keepdims=True)
        prob_b = (exp_part / row_sum).astype(bf16)
        out_block = jnp.einsum("hqk,khd->qhd", prob_b, values, preferred_element_type=f32)
        return (out_block.astype(bf16), (row_max + jnp.log(row_sum))[:, :, 0])

    starts = jnp.arange(span_len // block_len, dtype=jnp.int32) * block_len
    outputs, log_total = lax.map(one_block, starts)
    log_total = jnp.transpose(log_total, (1, 0, 2)).reshape(heads_now, span_len)
    return (outputs.reshape(span_len, heads_now, head_dim), log_total)


def attend_backward(queries, key_rows, values, segment, log_total, grad_heads, block_len):
    span_len, heads_now, head_dim = queries.shape
    score_scale = head_dim ** (-0.5)

    def one_block(carried, row_start):
        grad_k, grad_v = carried
        q_block = lax.dynamic_slice_in_dim(queries, row_start, block_len, 0)
        seg_block = lax.dynamic_slice_in_dim(segment, row_start, block_len, 0)
        g_block = lax.dynamic_slice_in_dim(grad_heads, row_start, block_len, 0)
        lse_block = lax.dynamic_slice_in_dim(log_total, row_start, block_len, 1)
        scores = (
            jnp.einsum("qhd,khd->hqk", q_block, key_rows, preferred_element_type=f32)
            * score_scale
        )
        scores = jnp.where(seg_block[None, :, None] == segment[None, None, :], scores, -1e30)
        prob_f = jnp.exp(scores - lse_block[:, :, None])
        grad_v = grad_v + jnp.einsum(
            "hqk,qhd->khd", prob_f.astype(bf16), g_block, preferred_element_type=f32
        )
        grad_p = jnp.einsum("qhd,khd->hqk", g_block, values, preferred_element_type=f32)
        inner_sum = jnp.sum(prob_f * grad_p, axis=2, keepdims=True)
        dscore = (prob_f * (grad_p - inner_sum)).astype(bf16)
        grad_q = (
            jnp.einsum("hqk,khd->qhd", dscore, key_rows, preferred_element_type=f32)
            * score_scale
        )
        grad_k = (
            grad_k
            + jnp.einsum("hqk,qhd->khd", dscore, q_block, preferred_element_type=f32)
            * score_scale
        )
        return ((grad_k, grad_v), grad_q)

    zeros_kv = jnp.zeros((span_len, heads_now, head_dim), f32)
    starts = jnp.arange(span_len // block_len, dtype=jnp.int32) * block_len
    (grad_k, grad_v), grad_q = lax.scan(one_block, (zeros_kv, zeros_kv), starts)
    return (grad_q.reshape(span_len, heads_now, head_dim), grad_k, grad_v)


def gather_expert(own, other):
    size = lax.axis_size("fsdp")
    place = lax.axis_index("fsdp")
    rows, columns = own.shape
    bit = size // 2
    piece, sent = own[None], other[None]
    while bit:
        received = swap(sent, "fsdp", bit)
        low = ((place // bit) % 2) == 0
        piece = jnp.stack(
            [jnp.where(low, piece, received), jnp.where(low, received, piece)], axis=1
        ).reshape(-1, rows, columns)
        sent = piece
        bit //= 2
    return piece.reshape(-1, columns)


def scatter_expert(grad):
    size = lax.axis_size("fsdp")
    place = lax.axis_index("fsdp")
    columns = grad.shape[1]
    rows = grad.shape[0] // size
    bit, many = 1, size // 2
    piece = grad.reshape(size, rows, columns)
    while bit < size:
        mine = (place // bit) % 2
        piece = piece.reshape(many, 2, rows, columns)
        kept = lax.dynamic_index_in_dim(piece, mine, 1, keepdims=False)
        received = swap(lax.dynamic_index_in_dim(piece, 1 - mine, 1, keepdims=False), "fsdp", bit)
        if many == 1:
            return kept[0], received[0]
        piece = (kept.astype(f32) + received.astype(f32)).astype(bf16)
        bit *= 2
        many //= 2


def to_group(rows):
    pair = jnp.stack([rows, swap(rows, "fsdp", lax.axis_size("fsdp") // 2)])
    return lax.all_gather(pair, "seq", axis=0, tiled=False)


def from_group(sums):
    rows, width = sums.shape[2:]
    mine = lax.psum_scatter(
        sums.astype(bf16).reshape(-1, width), "seq", scatter_dimension=0, tiled=True
    )
    other = swap(mine[rows:], "fsdp", lax.axis_size("fsdp") // 2)
    return mine[:rows].astype(f32) + other.astype(f32)


def body(
    tokens, lengths, routes, gates, gain_attn, gain_moe, w_qkv, w_out, w_gate_up, w_down, cotangent
):
    n_seq, n_fsdp = lax.axis_size("seq"), lax.axis_size("fsdp")
    at_seq, at_fsdp = lax.axis_index("seq"), lax.axis_index("fsdp")
    rows = tokens.shape[1]
    shard = D // n_fsdp
    local_count = w_gate_up.shape[0]
    per_half = local_count // 2
    half = at_fsdp // (n_fsdp // 2)
    heads_here = HEADS // n_seq
    width = heads_here * HEAD
    span_len = rows * n_seq

    packed = jnp.concatenate(
        [w_gate_up.reshape(local_count, shard, 2 * FFE), jnp.swapaxes(w_down, 1, 2)], axis=2
    )
    own_part = lax.dynamic_slice_in_dim(packed, half * per_half, per_half, 0)
    other_part = lax.dynamic_slice_in_dim(packed, (1 - half) * per_half, per_half, 0)
    experts = [gather_expert(own_part[i], other_part[i]) for i in range(per_half)]

    x_all = lax.all_gather(tokens[0], "seq", axis=0, tiled=True)
    part = lax.dynamic_slice_in_dim(
        w_qkv.reshape(shard, 3, HEADS, HEAD), at_seq * heads_here, heads_here, 2
    ).reshape(shard, 3 * width)
    gains = jnp.zeros((shard, 128), bf16).at[:, 0].set(gain_attn).at[:, 1].set(gain_moe)
    gathered = lax.all_gather(
        jnp.concatenate([part, gains], axis=1), "fsdp", axis=0, tiled=True
    )
    qkv_own = gathered[:, : 3 * width]
    gain_a = gathered[:, 3 * width].astype(f32)
    gain_m = gathered[:, 3 * width + 1].astype(f32)
    out_full = lax.all_gather(w_out, "fsdp", axis=0, tiled=True)

    routing = jnp.concatenate([routes[0].astype(f32), gates[0]], axis=1)
    routing = to_group(routing).reshape(2 * n_seq, rows, 2 * TOP)
    capacity = rows * TOP * 4 // (3 * local_count * n_seq) + 2
    capacity = -(-capacity // 8) * 8
    named = at_seq * local_count + half * per_half + lax.iota(jnp.int32, per_half)
    hits = routing[:, :, :TOP, None].astype(jnp.int32) == named
    mask = jnp.any(hits, axis=2)
    weight = jnp.sum(jnp.where(hits, routing[:, :, TOP:, None], 0.0), axis=2)
    below = (lax.iota(jnp.int32, rows)[:, None] > lax.iota(jnp.int32, rows)[None, :]).astype(bf16)
    rank = jnp.einsum("rq,bqe->bre", below, mask.astype(bf16), preferred_element_type=f32)
    rank = jnp.where(mask, rank.astype(jnp.int32), -1)
    picks = jnp.swapaxes(rank, 1, 2)[:, :, None, :] == lax.iota(jnp.int32, capacity)[:, None]
    share = jnp.sum(
        jnp.where(picks, jnp.swapaxes(weight, 1, 2)[:, :, None, :], 0.0), axis=3
    )
    picks = picks.astype(bf16)
    cot_all = to_group(cotangent[0]).reshape(2 * n_seq, rows, D)

    def normed_rows(values, gain):
        inverse = lax.rsqrt(jnp.mean(values * values, axis=1, keepdims=True) + epsilon)
        return (values * inverse * gain).astype(bf16), inverse

    normed_a, _ = normed_rows(x_all.astype(f32), gain_a)
    qkv = dot(normed_a, qkv_own, ((1,), (0,))).astype(bf16)
    spread = qkv.reshape(span_len, 3, heads_here, HEAD)
    segment = segment_ids(lengths[0], span_len)
    block_len = span_len // 3
    queries, key_rows, values = spread[:, 0], spread[:, 1], spread[:, 2]
    attended, log_total = attend_forward(queries, key_rows, values, segment, block_len)
    heads_rows = lax.all_to_all(
        attended.reshape(span_len, width), "seq", split_axis=0, concat_axis=1, tiled=True
    )
    x_float = tokens[0].astype(f32)
    resid = x_float + dot(heads_rows, out_full, ((1,), (0,)))
    normed_m, inv_m = normed_rows(resid, gain_m)
    moe_all = to_group(normed_m).reshape(2 * n_seq, rows, D)

    forward_parts, backward_parts, grads_own, grads_other = [], [], [], []
    for i in range(per_half):
        expert = experts[i]
        gate_up, down_t = expert[:, : 2 * FFE], expert[:, 2 * FFE :]
        pick = picks[:, i]
        share_i = share[:, i].reshape(-1, 1)
        slots = dot(pick, moe_all, ((2,), (1,)), ((0,), (0,))).astype(bf16).reshape(-1, D)
        grad_slots = dot(pick, cot_all, ((2,), (1,)), ((0,), (0,))).reshape(-1, D)
        grad_slots = (share_i * grad_slots).astype(bf16)
        proj = dot(slots, gate_up, ((1,), (0,)))
        gate_v, up_v = proj[:, :FFE], proj[:, FFE:]
        sigma = jax.nn.sigmoid(gate_v)
        silu_v = gate_v * sigma
        act = (silu_v * up_v).astype(bf16)
        produced = (share_i * dot(act, down_t, ((1,), (1,)))).astype(bf16)
        grad_act = dot(grad_slots, down_t, ((1,), (0,)))
        grad_gate = grad_act * up_v * (sigma * (1.0 + gate_v * (1.0 - sigma)))
        grad_up = grad_act * silu_v
        grad_proj = jnp.concatenate([grad_gate.astype(bf16), grad_up.astype(bf16)], axis=1)
        grad_in = dot(grad_proj, gate_up, ((1,), (1,))).astype(bf16)
        grad_expert = jnp.concatenate(
            [
                dot(slots, grad_proj, ((0,), (0,))).astype(bf16),
                dot(grad_slots, act, ((0,), (0,))).astype(bf16),
            ],
            axis=1,
        )
        forward_parts.append(produced.reshape(2 * n_seq, capacity, D))
        backward_parts.append(grad_in.reshape(2 * n_seq, capacity, D))
        mine, theirs = scatter_expert(grad_expert)
        grads_own.append(mine)
        grads_other.append(theirs)

    every_pick = picks.reshape(2 * n_seq, per_half * capacity, rows)

    def combine(parts):
        together = jnp.concatenate(parts, axis=1)
        sums = dot(every_pick, together, ((1,), (1,)), ((0,), (0,)))
        return from_group(sums.reshape(n_seq, 2, rows, D))

    grad_normed_m = combine(backward_parts)
    mixed = (resid + combine(forward_parts)).astype(bf16)

    scaled_m = grad_normed_m * gain_m
    grad_resid = (
        cotangent[0].astype(f32)
        + inv_m * scaled_m
        - inv_m * inv_m * inv_m * resid * jnp.mean(scaled_m * resid, axis=1, keepdims=True)
    )
    grad_gain_m = jnp.sum(grad_normed_m * resid * inv_m, axis=0)
    grad_attn = grad_resid.astype(bf16)
    grad_heads_rows = dot(grad_attn, out_full, ((1,), (1,))).astype(bf16)
    grad_heads = lax.all_to_all(
        grad_heads_rows, "seq", split_axis=1, concat_axis=0, tiled=True
    ).reshape(span_len, heads_here, HEAD)
    grad_out_w = dot(heads_rows, grad_attn, ((0,), (0,))).astype(bf16)
    out_sum = lax.psum_scatter(grad_out_w, "fsdp", scatter_dimension=0, tiled=True)
    out_sum = lax.psum(out_sum, "seq").astype(f32)

    grad_q, grad_k, grad_v = attend_backward(
        queries, key_rows, values, segment, log_total, grad_heads, block_len
    )
    grad_qkv = jnp.stack([grad_q, grad_k, grad_v], axis=1).astype(bf16)
    grad_qkv = grad_qkv.reshape(span_len, 3 * width)
    grad_normed_a = dot(grad_qkv, qkv_own, ((1,), (1,))).astype(bf16)
    grad_normed_a = lax.psum_scatter(
        grad_normed_a, "seq", scatter_dimension=0, tiled=True
    ).astype(f32)
    grad_qkv_w = dot(normed_a, grad_qkv, ((0,), (0,))).astype(bf16)
    qkv_sum = lax.psum_scatter(grad_qkv_w, "fsdp", scatter_dimension=0, tiled=True)
    qkv_sum = lax.all_gather(
        qkv_sum.reshape(shard, 3, width), "seq", axis=2, tiled=True
    ).reshape(shard, 3 * D)
    inv_a = lax.rsqrt(jnp.mean(x_float * x_float, axis=1, keepdims=True) + epsilon)
    scaled_a = grad_normed_a * gain_a
    grad_x = (
        grad_resid
        + inv_a * scaled_a
        - inv_a * inv_a * inv_a * x_float * jnp.mean(scaled_a * x_float, axis=1, keepdims=True)
    )
    grad_gain_a = jnp.sum(grad_normed_a * x_float * inv_a, axis=0)
    gain_sums = lax.psum(jnp.stack([grad_gain_a, grad_gain_m]), ("seq", "fsdp"))
    gain_sums = lax.dynamic_slice_in_dim(gain_sums, at_fsdp * shard, shard, 1)

    own_grads, other_grads = jnp.stack(grads_own), jnp.stack(grads_other)
    first = half == 0
    grad_all = jnp.concatenate(
        [jnp.where(first, own_grads, other_grads), jnp.where(first, other_grads, own_grads)]
    ).astype(f32)
    return (
        mixed[None],
        grad_x.astype(bf16)[None],
        gain_sums[0],
        gain_sums[1],
        qkv_sum.astype(f32),
        out_sum,
        grad_all[:, :, : 2 * FFE].reshape(local_count, shard, 2, FFE),
        jnp.swapaxes(grad_all[:, :, 2 * FFE :], 1, 2),
    )


def solution(mesh):
    placed = (
        P("fsdp", "seq", None),
        P("fsdp", None),
        P("fsdp", "seq", None),
        P("fsdp", "seq", None),
        P("fsdp"),
        P("fsdp"),
        P("fsdp", None),
        P("fsdp", None),
        P("seq", "fsdp", None, None),
        P("seq", None, "fsdp"),
        P("fsdp", "seq", None),
    )
    return jax.shard_map(
        body,
        mesh=mesh,
        in_specs=placed,
        out_specs=(
            P("fsdp", "seq", None),
            P("fsdp", "seq", None),
            P("fsdp"),
            P("fsdp"),
            P("fsdp", None),
            P("fsdp", None),
            P("seq", "fsdp", None, None),
            P("seq", None, "fsdp"),
        ),
        check_vma=False,
    )
```

```python
import jax
import jax.numpy as jnp
from jax import lax
from jax.experimental import pallas as pl
from jax.experimental.pallas import tpu as pltpu
from jax.sharding import PartitionSpec as P

D = 2048
HEADS = 16
HEAD = 128
FFE = 1024
TOP = 8

epsilon = 1e-06
f32 = jnp.float32
bf16 = jnp.bfloat16


def swap(value, axis, bit):
    size = lax.axis_size(axis)
    return lax.ppermute(value, axis, [(i, i ^ bit) for i in range(size)])


def dot(a, b, contract, batch=((), ())):
    return lax.dot_general(a, b, (contract, batch), preferred_element_type=f32)


def segment_ids(length_row, span_len):
    ends = jnp.cumsum(length_row)
    places = lax.iota(jnp.int32, span_len)
    return jnp.sum((places[:, None] >= ends[None, :]).astype(jnp.int32), axis=1)


def attend_forward(queries, key_rows, values, segment, block_len):
    span_len, heads_now, head_dim = queries.shape
    score_scale = head_dim ** (-0.5)

    def one_block(row_start):
        q_block = lax.dynamic_slice_in_dim(queries, row_start, block_len, 0)
        seg_block = lax.dynamic_slice_in_dim(segment, row_start, block_len, 0)
        scores = (
            jnp.einsum("qhd,khd->hqk", q_block, key_rows, preferred_element_type=f32)
            * score_scale
        )
        scores = jnp.where(seg_block[None, :, None] == segment[None, None, :], scores, -1e30)
        row_max = jnp.max(scores, axis=2, keepdims=True)
        exp_part = jnp.exp(scores - row_max)
        row_sum = jnp.sum(exp_part, axis=2, keepdims=True)
        prob_b = (exp_part / row_sum).astype(bf16)
        out_block = jnp.einsum("hqk,khd->qhd", prob_b, values, preferred_element_type=f32)
        return (out_block.astype(bf16), (row_max + jnp.log(row_sum))[:, :, 0])

    starts = jnp.arange(span_len // block_len, dtype=jnp.int32) * block_len
    outputs, log_total = lax.map(one_block, starts)
    log_total = jnp.transpose(log_total, (1, 0, 2)).reshape(heads_now, span_len)
    return (outputs.reshape(span_len, heads_now, head_dim), log_total)


def attend_backward(queries, key_rows, values, segment, log_total, grad_heads, block_len):
    span_len, heads_now, head_dim = queries.shape
    score_scale = head_dim ** (-0.5)

    def one_block(carried, row_start):
        grad_k, grad_v = carried
        q_block = lax.dynamic_slice_in_dim(queries, row_start, block_len, 0)
        seg_block = lax.dynamic_slice_in_dim(segment, row_start, block_len, 0)
        g_block = lax.dynamic_slice_in_dim(grad_heads, row_start, block_len, 0)
        lse_block = lax.dynamic_slice_in_dim(log_total, row_start, block_len, 1)
        scores = (
            jnp.einsum("qhd,khd->hqk", q_block, key_rows, preferred_element_type=f32)
            * score_scale
        )
        scores = jnp.where(seg_block[None, :, None] == segment[None, None, :], scores, -1e30)
        prob_f = jnp.exp(scores - lse_block[:, :, None])
        grad_v = grad_v + jnp.einsum(
            "hqk,qhd->khd", prob_f.astype(bf16), g_block, preferred_element_type=f32
        )
        grad_p = jnp.einsum("qhd,khd->hqk", g_block, values, preferred_element_type=f32)
        inner_sum = jnp.sum(prob_f * grad_p, axis=2, keepdims=True)
        dscore = (prob_f * (grad_p - inner_sum)).astype(bf16)
        grad_q = (
            jnp.einsum("hqk,khd->qhd", dscore, key_rows, preferred_element_type=f32)
            * score_scale
        )
        grad_k = (
            grad_k
            + jnp.einsum("hqk,qhd->khd", dscore, q_block, preferred_element_type=f32)
            * score_scale
        )
        return ((grad_k, grad_v), grad_q)

    zeros_kv = jnp.zeros((span_len, heads_now, head_dim), f32)
    starts = jnp.arange(span_len // block_len, dtype=jnp.int32) * block_len
    (grad_k, grad_v), grad_q = lax.scan(one_block, (zeros_kv, zeros_kv), starts)
    return (grad_q.reshape(span_len, heads_now, head_dim), grad_k, grad_v)


def after(value, *others):
    return lax.optimization_barrier((value, *others))[0]


def reversed_bits(index, size):
    count, total = size.bit_length() - 1, 0
    for bit in range(count):
        total = total + (((index >> bit) & 1) << (count - 1 - bit))
    return total


def start_expert(mine, sent, start):
    size = lax.axis_size("fsdp")
    mine = after(mine, start)
    pieces = {0: mine, size // 2: swap(after(sent, start), "fsdp", size // 2)}
    bit = size // 4
    while bit:
        pieces[bit] = swap(mine, "fsdp", bit)
        bit //= 2
    return pieces


def finish_expert(pieces, middle):
    size = lax.axis_size("fsdp")
    pieces = dict(pieces)
    for j in sorted(range(size), key=lambda j: (j & 1, j.bit_count())):
        if j not in pieces:
            low = j & -j
            pieces[j] = swap(after(pieces[j ^ low], middle), "fsdp", low)
    return [pieces[j] for j in range(size)]


def gather_rows(piece, axis):
    place, rows = lax.axis_index(axis), piece.shape[0]
    whole = jnp.zeros((lax.axis_size(axis) * rows, *piece.shape[1:]), piece.dtype)
    for k in range(lax.axis_size(axis)):
        part = swap(piece, axis, k) if k else piece
        whole = lax.dynamic_update_slice_in_dim(whole, part, (place ^ k) * rows, 0)
    return whole


def scatter_rows(sums, axis):
    place, rows = lax.axis_index(axis), sums.shape[0] // lax.axis_size(axis)
    parts = [
        lax.dynamic_slice_in_dim(sums, (place ^ k) * rows, rows, 0)
        for k in range(lax.axis_size(axis))
    ]
    return sum((swap(part, axis, k) if k else part).astype(f32) for k, part in enumerate(parts))


def gather_doubling(piece, axis, start):
    size, place = lax.axis_size(axis), lax.axis_index(axis)
    rows = piece.shape[0]
    whole = after(piece, start)[None]
    bit = size // 2
    while bit:
        received = swap(whole, axis, bit)
        low = (place // bit) % 2 == 0
        whole = jnp.stack(
            [jnp.where(low, whole, received), jnp.where(low, received, whole)], axis=1
        ).reshape(-1, *piece.shape)
        bit //= 2
    return whole.reshape(-1, *piece.shape[1:])


def expert_kernel(size, tiles, part, place_ref, share_ref, *rest):
    slots, pieces, rest = rest[:4], rest[4 : 4 + size], rest[4 + size :]
    made_ref, back_ref, send_ref, keep_ref, weights, x_ref, g_ref, act, grad_proj, sems = rest
    step = pl.program_id(0)
    place = place_ref[0]
    rows = weights.shape[0] // size
    ffe = act.shape[1]
    wide = ffe // tiles
    nn, nt, tn = ((1,), (0,)), ((1,), (1,)), ((0,), (0,))

    @pl.when(step == 0)
    def _():
        copies = [
            pltpu.make_async_copy(
                pieces[j].at[part],
                weights.at[pl.ds(pl.multiple_of((place ^ j) * rows, rows), rows)],
                sems.at[j],
            )
            for j in range(size)
        ]
        count = slots[0].shape[0]
        for k, slot in enumerate(slots):
            copies.append(
                pltpu.make_async_copy(
                    slot,
                    (x_ref, g_ref)[k // 2].at[pl.ds(k % 2 * count, count)],
                    sems.at[size + k],
                )
            )
        for copy in copies:
            copy.start()
        for copy in copies:
            copy.wait()

    @pl.when(step < tiles)
    def _():
        first = pl.multiple_of(step * wide, wide)
        gate = dot(x_ref[...], weights[:, pl.ds(first, wide)], nn)
        up = dot(x_ref[...], weights[:, pl.ds(pl.multiple_of(ffe + first, wide), wide)], nn)
        grad_act = dot(
            g_ref[...], weights[:, pl.ds(pl.multiple_of(2 * ffe + first, wide), wide)], nn
        )
        sigma = 1.0 / (1.0 + jnp.exp(-gate))
        silu = gate * sigma
        act[:, pl.ds(first, wide)] = (silu * up).astype(bf16)
        grad_proj[:, pl.ds(first, wide)] = (
            grad_act * up * (sigma * (1.0 + gate * (1.0 - sigma)))
        ).astype(bf16)
        grad_proj[:, pl.ds(pl.multiple_of(ffe + first, wide), wide)] = (grad_act * silu).astype(
            bf16
        )

    @pl.when(step >= tiles)
    def _():
        turn = step - tiles
        whose = place ^ reversed_bits((turn + size // 2) % size, size)
        at = pl.ds(pl.multiple_of(whose * rows, rows), rows)
        made_ref[...] = (
            share_ref[...] * dot(act[...], weights[at, 2 * ffe :], nt)
        ).astype(bf16)
        back_ref[...] = dot(grad_proj[...], weights[at, : 2 * ffe], nt).astype(bf16)

        def grads(out_ref):
            out_ref[0, :, : 2 * ffe] = dot(x_ref[:, at], grad_proj[...], tn).astype(bf16)
            out_ref[0, :, 2 * ffe :] = dot(g_ref[:, at], act[...], tn).astype(bf16)

        @pl.when(turn < size // 2)
        def _():
            grads(send_ref)

        @pl.when(turn >= size // 2)
        def _():
            grads(keep_ref)


def run_expert(place, share, slots, grad_slots, pieces, part):
    size, (_, rows, columns) = len(pieces), pieces[0].shape
    count = 2 * slots[0].shape[0]
    ffe = columns // 3
    tiles = 4
    half = size // 2

    def whose(step, place):
        turn = jnp.maximum(step - tiles, 0)
        return 0, place[0] ^ reversed_bits((turn + half) % size, size)

    flops = 2 * count * D * ffe * 9
    return pl.pallas_call(
        lambda *refs: expert_kernel(size, tiles, part, *refs),
        out_shape=[
            jax.ShapeDtypeStruct((count, D), bf16),
            jax.ShapeDtypeStruct((count, D), bf16),
            jax.ShapeDtypeStruct((half, rows, columns), bf16),
            jax.ShapeDtypeStruct((half, rows, columns), bf16),
        ],
        grid_spec=pltpu.PrefetchScalarGridSpec(
            num_scalar_prefetch=1,
            grid=(tiles + size,),
            in_specs=[
                pl.BlockSpec((count, 1), lambda step, place: (0, 0)),
                *[pl.BlockSpec(memory_space=pl.ANY)] * (size + 4),
            ],
            out_specs=[
                pl.BlockSpec((count, rows), whose),
                pl.BlockSpec((count, rows), whose),
                pl.BlockSpec(
                    (1, rows, columns), lambda t, place: (jnp.clip(t - tiles, 0, half - 1), 0, 0)
                ),
                pl.BlockSpec(
                    (1, rows, columns),
                    lambda t, place: (jnp.clip(t - tiles - half, 0, half - 1), 0, 0),
                ),
            ],
            scratch_shapes=[
                pltpu.VMEM((size * rows, columns), bf16),
                pltpu.VMEM((count, D), bf16),
                pltpu.VMEM((count, D), bf16),
                pltpu.VMEM((count, ffe), bf16),
                pltpu.VMEM((count, 2 * ffe), bf16),
                pltpu.SemaphoreType.DMA((size + 4,)),
            ],
        ),
        compiler_params=pltpu.CompilerParams(
            dimension_semantics=("arbitrary",), vmem_limit_bytes=60 * 2**20
        ),
        cost_estimate=pl.CostEstimate(
            flops=flops, bytes_accessed=8 * count * D + 8 * size * rows * columns, transcendentals=0
        ),
        name="expert",
    )(place, share, *slots, *grad_slots, *pieces)


class GradChain:
    def __init__(self, send, keep):
        self.bit, self.size = 1, lax.axis_size("fsdp")
        self.terms, self.send = [keep], send

    def sums(self):
        if self.bit == self.size:
            return self.terms[-1]
        received = swap(self.send, "fsdp", self.bit)
        self.terms.append(received)
        self.bit *= 2
        many = self.terms[0].shape[0] // 2
        if many:
            total = sum(t[many:].astype(f32) for t in self.terms)
            self.send = total.astype(bf16)
            self.terms = [t[:many] for t in self.terms]
            return self.send
        return received

    def ended(self):
        other = self.terms.pop()[0]
        return sum(t[0].astype(f32) for t in self.terms).astype(bf16), other


def to_group(rows, *others):
    own = lax.all_gather(rows, "seq", axis=0, tiled=False)
    swapped = swap(after(rows, *others) if others else rows, "fsdp", lax.axis_size("fsdp") // 2)
    return own, lax.all_gather(swapped, "seq", axis=0, tiled=False), swapped


def from_group(sums_own, sums_other):
    mine = lax.psum_scatter(sums_other, "seq", scatter_dimension=0, tiled=True)
    other = swap(mine, "fsdp", lax.axis_size("fsdp") // 2)
    mine = lax.psum_scatter(sums_own, "seq", scatter_dimension=0, tiled=True)
    return mine.astype(f32) + other.astype(f32)


def body(
    tokens, lengths, routes, gates, gain_attn, gain_moe, w_qkv, w_out, w_gate_up, w_down, cotangent
):
    n_seq, n_fsdp = lax.axis_size("seq"), lax.axis_size("fsdp")
    at_seq, at_fsdp = lax.axis_index("seq"), lax.axis_index("fsdp")
    rows = tokens.shape[1]
    shard = D // n_fsdp
    local_count = w_gate_up.shape[0]
    per_half = local_count // 2
    half = at_fsdp // (n_fsdp // 2)
    heads_here = HEADS // n_seq
    width = heads_here * HEAD
    span_len = rows * n_seq

    packed = jnp.concatenate(
        [w_gate_up.reshape(local_count, shard, 2 * FFE), jnp.swapaxes(w_down, 1, 2)], axis=2
    )
    own_part = lax.dynamic_slice_in_dim(packed, half * per_half, per_half, 0)
    other_part = lax.dynamic_slice_in_dim(packed, (1 - half) * per_half, per_half, 0)
    x_all = gather_rows(tokens[0], "seq")
    part = lax.dynamic_slice_in_dim(
        w_qkv.reshape(shard, 3, HEADS, HEAD), at_seq * heads_here, heads_here, 2
    ).reshape(shard, 3 * width)
    gains = jnp.zeros((shard, 128), bf16).at[:, 0].set(gain_attn).at[:, 1].set(gain_moe)
    gathered = lax.all_gather(
        jnp.concatenate([part, gains], axis=1), "fsdp", axis=0, tiled=True
    )
    qkv_own = gathered[:, : 3 * width]
    gain_a = gathered[:, 3 * width].astype(f32)
    gain_m = gathered[:, 3 * width + 1].astype(f32)
    out_full = gather_doubling(w_out, "fsdp", gathered)

    parts = per_half // 2
    routing = jnp.concatenate([routes[0].astype(f32), gates[0]], axis=1)
    routing = jnp.stack(to_group(routing)[:2]).reshape(2 * n_seq, rows, 2 * TOP)
    capacity = rows * TOP * 4 // (3 * local_count * n_seq) + 2
    capacity = -(-capacity // 8) * 8
    named = at_seq * local_count + half * per_half + lax.iota(jnp.int32, per_half)
    hits = routing[:, :, :TOP, None].astype(jnp.int32) == named
    mask = jnp.any(hits, axis=2)
    weight = jnp.sum(jnp.where(hits, routing[:, :, TOP:, None], 0.0), axis=2)
    below = (lax.iota(jnp.int32, rows)[:, None] > lax.iota(jnp.int32, rows)[None, :]).astype(bf16)
    rank = jnp.einsum("rq,bqe->bre", below, mask.astype(bf16), preferred_element_type=f32)
    rank = jnp.where(mask, rank.astype(jnp.int32), -1)
    picks = jnp.swapaxes(rank, 1, 2)[:, :, None, :] == lax.iota(jnp.int32, capacity)[:, None]
    share = jnp.sum(
        jnp.where(picks, jnp.swapaxes(weight, 1, 2)[:, :, None, :], 0.0), axis=3
    )
    picks = picks.astype(bf16)
    cot_all = to_group(after(cotangent[0], x_all, gathered))

    def normed_rows(values, gain):
        inverse = lax.rsqrt(jnp.mean(values * values, axis=1, keepdims=True) + epsilon)
        return (values * inverse * gain).astype(bf16), inverse

    normed_a, inv_all = normed_rows(x_all.astype(f32), gain_a)
    qkv = dot(normed_a, qkv_own, ((1,), (0,))).astype(bf16)
    spread = qkv.reshape(span_len, 3, heads_here, HEAD)
    segment = segment_ids(lengths[0], span_len)
    block_len = span_len // 3
    queries, key_rows, values = spread[:, 0], spread[:, 1], spread[:, 2]
    attended, log_total = attend_forward(queries, key_rows, values, segment, block_len)
    heads_rows = lax.all_to_all(
        attended.reshape(span_len, width), "seq", split_axis=0, concat_axis=1, tiled=True
    )
    first_part = start_expert(own_part[:2], other_part[:2], gathered)
    heads_rows = after(heads_rows, *first_part.values())
    x_float = tokens[0].astype(f32)
    resid = x_float + dot(heads_rows, out_full, ((1,), (0,)))
    normed_m, inv_m = normed_rows(resid, gain_m)
    moe_all = to_group(normed_m)

    begun = [first_part]
    for c in range(1, parts):
        begun.append(
            start_expert(
                own_part[2 * c : 2 * c + 2], other_part[2 * c : 2 * c + 2], moe_all[2]
            )
        )
    experts = [
        finish_expert(begun[c], heads_rows if c == 0 else moe_all[1]) for c in range(parts)
    ]

    place = jnp.full((1,), at_fsdp, jnp.int32)
    forward_parts, backward_parts, chains = [], [], []
    slots_of, grad_slots_of = [], []
    for i in range(per_half):
        for g in range(2):
            pick = picks[g * n_seq : (g + 1) * n_seq, i]
            share_i = share[g * n_seq : (g + 1) * n_seq, i].reshape(-1, 1)
            slots = dot(pick, moe_all[g], ((2,), (1,)), ((0,), (0,))).astype(bf16)
            slots_of.append(slots.reshape(-1, D))
            grad_slots = dot(pick, cot_all[g], ((2,), (1,)), ((0,), (0,))).reshape(-1, D)
            grad_slots_of.append((share_i * grad_slots).astype(bf16))
    for i in range(per_half):
        slots = slots_of[2 * i : 2 * i + 2]
        if i >= 2:
            slots = [after(slots[0], chains[i - 2].sums()), slots[1]]
        elif i < 1 and parts > 1:
            slots = [after(slots[0], begun[1][n_fsdp // 2]), slots[1]]
        made, back, send, keep = run_expert(
            place,
            share[:, i].reshape(-1, 1),
            slots,
            grad_slots_of[2 * i : 2 * i + 2],
            experts[i // 2],
            i % 2,
        )
        forward_parts.append(made.reshape(2, n_seq, capacity, D))
        backward_parts.append(back.reshape(2, n_seq, capacity, D))
        chains.append(GradChain(send, keep))

    every_pick = picks.reshape(2, n_seq, per_half * capacity, rows)

    def combine(parts, *others):
        sums = []
        for g in range(2):
            together = after(jnp.concatenate([part[g] for part in parts], axis=1), *others)
            total = dot(every_pick[g], together, ((1,), (1,)), ((0,), (0,)))
            sums.append(total.astype(bf16).reshape(span_len, D))
        return from_group(*sums)

    grad_normed_m = combine(backward_parts, chains[0].sums())
    grad_normed_m = after(grad_normed_m, *[chain.sums() for chain in chains[1:]])

    scaled_m = grad_normed_m * gain_m
    grad_resid = (
        cotangent[0].astype(f32)
        + inv_m * scaled_m
        - inv_m * inv_m * inv_m * resid * jnp.mean(scaled_m * resid, axis=1, keepdims=True)
    )
    grad_gain_m = jnp.sum(grad_normed_m * resid * inv_m, axis=0)
    grad_attn = grad_resid.astype(bf16)
    mixed = (resid + combine(forward_parts, grad_attn)).astype(bf16)
    grad_heads_rows = dot(grad_attn, out_full, ((1,), (1,))).astype(bf16)
    grad_heads = lax.all_to_all(
        grad_heads_rows, "seq", split_axis=1, concat_axis=0, tiled=True
    ).reshape(span_len, heads_here, HEAD)
    grad_out_w = dot(heads_rows, grad_attn, ((0,), (0,))).astype(bf16)
    out_sum = lax.psum_scatter(grad_out_w, "fsdp", scatter_dimension=0, tiled=True)
    out_sum = lax.psum(out_sum, "seq").astype(f32)

    grad_heads = after(grad_heads, *[chain.sums() for chain in chains])

    grad_q, grad_k, grad_v = attend_backward(
        queries, key_rows, values, segment, log_total, grad_heads, block_len
    )
    grad_qkv = jnp.stack([grad_q, grad_k, grad_v], axis=1).astype(bf16)
    grad_qkv = after(grad_qkv.reshape(span_len, 3 * width), mixed)
    part_normed_a = dot(grad_qkv, qkv_own, ((1,), (1,)))
    grad_normed_a = scatter_rows(part_normed_a.astype(bf16), "seq")
    part_gain_a = jnp.sum(part_normed_a * x_all.astype(f32) * inv_all, axis=0)
    gain_columns = jnp.zeros((D, 128), bf16)
    gain_columns = gain_columns.at[:, 0].set(part_gain_a.astype(bf16))
    gain_columns = gain_columns.at[:, 1].set(grad_gain_m.astype(bf16))
    grad_qkv_w = dot(normed_a, grad_qkv, ((0,), (0,))).astype(bf16)
    qkv_sum = lax.psum_scatter(
        jnp.concatenate([grad_qkv_w, gain_columns], axis=1), "fsdp", scatter_dimension=0, tiled=True
    )
    qkv_sum = lax.all_gather(qkv_sum, "seq", axis=0, tiled=False)
    gain_sums = jnp.sum(qkv_sum[:, :, 3 * width : 3 * width + 2].astype(f32), axis=0)
    qkv_sum = jnp.transpose(
        qkv_sum[:, :, : 3 * width].reshape(n_seq, shard, 3, width), (1, 2, 0, 3)
    ).reshape(shard, 3 * D)
    inv_a = lax.rsqrt(jnp.mean(x_float * x_float, axis=1, keepdims=True) + epsilon)
    scaled_a = grad_normed_a * gain_a
    grad_x = (
        grad_resid
        + inv_a * scaled_a
        - inv_a * inv_a * inv_a * x_float * jnp.mean(scaled_a * x_float, axis=1, keepdims=True)
    )

    for chain in chains:
        while chain.bit < n_fsdp:
            chain.sums()
    ended = [chain.ended() for chain in chains]
    own_grads, other_grads = jnp.stack([e[0] for e in ended]), jnp.stack([e[1] for e in ended])
    first = half == 0
    grad_all = jnp.concatenate(
        [jnp.where(first, own_grads, other_grads), jnp.where(first, other_grads, own_grads)]
    ).astype(f32)
    return (
        mixed[None],
        grad_x.astype(bf16)[None],
        gain_sums[:, 0],
        gain_sums[:, 1],
        qkv_sum.astype(f32),
        out_sum,
        grad_all[:, :, : 2 * FFE].reshape(local_count, shard, 2, FFE),
        jnp.swapaxes(grad_all[:, :, 2 * FFE :], 1, 2),
    )


def solution(mesh):
    placed = (
        P("fsdp", "seq", None),
        P("fsdp", None),
        P("fsdp", "seq", None),
        P("fsdp", "seq", None),
        P("fsdp"),
        P("fsdp"),
        P("fsdp", None),
        P("fsdp", None),
        P("seq", "fsdp", None, None),
        P("seq", None, "fsdp"),
        P("fsdp", "seq", None),
    )
    return jax.shard_map(
        body,
        mesh=mesh,
        in_specs=placed,
        out_specs=(
            P("fsdp", "seq", None),
            P("fsdp", "seq", None),
            P("fsdp"),
            P("fsdp"),
            P("fsdp", None),
            P("fsdp", None),
            P("seq", "fsdp", None, None),
            P("seq", None, "fsdp"),
        ),
        check_vma=False,
    )
```

```python
import jax
import jax.numpy as jnp
from jax import lax
from jax.experimental import pallas as pl
from jax.experimental.pallas import tpu as pltpu
from jax.sharding import PartitionSpec as P

D = 2048
HEADS = 16
HEAD = 128
FFE = 1024
TOP = 8

epsilon = 1e-06
f32 = jnp.float32
bf16 = jnp.bfloat16


def swap(value, axis, bit):
    size = lax.axis_size(axis)
    return lax.ppermute(value, axis, [(i, i ^ bit) for i in range(size)])


def dot(a, b, contract, batch=((), ())):
    return lax.dot_general(a, b, (contract, batch), preferred_element_type=f32)


def segment_ids(length_row, span_len):
    ends = jnp.cumsum(length_row)
    places = lax.iota(jnp.int32, span_len)
    return jnp.sum((places[:, None] >= ends[None, :]).astype(jnp.int32), axis=1)


def score_probs(keys, queries, seg_column, seg_row):
    raw = dot(keys, queries, ((1,), (1,)))
    raw = jnp.where(seg_column == seg_row, raw, -1e30)
    top = jnp.max(raw, axis=0, keepdims=True)
    part = jnp.exp((raw - top) * HEAD ** (-0.5))
    return part * (1.0 / jnp.sum(part, axis=0, keepdims=True))


def head_columns(heads_here, head):
    return [
        pl.ds(pl.multiple_of((third * heads_here + head) * HEAD, HEAD), HEAD) for third in range(3)
    ]


def attend_forward_kernel(heads_here, qkv_ref, seg_column, seg_row, out_ref):
    block = out_ref.shape[0]
    at = pl.ds(pl.multiple_of(pl.program_id(1) * block, block), block)
    q_at, k_at, v_at = head_columns(heads_here, pl.program_id(0))
    probs = score_probs(qkv_ref[:, k_at], qkv_ref[at, q_at], seg_column[...], seg_row[...])
    out_ref[...] = dot(qkv_ref[:, v_at], probs.astype(bf16), ((0,), (0,))).T.astype(bf16)


def attend_backward_kernel(
    heads_here, qkv_ref, grad_ref, seg_column, seg_row, out_ref, grad_k, grad_v
):
    block = grad_ref.shape[0]
    turn = pl.program_id(1)
    at = pl.ds(pl.multiple_of(turn * block, block), block)
    q_at, k_at, v_at = head_columns(heads_here, pl.program_id(0))
    queries, keys, grads = qkv_ref[at, q_at], qkv_ref[:, k_at], grad_ref[...]
    probs = score_probs(keys, queries, seg_column[...], seg_row[...])
    grad_probs = dot(qkv_ref[:, v_at], grads, ((1,), (1,)))
    inner = jnp.sum(probs * grad_probs, axis=0, keepdims=True)
    grad_scores = (probs * (grad_probs - inner)).astype(bf16)
    scale = HEAD ** (-0.5)

    @pl.when(turn == 0)
    def _():
        grad_k[...] = jnp.zeros_like(grad_k)
        grad_v[...] = jnp.zeros_like(grad_v)

    grad_v[...] += dot(probs.astype(bf16), grads, ((1,), (0,)))
    grad_k[...] += dot(grad_scores, queries, ((1,), (0,)))
    out_ref[at, q_at] = (dot(keys, grad_scores, ((0,), (0,))).T * scale).astype(bf16)

    @pl.when(turn == pl.num_programs(1) - 1)
    def _():
        out_ref[:, k_at] = (grad_k[...] * scale).astype(bf16)
        out_ref[:, v_at] = grad_v[...].astype(bf16)


def attend(qkv, segment, grad=None):
    span_len, columns = qkv.shape
    heads_here = columns // (3 * HEAD)
    blocks = 3
    block = span_len // blocks
    whole = pl.BlockSpec((span_len, columns), lambda h, i: (0, 0), pipeline_mode=pl.Buffered(1))
    cut = pl.BlockSpec((block, HEAD), lambda h, i: (i, h))
    segments = [
        pl.BlockSpec((span_len, 1), lambda h, i: (0, 0)),
        pl.BlockSpec((1, block), lambda h, i: (0, i)),
    ]
    backward = grad is not None
    return pl.pallas_call(
        lambda *refs: (attend_backward_kernel if backward else attend_forward_kernel)(
            heads_here, *refs
        ),
        out_shape=jax.ShapeDtypeStruct((span_len, columns if backward else columns // 3), bf16),
        grid=(heads_here, blocks),
        in_specs=[whole, *[cut] * backward, *segments],
        out_specs=pl.BlockSpec((span_len, columns), lambda h, i: (0, 0)) if backward else cut,
        scratch_shapes=[pltpu.VMEM((span_len, HEAD), f32)] * (2 * backward),
        compiler_params=pltpu.CompilerParams(
            dimension_semantics=("arbitrary", "arbitrary"), vmem_limit_bytes=60 * 2**20
        ),
        cost_estimate=pl.CostEstimate(
            flops=(40 if backward else 20) * span_len * span_len * HEAD * heads_here,
            bytes_accessed=4 * span_len * columns,
            transcendentals=span_len * span_len * heads_here,
        ),
        name="attend_backward" if backward else "attend_forward",
    )(*[qkv, *[grad] * backward, segment.reshape(span_len, 1), segment.reshape(1, span_len)])


def unpack_kernel(in_ref, out_ref):
    out_ref[...] = in_ref[0].astype(f32)


def unpack_columns(gathered, width, thirds):
    n_seq, rows, _ = gathered.shape
    return pl.pallas_call(
        unpack_kernel,
        out_shape=jax.ShapeDtypeStruct((rows, thirds * n_seq * width), f32),
        grid=(n_seq, thirds),
        in_specs=[pl.BlockSpec((1, rows, width), lambda s, p: (s, 0, p))],
        out_specs=pl.BlockSpec((rows, width), lambda s, p: (0, p * n_seq + s)),
        name="unpack",
    )(gathered)


def after(value, *others):
    if not others:
        return value
    return lax.optimization_barrier((value, *others))[0]


def reversed_bits(index, size):
    count, total = size.bit_length() - 1, 0
    for bit in range(count):
        total = total + (((index >> bit) & 1) << (count - 1 - bit))
    return total


def start_expert(mine, sent, *start):
    size = lax.axis_size("fsdp")
    mine, sent = after(mine, *start), after(sent, *start)
    pieces = {0: mine, size // 2: swap(sent, "fsdp", size // 2)}
    bit = size // 4
    while bit:
        pieces[bit] = swap(mine, "fsdp", bit)
        bit //= 2
    return pieces


def finish_expert(pieces):
    size = lax.axis_size("fsdp")
    pieces = dict(pieces)
    for j in sorted(range(size), key=lambda j: (j & 1, j.bit_count())):
        if j not in pieces:
            low = j & -j
            pieces[j] = swap(pieces[j ^ low], "fsdp", low)
    return [pieces[j] for j in range(size)]


def gather_rows(piece, axis):
    place, rows = lax.axis_index(axis), piece.shape[0]
    whole = jnp.zeros((lax.axis_size(axis) * rows, *piece.shape[1:]), piece.dtype)
    for k in range(lax.axis_size(axis)):
        part = swap(piece, axis, k) if k else piece
        whole = lax.dynamic_update_slice_in_dim(whole, part, (place ^ k) * rows, 0)
    return whole


def scatter_rows(sums, axis):
    place, rows = lax.axis_index(axis), sums.shape[0] // lax.axis_size(axis)
    parts = [
        lax.dynamic_slice_in_dim(sums, (place ^ k) * rows, rows, 0)
        for k in range(lax.axis_size(axis))
    ]
    return sum((swap(part, axis, k) if k else part).astype(f32) for k, part in enumerate(parts))


def expert_kernel(size, tiles, part, place_ref, share_ref, *rest):
    slots, pieces, rest = rest[:4], rest[4 : 4 + size], rest[4 + size :]
    made_ref, back_ref, send_ref, keep_ref, weights, x_ref, g_ref, act, grad_proj, sems = rest
    step = pl.program_id(0)
    place = place_ref[0]
    rows = weights.shape[0] // size
    ffe = act.shape[1]
    wide = ffe // tiles
    nn, nt, tn = ((1,), (0,)), ((1,), (1,)), ((0,), (0,))

    @pl.when(step == 0)
    def _():
        copies = [
            pltpu.make_async_copy(
                pieces[j].at[part],
                weights.at[pl.ds(pl.multiple_of((place ^ j) * rows, rows), rows)],
                sems.at[j],
            )
            for j in range(size)
        ]
        count = slots[0].shape[0]
        for k, slot in enumerate(slots):
            copies.append(
                pltpu.make_async_copy(
                    slot,
                    (x_ref, g_ref)[k // 2].at[pl.ds(k % 2 * count, count)],
                    sems.at[size + k],
                )
            )
        for copy in copies:
            copy.start()
        for copy in copies:
            copy.wait()

    @pl.when(step < tiles)
    def _():
        first = pl.multiple_of(step * wide, wide)
        gate = dot(x_ref[...], weights[:, pl.ds(first, wide)], nn)
        up = dot(x_ref[...], weights[:, pl.ds(pl.multiple_of(ffe + first, wide), wide)], nn)
        grad_act = dot(
            g_ref[...], weights[:, pl.ds(pl.multiple_of(2 * ffe + first, wide), wide)], nn
        )
        sigma = 1.0 / (1.0 + jnp.exp(-gate))
        silu = gate * sigma
        act[:, pl.ds(first, wide)] = (silu * up).astype(bf16)
        grad_proj[:, pl.ds(first, wide)] = (
            grad_act * up * (sigma * (1.0 + gate * (1.0 - sigma)))
        ).astype(bf16)
        grad_proj[:, pl.ds(pl.multiple_of(ffe + first, wide), wide)] = (grad_act * silu).astype(
            bf16
        )

    @pl.when(step >= tiles)
    def _():
        turn = step - tiles
        whose = place ^ reversed_bits((turn + size // 2) % size, size)
        at = pl.ds(pl.multiple_of(whose * rows, rows), rows)
        made_ref[...] = (
            share_ref[...] * dot(act[...], weights[at, 2 * ffe :], nt)
        ).astype(bf16)
        back_ref[...] = dot(grad_proj[...], weights[at, : 2 * ffe], nt).astype(bf16)

        def grads(out_ref):
            out_ref[0, :, : 2 * ffe] = dot(x_ref[:, at], grad_proj[...], tn).astype(bf16)
            out_ref[0, :, 2 * ffe :] = dot(g_ref[:, at], act[...], tn).astype(bf16)

        @pl.when(turn < size // 2)
        def _():
            grads(send_ref)

        @pl.when(turn >= size // 2)
        def _():
            grads(keep_ref)


def run_expert(place, share, slots, grad_slots, pieces, part):
    size, (_, rows, columns) = len(pieces), pieces[0].shape
    count = 2 * slots[0].shape[0]
    ffe = columns // 3
    tiles = 4
    half = size // 2

    def whose(step, place):
        turn = jnp.maximum(step - tiles, 0)
        return 0, place[0] ^ reversed_bits((turn + half) % size, size)

    return pl.pallas_call(
        lambda *refs: expert_kernel(size, tiles, part, *refs),
        out_shape=[
            jax.ShapeDtypeStruct((count, D), bf16),
            jax.ShapeDtypeStruct((count, D), bf16),
            jax.ShapeDtypeStruct((half, rows, columns), bf16),
            jax.ShapeDtypeStruct((half, rows, columns), bf16),
        ],
        grid_spec=pltpu.PrefetchScalarGridSpec(
            num_scalar_prefetch=1,
            grid=(tiles + size,),
            in_specs=[
                pl.BlockSpec((count, 1), lambda step, place: (0, 0)),
                *[pl.BlockSpec(memory_space=pl.ANY)] * (size + 4),
            ],
            out_specs=[
                pl.BlockSpec((count, rows), whose),
                pl.BlockSpec((count, rows), whose),
                pl.BlockSpec(
                    (1, rows, columns), lambda t, place: (jnp.clip(t - tiles, 0, half - 1), 0, 0)
                ),
                pl.BlockSpec(
                    (1, rows, columns),
                    lambda t, place: (jnp.clip(t - tiles - half, 0, half - 1), 0, 0),
                ),
            ],
            scratch_shapes=[
                pltpu.VMEM((size * rows, columns), bf16),
                pltpu.VMEM((count, D), bf16),
                pltpu.VMEM((count, D), bf16),
                pltpu.VMEM((count, ffe), bf16),
                pltpu.VMEM((count, 2 * ffe), bf16),
                pltpu.SemaphoreType.DMA((size + 4,)),
            ],
        ),
        compiler_params=pltpu.CompilerParams(
            dimension_semantics=("arbitrary",), vmem_limit_bytes=60 * 2**20
        ),
        cost_estimate=pl.CostEstimate(
            flops=18 * count * D * ffe,
            bytes_accessed=8 * count * D + 4 * size * rows * columns,
            transcendentals=count * ffe,
        ),
        name="expert",
    )(place, share, *slots, *grad_slots, *pieces)


class GradChain:
    def __init__(self, send, keep):
        self.bit, self.size = 1, lax.axis_size("fsdp")
        self.terms, self.send = [keep], send

    def sums(self):
        if self.bit == self.size:
            return self.terms[-1]
        received = swap(self.send, "fsdp", self.bit)
        self.terms.append(received)
        self.bit *= 2
        many = self.terms[0].shape[0] // 2
        if many:
            total = sum(t[many:].astype(f32) for t in self.terms)
            self.send = total.astype(bf16)
            self.terms = [t[:many] for t in self.terms]
            return self.send
        return received

    def ended(self):
        other = self.terms.pop()[0]
        return sum(t[0].astype(f32) for t in self.terms).astype(bf16), other


def to_group(rows, *others):
    own = lax.all_gather(rows, "seq", axis=0, tiled=False)
    swapped = swap(after(rows, *others), "fsdp", lax.axis_size("fsdp") // 2)
    return own, lax.all_gather(swapped, "seq", axis=0, tiled=False), swapped


def from_group(sums_own, sums_other):
    mine = lax.psum_scatter(sums_other, "seq", scatter_dimension=0, tiled=True)
    other = swap(mine, "fsdp", lax.axis_size("fsdp") // 2)
    mine = lax.psum_scatter(sums_own, "seq", scatter_dimension=0, tiled=True)
    return mine.astype(f32) + other.astype(f32)


def body(
    tokens, lengths, routes, gates, gain_attn, gain_moe, w_qkv, w_out, w_gate_up, w_down, cotangent
):
    n_seq, n_fsdp = lax.axis_size("seq"), lax.axis_size("fsdp")
    at_seq, at_fsdp = lax.axis_index("seq"), lax.axis_index("fsdp")
    rows = tokens.shape[1]
    shard = D // n_fsdp
    local_count = w_gate_up.shape[0]
    per_half = local_count // 2
    half = at_fsdp // (n_fsdp // 2)
    heads_here = HEADS // n_seq
    width = heads_here * HEAD
    span_len = rows * n_seq

    packed = jnp.concatenate(
        [w_gate_up.reshape(local_count, shard, 2 * FFE), jnp.swapaxes(w_down, 1, 2)], axis=2
    )
    own_part = lax.dynamic_slice_in_dim(packed, half * per_half, per_half, 0)
    other_part = lax.dynamic_slice_in_dim(packed, (1 - half) * per_half, per_half, 0)
    x_all = gather_rows(tokens[0], "seq")
    part = lax.dynamic_slice_in_dim(
        w_qkv.reshape(shard, 3, HEADS, HEAD), at_seq * heads_here, heads_here, 2
    ).reshape(shard, 3 * width)
    gains = jnp.zeros((shard, 128), bf16).at[:, 0].set(gain_attn).at[:, 1].set(gain_moe)
    gathered = lax.all_gather(
        jnp.concatenate([part, gains], axis=1), "fsdp", axis=0, tiled=True
    )
    qkv_own = gathered[:, : 3 * width]
    gain_a = gathered[:, 3 * width].astype(f32)
    gain_m = gathered[:, 3 * width + 1].astype(f32)
    out_full = lax.all_gather(after(w_out, x_all), "fsdp", axis=0, tiled=True)
    cot_other = swap(cotangent[0], "fsdp", n_fsdp // 2)

    routing = jnp.concatenate([routes[0].astype(f32), gates[0]], axis=1)
    routing = jnp.stack(to_group(routing)[:2]).reshape(2 * n_seq, rows, 2 * TOP)
    capacity = rows * TOP * 4 // (3 * local_count * n_seq) + 2
    capacity = -(-capacity // 8) * 8
    named = at_seq * local_count + half * per_half + lax.iota(jnp.int32, per_half)
    hits = routing[:, :, :TOP, None].astype(jnp.int32) == named
    mask = jnp.any(hits, axis=2)
    weight = jnp.sum(jnp.where(hits, routing[:, :, TOP:, None], 0.0), axis=2)
    below = (lax.iota(jnp.int32, rows)[:, None] > lax.iota(jnp.int32, rows)[None, :]).astype(bf16)
    rank = jnp.einsum("rq,bqe->bre", below, mask.astype(bf16), preferred_element_type=f32)
    rank = jnp.where(mask, rank.astype(jnp.int32), -1)
    picks = jnp.swapaxes(rank, 1, 2)[:, :, None, :] == lax.iota(jnp.int32, capacity)[:, None]
    share = jnp.sum(
        jnp.where(picks, jnp.swapaxes(weight, 1, 2)[:, :, None, :], 0.0), axis=3
    )
    picks = picks.astype(bf16)

    def normed_rows(values, gain):
        inverse = lax.rsqrt(jnp.mean(values * values, axis=1, keepdims=True) + epsilon)
        return (values * inverse * gain).astype(bf16), inverse

    x_all = after(x_all, own_part, other_part, picks, share, cot_other)
    normed_a, inv_all = normed_rows(x_all.astype(f32), gain_a)
    qkv = dot(normed_a, qkv_own, ((1,), (0,))).astype(bf16)
    segment = segment_ids(lengths[0], span_len)
    attended = attend(qkv, segment)
    heads_rows = lax.all_to_all(attended, "seq", split_axis=0, concat_axis=1, tiled=True)
    cot_own = gather_rows(after(cotangent[0], x_all), "seq")
    cot_all = [cot_own, gather_rows(after(cot_other, x_all), "seq")]
    cot_all = [rows_of.reshape(n_seq, rows, D) for rows_of in cot_all]
    begun = [start_expert(own_part[:1], other_part[:1])]
    heads_rows = after(heads_rows, cot_own, *begun[0].values())
    x_float = tokens[0].astype(f32)
    resid = x_float + dot(heads_rows, out_full, ((1,), (0,)))
    normed_m, inv_m = normed_rows(resid, gain_m)
    moe_all = to_group(normed_m)

    for i in range(1, per_half):
        begun.append(start_expert(own_part[i : i + 1], other_part[i : i + 1], attended))
    experts = [finish_expert(pieces) for pieces in begun]

    place = jnp.full((1,), at_fsdp, jnp.int32)
    forward_parts, backward_parts, chains = [], [], []
    def dispatch(i, g, source, weighted):
        at = slice(g * n_seq, (g + 1) * n_seq)
        part = dot(picks[at, i], source, ((2,), (1,)), ((0,), (0,)))
        if weighted:
            part = part * share[at, i, :, None]
        return part.astype(bf16).reshape(-1, D)

    grad_slots = [[dispatch(i, g, cot_all[g], True) for g in range(2)] for i in range(per_half)]
    for i in range(per_half):
        ready = list(backward_parts[-1:]) + [experts[i][j] for j in range(n_fsdp - 1)]
        if i + 1 < per_half:
            ready.extend(begun[i + 1].values())
        if i >= 2:
            ready.append(chains[i - 2].sums())
        if i >= 3:
            ready.append(chains[i - 3].sums())
        slots = [dispatch(i, g, after(moe_all[g], *ready), False) for g in range(2)]
        if i == 0:
            slots[0] = after(slots[0], *[part for parts in grad_slots for part in parts])
        made, back, send, keep = run_expert(
            place, share[:, i].reshape(-1, 1), slots, grad_slots[i], experts[i], 0
        )
        forward_parts.append(made.reshape(2, n_seq, capacity, D))
        backward_parts.append(back.reshape(2, n_seq, capacity, D))
        chains.append(GradChain(send, keep))

    every_pick = picks.reshape(2, n_seq, per_half * capacity, rows)

    def combine(parts, *others):
        sums = []
        for g in range(2):
            together = after(jnp.concatenate([part[g] for part in parts], axis=1), *others)
            total = dot(every_pick[g], together, ((1,), (1,)), ((0,), (0,)))
            sums.append(total.astype(bf16).reshape(span_len, D))
        return sums

    backward_sums = combine(backward_parts, *[chain.sums() for chain in chains[:-1]])
    grad_normed_m = from_group(*backward_sums)
    forward_sums = combine(forward_parts, *backward_sums, chains[-1].sums())
    grad_normed_m = after(grad_normed_m, *forward_sums)

    scaled_m = grad_normed_m * gain_m
    grad_resid = (
        cotangent[0].astype(f32)
        + inv_m * scaled_m
        - inv_m * inv_m * inv_m * resid * jnp.mean(scaled_m * resid, axis=1, keepdims=True)
    )
    grad_gain_m = jnp.sum(grad_normed_m * resid * inv_m, axis=0)
    grad_attn = grad_resid.astype(bf16)
    mixed = (resid + from_group(*forward_sums)).astype(bf16)
    grad_heads_rows = dot(grad_attn, out_full, ((1,), (1,))).astype(bf16)
    grad_heads = lax.all_to_all(
        grad_heads_rows, "seq", split_axis=1, concat_axis=0, tiled=True
    )
    grad_heads = after(grad_heads, chains[-1].sums())
    out_sum = None
    for k in range(n_seq):
        columns = lax.dynamic_slice_in_dim(grad_attn, (at_seq ^ k) * width, width, 1)
        part = dot(heads_rows, columns, ((0,), (0,))).astype(bf16)
        part = (swap(part, "seq", k) if k else part).astype(f32)
        out_sum = part if out_sum is None else out_sum + part
    out_sum = lax.psum_scatter(out_sum.astype(bf16), "fsdp", scatter_dimension=0, tiled=True)
    out_sum = unpack_columns(lax.all_gather(out_sum, "seq", axis=0, tiled=False), width, 1)

    grad_qkv = attend(qkv, segment, grad_heads)
    grad_qkv = after(grad_qkv, mixed, *[chain.sums() for chain in chains])
    part_normed_a = dot(grad_qkv, qkv_own, ((1,), (1,)))
    grad_normed_a = scatter_rows(part_normed_a.astype(bf16), "seq")
    part_gain_a = jnp.sum(part_normed_a * x_all.astype(f32) * inv_all, axis=0)
    gain_columns = jnp.zeros((D, 128), bf16)
    gain_columns = gain_columns.at[:, 0].set(part_gain_a.astype(bf16))
    gain_columns = gain_columns.at[:, 1].set(grad_gain_m.astype(bf16))
    grad_qkv_w = dot(normed_a, grad_qkv, ((0,), (0,))).astype(bf16)
    qkv_sum = lax.psum_scatter(
        jnp.concatenate([grad_qkv_w, gain_columns], axis=1), "fsdp", scatter_dimension=0, tiled=True
    )
    qkv_sum = after(qkv_sum, grad_normed_a, *[chain.sums() for chain in chains])
    qkv_sum = lax.all_gather(qkv_sum, "seq", axis=0, tiled=False)
    gain_sums = jnp.sum(qkv_sum[:, :, 3 * width : 3 * width + 2].astype(f32), axis=0)
    qkv_sum = unpack_columns(qkv_sum, width, 3)
    inv_a = lax.rsqrt(jnp.mean(x_float * x_float, axis=1, keepdims=True) + epsilon)
    scaled_a = grad_normed_a * gain_a
    grad_x = (
        grad_resid
        + inv_a * scaled_a
        - inv_a * inv_a * inv_a * x_float * jnp.mean(scaled_a * x_float, axis=1, keepdims=True)
    )

    for chain in chains:
        while chain.bit < n_fsdp:
            chain.sums()
    ended = [chain.ended() for chain in chains]
    own_grads, other_grads = jnp.stack([e[0] for e in ended]), jnp.stack([e[1] for e in ended])
    first = half == 0
    grad_all = jnp.concatenate(
        [jnp.where(first, own_grads, other_grads), jnp.where(first, other_grads, own_grads)]
    ).astype(f32)
    return (
        mixed[None],
        grad_x.astype(bf16)[None],
        gain_sums[:, 0],
        gain_sums[:, 1],
        qkv_sum,
        out_sum,
        grad_all[:, :, : 2 * FFE].reshape(local_count, shard, 2, FFE),
        jnp.swapaxes(grad_all[:, :, 2 * FFE :], 1, 2),
    )


def solution(mesh):
    placed = (
        P("fsdp", "seq", None),
        P("fsdp", None),
        P("fsdp", "seq", None),
        P("fsdp", "seq", None),
        P("fsdp"),
        P("fsdp"),
        P("fsdp", None),
        P("fsdp", None),
        P("seq", "fsdp", None, None),
        P("seq", None, "fsdp"),
        P("fsdp", "seq", None),
    )
    return jax.shard_map(
        body,
        mesh=mesh,
        in_specs=placed,
        out_specs=(
            P("fsdp", "seq", None),
            P("fsdp", "seq", None),
            P("fsdp"),
            P("fsdp"),
            P("fsdp", None),
            P("fsdp", None),
            P("seq", "fsdp", None, None),
            P("seq", None, "fsdp"),
        ),
        check_vma=False,
    )
```

```python
import jax
import jax.numpy as jnp
from jax import lax
from jax.experimental import pallas as pl
from jax.experimental.pallas import tpu as pltpu
from jax.sharding import PartitionSpec as P

D = 2048
HEADS = 16
HEAD = 128
FFE = 1024
TOP = 8

epsilon = 1e-06
f32 = jnp.float32
bf16 = jnp.bfloat16


def swap(value, axis, bit):
    size = lax.axis_size(axis)
    return lax.ppermute(value, axis, [(i, i ^ bit) for i in range(size)])


def dot(a, b, contract, batch=((), ())):
    return lax.dot_general(a, b, (contract, batch), preferred_element_type=f32)


def segment_ids(length_row, span_len):
    ends = jnp.cumsum(length_row)
    places = lax.iota(jnp.int32, span_len)
    return jnp.sum((places[:, None] >= ends[None, :]).astype(jnp.int32), axis=1)


def score_probs(keys, queries, seg_column, seg_row):
    raw = dot(keys, queries, ((1,), (1,)))
    raw = jnp.where(seg_column == seg_row, raw, -1e30)
    top = jnp.max(raw, axis=0, keepdims=True)
    part = jnp.exp((raw - top) * HEAD ** (-0.5))
    return part * (1.0 / jnp.sum(part, axis=0, keepdims=True))


def head_columns(heads_here, head):
    return [
        pl.ds(pl.multiple_of((third * heads_here + head) * HEAD, HEAD), HEAD) for third in range(3)
    ]


def attend_forward_kernel(heads_here, qkv_ref, seg_column, seg_row, out_ref):
    block = out_ref.shape[0]
    at = pl.ds(pl.multiple_of(pl.program_id(1) * block, block), block)
    q_at, k_at, v_at = head_columns(heads_here, pl.program_id(0))
    probs = score_probs(qkv_ref[:, k_at], qkv_ref[at, q_at], seg_column[...], seg_row[...])
    out_ref[...] = dot(qkv_ref[:, v_at], probs.astype(bf16), ((0,), (0,))).T.astype(bf16)


def attend_backward_kernel(
    heads_here, qkv_ref, grad_ref, seg_column, seg_row, out_ref, grad_k, grad_v
):
    block = grad_ref.shape[0]
    turn = pl.program_id(1)
    at = pl.ds(pl.multiple_of(turn * block, block), block)
    q_at, k_at, v_at = head_columns(heads_here, pl.program_id(0))
    queries, keys, grads = qkv_ref[at, q_at], qkv_ref[:, k_at], grad_ref[...]
    probs = score_probs(keys, queries, seg_column[...], seg_row[...])
    grad_probs = dot(qkv_ref[:, v_at], grads, ((1,), (1,)))
    inner = jnp.sum(probs * grad_probs, axis=0, keepdims=True)
    grad_scores = (probs * (grad_probs - inner)).astype(bf16)
    scale = HEAD ** (-0.5)

    @pl.when(turn == 0)
    def _():
        grad_k[...] = jnp.zeros_like(grad_k)
        grad_v[...] = jnp.zeros_like(grad_v)

    grad_v[...] += dot(probs.astype(bf16), grads, ((1,), (0,)))
    grad_k[...] += dot(grad_scores, queries, ((1,), (0,)))
    out_ref[at, q_at] = (dot(keys, grad_scores, ((0,), (0,))).T * scale).astype(bf16)

    @pl.when(turn == pl.num_programs(1) - 1)
    def _():
        out_ref[:, k_at] = (grad_k[...] * scale).astype(bf16)
        out_ref[:, v_at] = grad_v[...].astype(bf16)


def attend(qkv, segment, grad=None):
    span_len, columns = qkv.shape
    heads_here = columns // (3 * HEAD)
    blocks = 3
    block = span_len // blocks
    whole = pl.BlockSpec((span_len, columns), lambda h, i: (0, 0), pipeline_mode=pl.Buffered(1))
    cut = pl.BlockSpec((block, HEAD), lambda h, i: (i, h))
    segments = [
        pl.BlockSpec((span_len, 1), lambda h, i: (0, 0)),
        pl.BlockSpec((1, block), lambda h, i: (0, i)),
    ]
    backward = grad is not None
    return pl.pallas_call(
        lambda *refs: (attend_backward_kernel if backward else attend_forward_kernel)(
            heads_here, *refs
        ),
        out_shape=jax.ShapeDtypeStruct((span_len, columns if backward else columns // 3), bf16),
        grid=(heads_here, blocks),
        in_specs=[whole, *[cut] * backward, *segments],
        out_specs=pl.BlockSpec((span_len, columns), lambda h, i: (0, 0)) if backward else cut,
        scratch_shapes=[pltpu.VMEM((span_len, HEAD), f32)] * (2 * backward),
        compiler_params=pltpu.CompilerParams(
            dimension_semantics=("arbitrary", "arbitrary"), vmem_limit_bytes=60 * 2**20
        ),
        cost_estimate=pl.CostEstimate(
            flops=(40 if backward else 20) * span_len * span_len * HEAD * heads_here,
            bytes_accessed=4 * span_len * columns,
            transcendentals=span_len * span_len * heads_here,
        ),
        name="attend_backward" if backward else "attend_forward",
    )(*[qkv, *[grad] * backward, segment.reshape(span_len, 1), segment.reshape(1, span_len)])


def unpack_kernel(in_ref, out_ref):
    out_ref[...] = in_ref[0].astype(f32)


def unpack_columns(gathered, width, thirds):
    n_seq, rows, _ = gathered.shape
    return pl.pallas_call(
        unpack_kernel,
        out_shape=jax.ShapeDtypeStruct((rows, thirds * n_seq * width), f32),
        grid=(n_seq, thirds),
        in_specs=[pl.BlockSpec((1, rows, width), lambda s, p: (s, 0, p))],
        out_specs=pl.BlockSpec((rows, width), lambda s, p: (0, p * n_seq + s)),
        name="unpack",
    )(gathered)


def after(value, *others):
    if not others:
        return value
    return lax.optimization_barrier((value, *others))[0]


def reversed_bits(index, size):
    count, total = size.bit_length() - 1, 0
    for bit in range(count):
        total = total + (((index >> bit) & 1) << (count - 1 - bit))
    return total


def start_expert(mine, sent, *start):
    size = lax.axis_size("fsdp")
    mine, sent = after(mine, *start), after(sent, *start)
    pieces = {size // 2: swap(sent, "fsdp", size // 2)}
    bit = size // 4
    while bit > 1:
        pieces[bit] = swap(mine, "fsdp", bit)
        bit //= 2
    return pieces


def finish_expert(pieces, *start):
    size = lax.axis_size("fsdp")
    pieces = dict(pieces)
    for j in sorted(range(2, size, 2), key=lambda j: j.bit_count()):
        if j not in pieces:
            low = j & -j
            pieces[j] = swap(after(pieces[j ^ low], *start), "fsdp", low)
    return [pieces[j] for j in range(2, size, 2)]


def gather_rows(piece, axis, *others):
    place, rows = lax.axis_index(axis), piece.shape[0]
    whole = jnp.zeros((lax.axis_size(axis) * rows, *piece.shape[1:]), piece.dtype)
    for k in range(lax.axis_size(axis)):
        part = swap(piece, axis, k) if k else after(piece, *others)
        whole = lax.dynamic_update_slice_in_dim(whole, part, (place ^ k) * rows, 0)
    return whole


def scatter_rows(sums, axis):
    place, rows = lax.axis_index(axis), sums.shape[0] // lax.axis_size(axis)
    parts = [
        lax.dynamic_slice_in_dim(sums, (place ^ k) * rows, rows, 0)
        for k in range(lax.axis_size(axis))
    ]
    return sum((swap(part, axis, k) if k else part).astype(f32) for k, part in enumerate(parts))


def expert_kernel(size, tiles, parts, place_ref, share_ref, *rest):
    arrays = 1 + max(array for array, _ in parts)
    slots, pieces, rest = rest[:4], rest[4 : 4 + arrays], rest[4 + arrays :]
    made_refs, back_refs, rest = rest[:2], rest[2:4], rest[4:]
    send_ref, keep_ref, weights, x_ref, g_ref, act, grad_proj, sems = rest
    step = pl.program_id(0)
    place = place_ref[0]
    rows = weights.shape[0] // size
    ffe = act.shape[1]
    wide = ffe // tiles
    nn, nt, tn = ((1,), (0,)), ((1,), (1,)), ((0,), (0,))

    @pl.when(step == 0)
    def _():
        copies = [
            pltpu.make_async_copy(
                pieces[parts[j][0]].at[parts[j][1]],
                weights.at[pl.ds(pl.multiple_of((place ^ j) * rows, rows), rows)],
                sems.at[j],
            )
            for j in range(size)
        ]
        count = slots[0].shape[0]
        for k, slot in enumerate(slots):
            copies.append(
                pltpu.make_async_copy(
                    slot,
                    (x_ref, g_ref)[k // 2].at[pl.ds(k % 2 * count, count)],
                    sems.at[size + k],
                )
            )
        for copy in copies:
            copy.start()
        for copy in copies:
            copy.wait()

    @pl.when(step < tiles)
    def _():
        first = pl.multiple_of(step * wide, wide)
        gate = dot(x_ref[...], weights[:, pl.ds(first, wide)], nn)
        up = dot(x_ref[...], weights[:, pl.ds(pl.multiple_of(ffe + first, wide), wide)], nn)
        grad_act = dot(
            g_ref[...], weights[:, pl.ds(pl.multiple_of(2 * ffe + first, wide), wide)], nn
        )
        sigma = 1.0 / (1.0 + jnp.exp(-gate))
        silu = gate * sigma
        act[:, pl.ds(first, wide)] = (silu * up).astype(bf16)
        grad_proj[:, pl.ds(first, wide)] = (
            grad_act * up * (sigma * (1.0 + gate * (1.0 - sigma)))
        ).astype(bf16)
        grad_proj[:, pl.ds(pl.multiple_of(ffe + first, wide), wide)] = (grad_act * silu).astype(
            bf16
        )

    @pl.when(step >= tiles)
    def _():
        turn = step - tiles
        whose = place ^ reversed_bits((turn + size // 2) % size, size)
        at = pl.ds(pl.multiple_of(whose * rows, rows), rows)
        count = act.shape[0] // 2
        made = (share_ref[...] * dot(act[...], weights[at, 2 * ffe :], nt)).astype(bf16)
        back = dot(grad_proj[...], weights[at, : 2 * ffe], nt).astype(bf16)
        for g in range(2):
            made_refs[g][...] = made[g * count : (g + 1) * count]
            back_refs[g][...] = back[g * count : (g + 1) * count]

        def grads(out_ref):
            out_ref[0, :, : 2 * ffe] = dot(x_ref[:, at], grad_proj[...], tn).astype(bf16)
            out_ref[0, :, 2 * ffe :] = dot(g_ref[:, at], act[...], tn).astype(bf16)

        @pl.when(turn < size // 2)
        def _():
            grads(send_ref)

        @pl.when(turn >= size // 2)
        def _():
            grads(keep_ref)


def run_expert(place, share, slots, grad_slots, pieces, parts):
    size, (_, rows, columns) = len(parts), pieces[0].shape
    count = 2 * slots[0].shape[0]
    ffe = columns // 3
    tiles = 4
    half = size // 2

    def whose(step, place):
        turn = jnp.maximum(step - tiles, 0)
        return 0, place[0] ^ reversed_bits((turn + half) % size, size)

    return pl.pallas_call(
        lambda *refs: expert_kernel(size, tiles, parts, *refs),
        out_shape=[
            *[jax.ShapeDtypeStruct((count // 2, D), bf16)] * 4,
            jax.ShapeDtypeStruct((half, rows, columns), bf16),
            jax.ShapeDtypeStruct((half, rows, columns), bf16),
        ],
        grid_spec=pltpu.PrefetchScalarGridSpec(
            num_scalar_prefetch=1,
            grid=(tiles + size,),
            in_specs=[
                pl.BlockSpec((count, 1), lambda step, place: (0, 0)),
                *[pl.BlockSpec(memory_space=pl.ANY)] * (len(pieces) + 4),
            ],
            out_specs=[
                *[pl.BlockSpec((count // 2, rows), whose)] * 4,
                pl.BlockSpec(
                    (1, rows, columns), lambda t, place: (jnp.clip(t - tiles, 0, half - 1), 0, 0)
                ),
                pl.BlockSpec(
                    (1, rows, columns),
                    lambda t, place: (jnp.clip(t - tiles - half, 0, half - 1), 0, 0),
                ),
            ],
            scratch_shapes=[
                pltpu.VMEM((size * rows, columns), bf16),
                pltpu.VMEM((count, D), bf16),
                pltpu.VMEM((count, D), bf16),
                pltpu.VMEM((count, ffe), bf16),
                pltpu.VMEM((count, 2 * ffe), bf16),
                pltpu.SemaphoreType.DMA((size + 4,)),
            ],
        ),
        compiler_params=pltpu.CompilerParams(
            dimension_semantics=("arbitrary",), vmem_limit_bytes=60 * 2**20
        ),
        cost_estimate=pl.CostEstimate(
            flops=18 * count * D * ffe,
            bytes_accessed=8 * count * D + 4 * size * rows * columns,
            transcendentals=count * ffe,
        ),
        name="expert",
    )(place, share, *slots, *grad_slots, *pieces)


class GradChain:
    def __init__(self, send, keep):
        self.bit, self.size = 1, lax.axis_size("fsdp")
        self.terms, self.send = [keep], send

    def arrive(self):
        if self.bit < self.size:
            self.terms.append(swap(self.send, "fsdp", self.bit))
            self.bit *= 2
        return self.terms[-1]

    def add(self, *others):
        many = self.terms[0].shape[0] // 2
        if many:
            self.terms[0] = after(self.terms[0], *others)
            self.send = sum(t[many:].astype(f32) for t in self.terms).astype(bf16)
            self.terms = [t[:many] for t in self.terms]
        return self.send

    def sums(self):
        self.arrive()
        return self.add()

    def ended(self):
        other = self.terms.pop()[0]
        return sum(t[0].astype(f32) for t in self.terms).astype(bf16), other


def body(
    tokens, lengths, routes, gates, gain_attn, gain_moe, w_qkv, w_out, w_gate_up, w_down, cotangent
):
    n_seq, n_fsdp = lax.axis_size("seq"), lax.axis_size("fsdp")
    at_seq, at_fsdp = lax.axis_index("seq"), lax.axis_index("fsdp")
    rows = tokens.shape[1]
    shard = D // n_fsdp
    local_count = w_gate_up.shape[0]
    per_half = local_count // 2
    half = at_fsdp // (n_fsdp // 2)
    heads_here = HEADS // n_seq
    width = heads_here * HEAD
    span_len = rows * n_seq

    packed = jnp.concatenate(
        [w_gate_up.reshape(local_count, shard, 2 * FFE), jnp.swapaxes(w_down, 1, 2)], axis=2
    )
    own_part = lax.dynamic_slice_in_dim(packed, half * per_half, per_half, 0)
    other_part = lax.dynamic_slice_in_dim(packed, (1 - half) * per_half, per_half, 0)
    cot_other = swap(cotangent[0], "fsdp", n_fsdp // 2)

    part = lax.dynamic_slice_in_dim(
        w_qkv.reshape(shard, 3, HEADS, HEAD), at_seq * heads_here, heads_here, 2
    ).reshape(shard, 3 * width)
    gains = jnp.zeros((shard, 128), bf16).at[:, 0].set(gain_attn).at[:, 1].set(gain_moe)
    gathered = lax.all_gather(
        jnp.concatenate([part, gains], axis=1), "fsdp", axis=0, tiled=True
    )
    qkv_own = gathered[:, : 3 * width]
    gain_a = gathered[:, 3 * width].astype(f32)
    gain_m = gathered[:, 3 * width + 1].astype(f32)

    routing = jnp.concatenate([routes[0].astype(f32), gates[0]], axis=1)
    routing = jnp.stack([routing, swap(routing, "fsdp", n_fsdp // 2)])
    routing = jnp.swapaxes(lax.all_gather(routing, "seq", axis=0, tiled=False), 0, 1)
    routing = routing.reshape(2 * n_seq, rows, 2 * TOP)
    capacity = rows * TOP * 4 // (3 * local_count * n_seq) + 2
    capacity = -(-capacity // 8) * 8
    named = at_seq * local_count + half * per_half + lax.iota(jnp.int32, per_half)
    hits = routing[:, :, :TOP, None].astype(jnp.int32) == named
    mask = jnp.any(hits, axis=2)
    weight = jnp.sum(jnp.where(hits, routing[:, :, TOP:, None], 0.0), axis=2)
    below = (lax.iota(jnp.int32, rows)[:, None] > lax.iota(jnp.int32, rows)[None, :]).astype(bf16)
    rank = jnp.einsum("rq,bqe->bre", below, mask.astype(bf16), preferred_element_type=f32)
    rank = jnp.where(mask, rank.astype(jnp.int32), -1)
    picks = jnp.swapaxes(rank, 1, 2)[:, :, None, :] == lax.iota(jnp.int32, capacity)[:, None]
    share = jnp.sum(
        jnp.where(picks, jnp.swapaxes(weight, 1, 2)[:, :, None, :], 0.0), axis=3
    )
    picks = picks.astype(bf16)

    def normed_rows(values, gain):
        inverse = lax.rsqrt(jnp.mean(values * values, axis=1, keepdims=True) + epsilon)
        return (values * inverse * gain).astype(bf16), inverse

    x_all = gather_rows(tokens[0], "seq", own_part, other_part, picks, share, cot_other)
    out_full = lax.all_gather(after(w_out, x_all), "fsdp", axis=0, tiled=True)
    normed_a, inv_all = normed_rows(x_all.astype(f32), gain_a)
    qkv = dot(normed_a, qkv_own, ((1,), (0,))).astype(bf16)
    segment = segment_ids(lengths[0], span_len)
    attended = attend(qkv, segment)
    heads_rows = lax.all_to_all(attended, "seq", split_axis=0, concat_axis=1, tiled=True)
    cot_own = gather_rows(after(cotangent[0], x_all), "seq")
    cot_all = [cot_own, gather_rows(after(cot_other, x_all), "seq")]
    cot_all = [rows_of.reshape(n_seq, rows, D) for rows_of in cot_all]
    beside = swap(after(own_part, x_all), "fsdp", 1)
    heads_rows = after(heads_rows, cot_own, beside)
    begun = [start_expert(own_part[:1], other_part[:1], out_full)]
    x_float = tokens[0].astype(f32)
    resid = x_float + dot(heads_rows, out_full, ((1,), (0,)))
    normed_m, inv_m = normed_rows(resid, gain_m)
    moe_own = lax.all_gather(normed_m, "seq", axis=0, tiled=False)
    moe_other = swap(after(normed_m, *begun[0].values()), "fsdp", n_fsdp // 2)
    experts = [finish_expert(begun[0], heads_rows)]
    moe_other = after(moe_other, moe_own, cot_all[1], *experts[0])
    moe_all = [moe_own, lax.all_gather(moe_other, "seq", axis=0, tiled=False), moe_other]

    place = jnp.full((1,), at_fsdp, jnp.int32)
    forward_parts, backward_parts, chains = [], [], []

    def dispatch(i, g, source, weighted):
        at = slice(g * n_seq, (g + 1) * n_seq)
        part = dot(picks[at, i], source, ((2,), (1,)), ((0,), (0,)))
        if weighted:
            part = part * share[at, i, :, None]
        return part.astype(bf16).reshape(-1, D)

    def begin(i, *start):
        if i < per_half:
            begun.append(start_expert(own_part[i : i + 1], other_part[i : i + 1], *start))

    grad_slots = [[dispatch(i, g, cot_all[g], True) for g in range(2)] for i in range(per_half)]
    begin(1, moe_all[2])
    begin(2, moe_all[1])
    experts.append(finish_expert(begun[1], moe_all[1]))
    for i in range(per_half):
        ready = list(experts[i])
        near = jnp.concatenate(experts[i])
        near = swap(after(near, *(backward_parts[-1][:1] if i else [])), "fsdp", 1)
        if i:
            ready.extend(backward_parts[-1])
        if i + 1 < per_half:
            ready.extend(begun[i + 1].values())
        if i >= 2:
            ready.append(chains[i - 2].sums())
        if i >= 3:
            ready.append(chains[i - 3].sums())
        slots = [dispatch(i, g, after(moe_all[g], *ready), False) for g in range(2)]
        if i == 0:
            slots[0] = after(slots[0], *[part for parts in grad_slots for part in parts])
        pieces = [own_part, beside, *experts[i], near]
        parts = [(0, i), (1, i)]
        for j in range(1, n_fsdp // 2):
            parts.extend([(j + 1, 0), (n_fsdp // 2 + 1, j - 1)])
        *made, send, keep = run_expert(
            place, share[:, i].reshape(-1, 1), slots, grad_slots[i], pieces, parts
        )
        forward_parts.append([part.reshape(n_seq, capacity, D) for part in made[:2]])
        backward_parts.append([part.reshape(n_seq, capacity, D) for part in made[2:]])
        chains.append(GradChain(send, keep))
        begin(i + 3, backward_parts[-1][0])
        if i + 2 < per_half:
            experts.append(finish_expert(begun[i + 2], backward_parts[-1][0]))

    every_pick = picks.reshape(2, n_seq, per_half * capacity, rows)

    def combine(parts, g, *others):
        together = after(jnp.concatenate([part[g] for part in parts], axis=1), *others)
        total = dot(every_pick[g], together, ((1,), (1,)), ((0,), (0,)))
        return total.astype(bf16).reshape(span_len, D)

    def scatter(sums, *others):
        return lax.psum_scatter(after(sums, *others), "seq", scatter_dimension=0, tiled=True)

    back_other = combine(backward_parts, 1, *[chain.arrive() for chain in chains[:-1]])
    back_own = combine(backward_parts, 0, back_other)
    swapped_back = swap(scatter(back_other), "fsdp", n_fsdp // 2)
    ready = [chains[-2].add(back_own), chains[-1].arrive()]
    made_other = combine(forward_parts, 1, back_own)
    made_own = combine(forward_parts, 0, made_other, *ready)
    mixed_own = scatter_rows(made_own, "seq")
    mixed_other = scatter(made_other, back_own)
    grad_normed_m = after(scatter(back_own), mixed_own).astype(f32) + swapped_back.astype(f32)

    scaled_m = grad_normed_m * gain_m
    grad_resid = (
        cotangent[0].astype(f32)
        + inv_m * scaled_m
        - inv_m * inv_m * inv_m * resid * jnp.mean(scaled_m * resid, axis=1, keepdims=True)
    )
    grad_gain_m = jnp.sum(grad_normed_m * resid * inv_m, axis=0)
    grad_attn = grad_resid.astype(bf16)
    grad_heads_rows = dot(grad_attn, out_full, ((1,), (1,))).astype(bf16)
    grad_heads = lax.all_to_all(
        grad_heads_rows, "seq", split_axis=1, concat_axis=0, tiled=True
    )
    ready = [chain.add(grad_heads_rows) for chain in (*chains[1:-2], chains[-1])]
    grad_heads = after(grad_heads, chains[-2].arrive(), *ready)
    out_sum = []
    for k in range(n_seq):
        columns = lax.dynamic_slice_in_dim(grad_attn, (at_seq ^ k) * width, width, 1)
        part = dot(heads_rows, columns, ((0,), (0,))).astype(bf16)
        out_sum.append(swap(after(part, grad_heads), "seq", k) if k else part)
    grad_qkv = attend(qkv, segment, grad_heads)
    ready = [chain.arrive() for chain in (*chains[1:-2], chains[-1])]
    grad_qkv = after(grad_qkv, mixed_other, *ready)
    mixed_other = swap(after(mixed_other, grad_qkv), "fsdp", n_fsdp // 2)
    mixed = (resid + mixed_own + mixed_other.astype(f32)).astype(bf16)

    grad_qkv_w = dot(normed_a, grad_qkv, ((0,), (0,))).astype(bf16)
    qkv_sum = lax.psum_scatter(grad_qkv_w, "fsdp", scatter_dimension=0, tiled=True)
    part_normed_a = dot(after(grad_qkv, grad_qkv_w), qkv_own, ((1,), (1,)))
    part_sent = part_normed_a.astype(bf16)
    ready = [chain.add(part_sent) for chain in chains[-2:]]
    out_sum[0] = after(out_sum[0], part_sent)
    grad_normed_a = scatter_rows(after(part_sent, *out_sum, *ready), "seq")
    out_sum = sum(part.astype(f32) for part in out_sum)
    out_sum = after(out_sum.astype(bf16), qkv_sum)
    out_sum = lax.psum_scatter(out_sum, "fsdp", scatter_dimension=0, tiled=True)
    out_sum = unpack_columns(lax.all_gather(out_sum, "seq", axis=0, tiled=False), width, 1)
    part_gain_a = jnp.sum(part_normed_a * x_all.astype(f32) * inv_all, axis=0)
    gain_sums = jnp.zeros((D, 128), bf16)
    gain_sums = gain_sums.at[:, 0].set(part_gain_a.astype(bf16))
    gain_sums = gain_sums.at[:, 1].set(grad_gain_m.astype(bf16))
    gain_sums = lax.psum_scatter(after(gain_sums, qkv_sum), "fsdp", scatter_dimension=0, tiled=True)
    gain_sums = lax.all_gather(gain_sums, "seq", axis=0, tiled=False)
    gain_sums = jnp.sum(gain_sums[:, :, :2].astype(f32), axis=0)
    qkv_sum = after(qkv_sum, grad_normed_a)
    qkv_sum = lax.all_gather(qkv_sum, "seq", axis=0, tiled=False)
    qkv_sum = unpack_columns(qkv_sum, width, 3)
    inv_a = lax.rsqrt(jnp.mean(x_float * x_float, axis=1, keepdims=True) + epsilon)
    scaled_a = grad_normed_a * gain_a
    grad_x = (
        grad_resid
        + inv_a * scaled_a
        - inv_a * inv_a * inv_a * x_float * jnp.mean(scaled_a * x_float, axis=1, keepdims=True)
    )

    for chain in chains:
        while chain.bit < n_fsdp:
            chain.sums()
    ended = [chain.ended() for chain in chains]
    own_grads, other_grads = jnp.stack([e[0] for e in ended]), jnp.stack([e[1] for e in ended])
    first = half == 0
    grad_all = jnp.concatenate(
        [jnp.where(first, own_grads, other_grads), jnp.where(first, other_grads, own_grads)]
    ).astype(f32)
    return (
        mixed[None],
        grad_x.astype(bf16)[None],
        gain_sums[:, 0],
        gain_sums[:, 1],
        qkv_sum,
        out_sum,
        grad_all[:, :, : 2 * FFE].reshape(local_count, shard, 2, FFE),
        jnp.swapaxes(grad_all[:, :, 2 * FFE :], 1, 2),
    )


def solution(mesh):
    placed = (
        P("fsdp", "seq", None),
        P("fsdp", None),
        P("fsdp", "seq", None),
        P("fsdp", "seq", None),
        P("fsdp"),
        P("fsdp"),
        P("fsdp", None),
        P("fsdp", None),
        P("seq", "fsdp", None, None),
        P("seq", None, "fsdp"),
        P("fsdp", "seq", None),
    )
    return jax.shard_map(
        body,
        mesh=mesh,
        in_specs=placed,
        out_specs=(
            P("fsdp", "seq", None),
            P("fsdp", "seq", None),
            P("fsdp"),
            P("fsdp"),
            P("fsdp", None),
            P("fsdp", None),
            P("seq", "fsdp", None, None),
            P("seq", None, "fsdp"),
        ),
        check_vma=False,
    )
```

```python
import jax
import jax.numpy as jnp
from jax import lax
from jax.experimental import pallas as pl
from jax.experimental.pallas import tpu as pltpu
from jax.sharding import PartitionSpec as P

D = 2048
HEADS = 16
HEAD = 128
FFE = 1024
TOP = 8

epsilon = 1e-06
f32 = jnp.float32
bf16 = jnp.bfloat16


def swap(value, axis, bit):
    size = lax.axis_size(axis)
    return lax.ppermute(value, axis, [(i, i ^ bit) for i in range(size)])


def dot(a, b, contract, batch=((), ())):
    return lax.dot_general(a, b, (contract, batch), preferred_element_type=f32)


def segment_ids(length_row, span_len):
    ends = jnp.cumsum(length_row)
    places = lax.iota(jnp.int32, span_len)
    return jnp.sum((places[:, None] >= ends[None, :]).astype(jnp.int32), axis=1)


def score_probs(keys, queries, seg_column, seg_row):
    raw = dot(keys, queries, ((1,), (1,)))
    raw = jnp.where(seg_column == seg_row, raw, -1e30)
    top = jnp.max(raw, axis=0, keepdims=True)
    part = jnp.exp((raw - top) * HEAD ** (-0.5))
    return part * (1.0 / jnp.sum(part, axis=0, keepdims=True))


def head_columns(heads_here, head):
    return [
        pl.ds(pl.multiple_of((third * heads_here + head) * HEAD, HEAD), HEAD) for third in range(3)
    ]


def attend_forward_kernel(heads_here, qkv_ref, seg_column, seg_row, out_ref):
    block = out_ref.shape[0]
    at = pl.ds(pl.multiple_of(pl.program_id(1) * block, block), block)
    q_at, k_at, v_at = head_columns(heads_here, pl.program_id(0))
    probs = score_probs(qkv_ref[:, k_at], qkv_ref[at, q_at], seg_column[...], seg_row[...])
    out_ref[...] = dot(qkv_ref[:, v_at], probs.astype(bf16), ((0,), (0,))).T.astype(bf16)


def attend_backward_kernel(
    heads_here, qkv_ref, grad_ref, seg_column, seg_row, out_ref, grad_k, grad_v
):
    block = grad_ref.shape[0]
    turn = pl.program_id(1)
    at = pl.ds(pl.multiple_of(turn * block, block), block)
    q_at, k_at, v_at = head_columns(heads_here, pl.program_id(0))
    queries, keys, grads = qkv_ref[at, q_at], qkv_ref[:, k_at], grad_ref[...]
    probs = score_probs(keys, queries, seg_column[...], seg_row[...])
    grad_probs = dot(qkv_ref[:, v_at], grads, ((1,), (1,)))
    inner = jnp.sum(probs * grad_probs, axis=0, keepdims=True)
    grad_scores = (probs * (grad_probs - inner)).astype(bf16)
    scale = HEAD ** (-0.5)

    @pl.when(turn == 0)
    def _():
        grad_k[...] = jnp.zeros_like(grad_k)
        grad_v[...] = jnp.zeros_like(grad_v)

    grad_v[...] += dot(probs.astype(bf16), grads, ((1,), (0,)))
    grad_k[...] += dot(grad_scores, queries, ((1,), (0,)))
    out_ref[at, q_at] = (dot(keys, grad_scores, ((0,), (0,))).T * scale).astype(bf16)

    @pl.when(turn == pl.num_programs(1) - 1)
    def _():
        out_ref[:, k_at] = (grad_k[...] * scale).astype(bf16)
        out_ref[:, v_at] = grad_v[...].astype(bf16)


def attend(qkv, segment, grad=None):
    span_len, columns = qkv.shape
    heads_here = columns // (3 * HEAD)
    blocks = 3
    block = span_len // blocks
    whole = pl.BlockSpec((span_len, columns), lambda h, i: (0, 0), pipeline_mode=pl.Buffered(1))
    cut = pl.BlockSpec((block, HEAD), lambda h, i: (i, h))
    segments = [
        pl.BlockSpec((span_len, 1), lambda h, i: (0, 0)),
        pl.BlockSpec((1, block), lambda h, i: (0, i)),
    ]
    backward = grad is not None
    return pl.pallas_call(
        lambda *refs: (attend_backward_kernel if backward else attend_forward_kernel)(
            heads_here, *refs
        ),
        out_shape=jax.ShapeDtypeStruct((span_len, columns if backward else columns // 3), bf16),
        grid=(heads_here, blocks),
        in_specs=[whole, *[cut] * backward, *segments],
        out_specs=pl.BlockSpec((span_len, columns), lambda h, i: (0, 0)) if backward else cut,
        scratch_shapes=[pltpu.VMEM((span_len, HEAD), f32)] * (2 * backward),
        compiler_params=pltpu.CompilerParams(
            dimension_semantics=("arbitrary", "arbitrary"), vmem_limit_bytes=60 * 2**20
        ),
        cost_estimate=pl.CostEstimate(
            flops=(40 if backward else 20) * span_len * span_len * HEAD * heads_here,
            bytes_accessed=4 * span_len * columns,
            transcendentals=span_len * span_len * heads_here,
        ),
        name="attend_backward" if backward else "attend_forward",
    )(*[qkv, *[grad] * backward, segment.reshape(span_len, 1), segment.reshape(1, span_len)])


def finish_kernel(in_ref, gate_ref, down_ref):
    ffe = down_ref.shape[1]
    whole = in_ref[0].astype(f32)
    gate_ref[0, :, 0, :] = whole[:, :ffe]
    gate_ref[0, :, 1, :] = whole[:, ffe : 2 * ffe]
    down_ref[0] = whole[:, 2 * ffe :].T


def finish_grads(packed):
    count, rows, columns = packed.shape
    ffe = columns // 3
    return pl.pallas_call(
        finish_kernel,
        out_shape=[
            jax.ShapeDtypeStruct((count, rows, 2, ffe), f32),
            jax.ShapeDtypeStruct((count, ffe, rows), f32),
        ],
        grid=(count,),
        in_specs=[pl.BlockSpec((1, rows, columns), lambda e: (e, 0, 0))],
        out_specs=[
            pl.BlockSpec((1, rows, 2, ffe), lambda e: (e, 0, 0, 0)),
            pl.BlockSpec((1, ffe, rows), lambda e: (e, 0, 0)),
        ],
        compiler_params=pltpu.CompilerParams(vmem_limit_bytes=60 * 2**20),
        name="finish",
    )(packed)


def unpack_kernel(in_ref, out_ref):
    out_ref[...] = in_ref[0].astype(f32)


def unpack_columns(gathered, width, thirds):
    n_seq, rows, _ = gathered.shape
    return pl.pallas_call(
        unpack_kernel,
        out_shape=jax.ShapeDtypeStruct((rows, thirds * n_seq * width), f32),
        grid=(n_seq, thirds),
        in_specs=[pl.BlockSpec((1, rows, width), lambda s, p: (s, 0, p))],
        out_specs=pl.BlockSpec((rows, width), lambda s, p: (0, p * n_seq + s)),
        name="unpack",
    )(gathered)


def after(value, *others):
    if not others:
        return value
    return lax.optimization_barrier((value, *others))[0]


def reversed_bits(index, size):
    count, total = size.bit_length() - 1, 0
    for bit in range(count):
        total = total + (((index >> bit) & 1) << (count - 1 - bit))
    return total


def start_expert(mine, sent, *start, later=()):
    size = lax.axis_size("fsdp")
    mine, sent = after(mine, *start, *later), after(sent, *start)
    pieces = {size // 2: swap(sent, "fsdp", size // 2)}
    bit = size // 4
    while bit > 1:
        pieces[bit] = swap(mine, "fsdp", bit)
        bit //= 2
    return pieces


def finish_expert(pieces, *start):
    size = lax.axis_size("fsdp")
    pieces, brought = dict(pieces), {}
    for j in sorted(range(2, size, 2), key=lambda j: j.bit_count()):
        if j not in pieces:
            low = j & -j
            pieces[j] = brought[j] = swap(after(pieces[j ^ low], *start), "fsdp", low)
    return brought


def both_cores(pieces, *start):
    size = lax.axis_size("fsdp")
    return lax.all_gather(
        after(jnp.concatenate(pieces), *start),
        "fsdp",
        axis=0,
        tiled=True,
        axis_index_groups=[[i, i + 1] for i in range(0, size, 2)],
    )


def send_rows(piece, axis, *start):
    sent = after(piece, *start)
    return [piece, *[swap(sent, axis, k) for k in range(1, lax.axis_size(axis))]]


def join_rows(pieces, axis, *others):
    place, rows = lax.axis_index(axis), pieces[0].shape[0]
    whole = jnp.zeros((len(pieces) * rows, *pieces[0].shape[1:]), pieces[0].dtype)
    for k, piece in enumerate(pieces):
        piece = piece if k else after(piece, *others)
        whole = lax.dynamic_update_slice_in_dim(whole, piece, (place ^ k) * rows, 0)
    return whole


def scatter_rows(sums, axis):
    place, rows = lax.axis_index(axis), sums.shape[0] // lax.axis_size(axis)
    parts = [
        lax.dynamic_slice_in_dim(sums, (place ^ k) * rows, rows, 0)
        for k in range(lax.axis_size(axis))
    ]
    return sum((swap(part, axis, k) if k else part).astype(f32) for k, part in enumerate(parts))


def expert_kernel(size, tiles, parts, place_ref, share_ref, *rest):
    arrays = 1 + max(part[0] for part in parts)
    slots, pieces, rest = rest[:4], rest[4 : 4 + arrays], rest[4 + arrays :]
    made_refs, back_refs, rest = rest[:2], rest[2:4], rest[4:]
    grad_ref, weights, x_ref, g_ref, act, grad_proj, sems = rest
    step = pl.program_id(0)
    place = place_ref[0]
    rows = weights.shape[0] // size
    ffe = act.shape[1]
    wide = ffe // tiles
    nn, nt, tn = ((1,), (0,)), ((1,), (1,)), ((0,), (0,))

    @pl.when(step == 0)
    def _():
        copies = [
            pltpu.make_async_copy(
                pieces[parts[j][0]].at[parts[j][1] + parts[j][2] * (1 - (place & 1))],
                weights.at[pl.ds(pl.multiple_of((place ^ j) * rows, rows), rows)],
                sems.at[j],
            )
            for j in range(size)
        ]
        count = slots[0].shape[0]
        for k, slot in enumerate(slots):
            copies.append(
                pltpu.make_async_copy(
                    slot,
                    (x_ref, g_ref)[k // 2].at[pl.ds(k % 2 * count, count)],
                    sems.at[size + k],
                )
            )
        for copy in copies:
            copy.start()
        for copy in copies:
            copy.wait()

    @pl.when(step < tiles)
    def _():
        first = pl.multiple_of(step * wide, wide)
        gate = dot(x_ref[...], weights[:, pl.ds(first, wide)], nn)
        up = dot(x_ref[...], weights[:, pl.ds(pl.multiple_of(ffe + first, wide), wide)], nn)
        grad_act = dot(
            g_ref[...], weights[:, pl.ds(pl.multiple_of(2 * ffe + first, wide), wide)], nn
        )
        sigma = 1.0 / (1.0 + jnp.exp(-gate))
        silu = gate * sigma
        act[:, pl.ds(first, wide)] = (silu * up).astype(bf16)
        grad_proj[:, pl.ds(first, wide)] = (
            grad_act * up * (sigma * (1.0 + gate * (1.0 - sigma)))
        ).astype(bf16)
        grad_proj[:, pl.ds(pl.multiple_of(ffe + first, wide), wide)] = (grad_act * silu).astype(
            bf16
        )

    @pl.when(step >= tiles)
    def _():
        turn = step - tiles
        whose = place ^ reversed_bits((turn + size // 2) % size, size)
        at = pl.ds(pl.multiple_of(whose * rows, rows), rows)
        count = act.shape[0] // 2
        made = (share_ref[...] * dot(act[...], weights[at, 2 * ffe :], nt)).astype(bf16)
        back = dot(grad_proj[...], weights[at, : 2 * ffe], nt).astype(bf16)
        for g in range(2):
            made_refs[g][...] = made[g * count : (g + 1) * count]
            back_refs[g][...] = back[g * count : (g + 1) * count]

        grad_ref[0, :, : 2 * ffe] = dot(x_ref[:, at], grad_proj[...], tn).astype(bf16)
        grad_ref[0, :, 2 * ffe :] = dot(g_ref[:, at], act[...], tn).astype(bf16)


def run_expert(place, share, slots, grad_slots, pieces, parts):
    size, (_, rows, columns) = len(parts), pieces[0].shape
    count = 2 * slots[0].shape[0]
    ffe = columns // 3
    tiles = 4
    half = size // 2

    def whose(step, place):
        turn = jnp.maximum(step - tiles, 0)
        return 0, place[0] ^ reversed_bits((turn + half) % size, size)

    def stands(step, place):
        turn = jnp.maximum(step - tiles, 0)
        core = (whose(step, place)[1]) & 1
        return core * half + turn % half, 0, 0

    return pl.pallas_call(
        lambda *refs: expert_kernel(size, tiles, parts, *refs),
        out_shape=[
            *[jax.ShapeDtypeStruct((count // 2, D), bf16)] * 4,
            jax.ShapeDtypeStruct((size, rows, columns), bf16),
        ],
        grid_spec=pltpu.PrefetchScalarGridSpec(
            num_scalar_prefetch=1,
            grid=(tiles + size,),
            in_specs=[
                pl.BlockSpec((count, 1), lambda step, place: (0, 0)),
                *[pl.BlockSpec(memory_space=pl.ANY)] * (len(pieces) + 4),
            ],
            out_specs=[
                *[pl.BlockSpec((count // 2, rows), whose)] * 4,
                pl.BlockSpec((1, rows, columns), stands),
            ],
            scratch_shapes=[
                pltpu.VMEM((size * rows, columns), bf16),
                pltpu.VMEM((count, D), bf16),
                pltpu.VMEM((count, D), bf16),
                pltpu.VMEM((count, ffe), bf16),
                pltpu.VMEM((count, 2 * ffe), bf16),
                pltpu.SemaphoreType.DMA((size + 4,)),
            ],
        ),
        compiler_params=pltpu.CompilerParams(
            dimension_semantics=("arbitrary",), vmem_limit_bytes=60 * 2**20
        ),
        cost_estimate=pl.CostEstimate(
            flops=18 * count * D * ffe,
            bytes_accessed=8 * count * D + 4 * size * rows * columns,
            transcendentals=count * ffe,
        ),
        name="expert",
    )(place, share, *slots, *grad_slots, *pieces)


class GradChain:
    def __init__(self, grad):
        self.bit, self.size = 1, lax.axis_size("fsdp")
        rows, columns = grad.shape[1:]
        core_sums = lax.psum_scatter(
            grad.reshape(-1, columns),
            "fsdp",
            scatter_dimension=0,
            tiled=True,
            axis_index_groups=[[i, i + 1] for i in range(0, self.size, 2)],
        )
        self.terms = [core_sums.reshape(-1, rows, columns)]

    def arrive(self):
        if 1 < self.bit < self.size:
            self.terms.append(swap(self.send, "fsdp", self.bit))
        self.bit = min(2 * self.bit, self.size)
        return self.terms[-1]

    def add(self, *others):
        many = self.terms[0].shape[0] // 2
        if many:
            self.terms[0] = after(self.terms[0], *others)
            self.send = sum(t[many:].astype(f32) for t in self.terms).astype(bf16)
            self.terms = [t[:many] for t in self.terms]
        return self.send

    def sums(self):
        self.arrive()
        return self.add()

    def ended(self):
        other = self.terms.pop()[0]
        return sum(t[0].astype(f32) for t in self.terms).astype(bf16), other


def body(
    tokens, lengths, routes, gates, gain_attn, gain_moe, w_qkv, w_out, w_gate_up, w_down, cotangent
):
    n_seq, n_fsdp = lax.axis_size("seq"), lax.axis_size("fsdp")
    at_seq, at_fsdp = lax.axis_index("seq"), lax.axis_index("fsdp")
    rows = tokens.shape[1]
    shard = D // n_fsdp
    local_count = w_gate_up.shape[0]
    per_half = local_count // 2
    half = at_fsdp // (n_fsdp // 2)
    heads_here = HEADS // n_seq
    width = heads_here * HEAD
    span_len = rows * n_seq

    packed = jnp.concatenate(
        [w_gate_up.reshape(local_count, shard, 2 * FFE), jnp.swapaxes(w_down, 1, 2)], axis=2
    )
    own_part = lax.dynamic_slice_in_dim(packed, half * per_half, per_half, 0)
    other_part = lax.dynamic_slice_in_dim(packed, (1 - half) * per_half, per_half, 0)
    cot_other = swap(cotangent[0], "fsdp", n_fsdp // 2)
    begun = [start_expert(own_part[:1], other_part[:1], later=(cot_other,))]
    x_parts = send_rows(tokens[0], "seq")
    cot_own = join_rows(send_rows(cotangent[0], "seq", *x_parts), "seq")

    part = lax.dynamic_slice_in_dim(
        w_qkv.reshape(shard, 3, HEADS, HEAD), at_seq * heads_here, heads_here, 2
    ).reshape(shard, 3 * width)
    gains = jnp.zeros((shard, 128), bf16).at[:, 0].set(gain_attn).at[:, 1].set(gain_moe)
    gathered = lax.all_gather(
        jnp.concatenate([part, gains], axis=1), "fsdp", axis=0, tiled=True
    )
    qkv_own = gathered[:, : 3 * width]
    gain_a = gathered[:, 3 * width].astype(f32)
    gain_m = gathered[:, 3 * width + 1].astype(f32)

    routing = jnp.concatenate([routes[0].astype(f32), gates[0]], axis=1)
    routing = jnp.stack([routing, swap(routing, "fsdp", n_fsdp // 2)])
    routing = jnp.swapaxes(lax.all_gather(routing, "seq", axis=0, tiled=False), 0, 1)
    routing = routing.reshape(2 * n_seq, rows, 2 * TOP)
    capacity = rows * TOP * 4 // (3 * local_count * n_seq) + 2
    capacity = -(-capacity // 8) * 8
    named = at_seq * local_count + half * per_half + lax.iota(jnp.int32, per_half)
    hits = routing[:, :, :TOP, None].astype(jnp.int32) == named
    mask = jnp.any(hits, axis=2)
    weight = jnp.sum(jnp.where(hits, routing[:, :, TOP:, None], 0.0), axis=2)
    below = (lax.iota(jnp.int32, rows)[:, None] > lax.iota(jnp.int32, rows)[None, :]).astype(bf16)
    rank = jnp.einsum("rq,bqe->bre", below, mask.astype(bf16), preferred_element_type=f32)
    rank = jnp.where(mask, rank.astype(jnp.int32), -1)
    picks = jnp.swapaxes(rank, 1, 2)[:, :, None, :] == lax.iota(jnp.int32, capacity)[:, None]
    share = jnp.sum(
        jnp.where(picks, jnp.swapaxes(weight, 1, 2)[:, :, None, :], 0.0), axis=3
    )
    picks = picks.astype(bf16)

    def normed_rows(values, gain):
        inverse = lax.rsqrt(jnp.mean(values * values, axis=1, keepdims=True) + epsilon)
        return (values * inverse * gain).astype(bf16), inverse

    x_all = join_rows(
        x_parts, "seq", own_part, other_part, picks, share, cot_own, begun[0][n_fsdp // 2]
    )
    out_full = lax.all_gather(after(w_out, x_all), "fsdp", axis=0, tiled=True)
    normed_a, _ = normed_rows(x_all.astype(f32), gain_a)
    qkv = dot(normed_a, qkv_own, ((1,), (0,))).astype(bf16)
    segment = segment_ids(lengths[0], span_len)
    attended = attend(qkv, segment)
    heads_rows = lax.all_to_all(attended, "seq", split_axis=0, concat_axis=1, tiled=True)
    cot_all = [cot_own, join_rows(send_rows(cot_other, "seq", cot_own), "seq")]
    cot_all = [rows_of.reshape(n_seq, rows, D) for rows_of in cot_all]
    experts = [finish_expert(begun[0], x_all)]
    heads_rows = after(heads_rows, *cot_all, *experts[0].values(), *begun[0].values())
    x_float = tokens[0].astype(f32)
    resid = x_float + dot(heads_rows, out_full, ((1,), (0,)))
    normed_m, inv_m = normed_rows(resid, gain_m)
    moe_own = lax.all_gather(normed_m, "seq", axis=0, tiled=False)
    moe_other = after(swap(normed_m, "fsdp", n_fsdp // 2), moe_own)
    moe_all = [moe_own, lax.all_gather(moe_other, "seq", axis=0, tiled=False), moe_other]

    place = jnp.full((1,), at_fsdp, jnp.int32)
    forward_parts, backward_parts, chains = [], [], []

    def dispatch(i, g, source, weighted):
        at = slice(g * n_seq, (g + 1) * n_seq)
        part = dot(picks[at, i], source, ((2,), (1,)), ((0,), (0,)))
        if weighted:
            part = part * share[at, i, :, None]
        return part.astype(bf16).reshape(-1, D)

    def begin(i, *start):
        if i < per_half:
            begun.append(start_expert(own_part[i : i + 1], other_part[i : i + 1], *start))

    begin(1, moe_all[2])
    begin(2, moe_all[1])
    beside = swap(after(own_part, normed_m), "fsdp", 1)
    near = [both_cores(list(begun[0].values()))]
    for i in range(per_half):
        first, later = begun[i], experts[i]
        ready = [near[i], *later.values()]
        last = jnp.concatenate(list(later.values()))
        last = swap(after(last, *(backward_parts[-1][:1] if i else [])), "fsdp", 1)
        if i:
            ready.extend(backward_parts[-1])
        cots = [after(cot_all[g], *ready) for g in range(2)]
        if i + 1 < per_half:
            ready.extend(begun[i + 1].values())
        if i >= 2:
            ready.append(chains[i - 2].sums())
        if i >= 3:
            ready.append(chains[i - 3].sums())
        slots = [dispatch(i, g, after(moe_all[g], *ready), False) for g in range(2)]
        grad_slots = [dispatch(i, g, cots[g], True) for g in range(2)]
        if i + 1 < per_half:
            experts.append(finish_expert(begun[i + 1], slots[1]))
            near.append(both_cores(list(begun[i + 1].values()), slots[1]))
        even = [*first, *later]
        pieces = [own_part, beside, near[i], last, *first.values(), *later.values()]
        parts = {0: (0, i, 0), 1: (1, i, 0)}
        for n, j in enumerate(even):
            parts[j] = (4 + n, 0, 0)
            parts[j + 1] = (2, n, len(first)) if j in first else (3, n - len(first), 0)
        parts = [parts[j] for j in range(n_fsdp)]
        *made, grad = run_expert(
            place, share[:, i].reshape(-1, 1), slots, grad_slots, pieces, parts
        )
        forward_parts.append([part.reshape(n_seq, capacity, D) for part in made[:2]])
        backward_parts.append([part.reshape(n_seq, capacity, D) for part in made[2:]])
        chains.append(GradChain(grad))
        begin(i + 3, backward_parts[-1][0])

    every_pick = picks.reshape(2, n_seq, per_half * capacity, rows)

    def combine(parts, g, *others):
        together = after(jnp.concatenate([part[g] for part in parts], axis=1), *others)
        total = dot(every_pick[g], together, ((1,), (1,)), ((0,), (0,)))
        return total.astype(bf16).reshape(span_len, D)

    def scatter(sums, *others):
        return lax.psum_scatter(after(sums, *others), "seq", scatter_dimension=0, tiled=True)

    back_other = combine(backward_parts, 1)
    back_own = combine(backward_parts, 0, back_other)
    swapped_back = scatter(back_other)
    grad_normed_m = scatter(back_own, swapped_back)
    swapped_back = swap(swapped_back, "fsdp", n_fsdp // 2)
    ready = [chain.arrive() for chain in chains]
    ready.extend(chain.add(back_own) for chain in chains[1:-1])
    made_other = combine(forward_parts, 1, back_own)
    made_own = combine(forward_parts, 0, made_other, *ready)
    grad_normed_m = after(grad_normed_m, made_own).astype(f32) + swapped_back.astype(f32)

    scaled_m = grad_normed_m * gain_m
    grad_resid = (
        cotangent[0].astype(f32)
        + inv_m * scaled_m
        - inv_m * inv_m * inv_m * resid * jnp.mean(scaled_m * resid, axis=1, keepdims=True)
    )
    grad_gain_m = jnp.sum(grad_normed_m * resid * inv_m, axis=0)
    grad_attn = grad_resid.astype(bf16)
    grad_heads_rows = dot(grad_attn, out_full, ((1,), (1,))).astype(bf16)
    mixed_other = scatter(made_other, grad_heads_rows)
    mixed_own = scatter(made_own, grad_heads_rows)
    grad_heads = lax.all_to_all(
        grad_heads_rows, "seq", split_axis=1, concat_axis=0, tiled=True
    )
    ready = [chains[-1].add(grad_heads_rows)]
    chains[-2].arrive()
    ready.append(chains[-2].add(grad_heads_rows))
    grad_heads = after(grad_heads, *ready)
    out_sum = []
    for k in range(n_seq):
        columns = lax.dynamic_slice_in_dim(grad_attn, (at_seq ^ k) * width, width, 1)
        part = dot(heads_rows, columns, ((0,), (0,))).astype(bf16)
        out_sum.append(part)
    grad_qkv = attend(qkv, segment, grad_heads)
    ready = [chain.arrive() for chain in chains[1:-2]]
    grad_qkv = after(grad_qkv, mixed_other, *ready)
    mixed_other = swap(mixed_other, "fsdp", n_fsdp // 2)
    mixed = (resid + mixed_own.astype(f32) + mixed_other.astype(f32)).astype(bf16)

    grad_qkv_w = dot(normed_a, grad_qkv, ((0,), (0,))).astype(bf16)
    reduced_qkv = lax.psum_scatter(grad_qkv_w, "fsdp", scatter_dimension=0, tiled=True)
    part_normed_a = dot(after(grad_qkv, grad_qkv_w), qkv_own, ((1,), (1,)))
    part_sent = part_normed_a.astype(bf16)
    chains[-1].arrive()
    ready = [chains[-1].add(part_sent)]
    out_sum = [swap(after(p, grad_qkv_w), "seq", k) if k else p for k, p in enumerate(out_sum)]
    grad_normed_a = scatter_rows(after(part_sent, *out_sum), "seq")
    qkv_sum = after(reduced_qkv, mixed_other, *ready, *out_sum[1:])
    qkv_sum = lax.all_gather(qkv_sum, "seq", axis=0, tiled=False)
    out_sum[0] = after(out_sum[0], qkv_sum)
    out_sum = sum(part.astype(f32) for part in out_sum).astype(bf16)
    gain_column = jnp.zeros((D, 128), bf16).at[:, 0].set(grad_gain_m.astype(bf16))
    out_sum = jnp.concatenate([out_sum, gain_column], axis=1)
    out_sum = lax.psum_scatter(out_sum, "fsdp", scatter_dimension=0, tiled=True)
    out_sum = lax.all_gather(out_sum, "seq", axis=0, tiled=False)
    qkv_sum = unpack_columns(qkv_sum, width, 3)
    gain_m_sum = jnp.sum(out_sum[:, :, width].astype(f32), axis=0)
    out_sum = unpack_columns(out_sum, width, 1)
    gain_a_sum = jnp.sum(w_qkv.astype(f32) * qkv_sum, axis=1) / gain_attn.astype(f32)
    inv_a = lax.rsqrt(jnp.mean(x_float * x_float, axis=1, keepdims=True) + epsilon)
    scaled_a = grad_normed_a * gain_a
    grad_x = (
        grad_resid
        + inv_a * scaled_a
        - inv_a * inv_a * inv_a * x_float * jnp.mean(scaled_a * x_float, axis=1, keepdims=True)
    )

    for chain in chains:
        while chain.bit < n_fsdp:
            chain.sums()
    ended = [chain.ended() for chain in chains]
    own_grads, other_grads = jnp.stack([e[0] for e in ended]), jnp.stack([e[1] for e in ended])
    first = half == 0
    grad_all = jnp.concatenate(
        [jnp.where(first, own_grads, other_grads), jnp.where(first, other_grads, own_grads)]
    )
    grad_gate_up, grad_down = finish_grads(grad_all)
    return (
        mixed[None],
        grad_x.astype(bf16)[None],
        gain_a_sum,
        gain_m_sum,
        qkv_sum,
        out_sum,
        grad_gate_up,
        grad_down,
    )


def solution(mesh):
    placed = (
        P("fsdp", "seq", None),
        P("fsdp", None),
        P("fsdp", "seq", None),
        P("fsdp", "seq", None),
        P("fsdp"),
        P("fsdp"),
        P("fsdp", None),
        P("fsdp", None),
        P("seq", "fsdp", None, None),
        P("seq", None, "fsdp"),
        P("fsdp", "seq", None),
    )
    return jax.shard_map(
        body,
        mesh=mesh,
        in_specs=placed,
        out_specs=(
            P("fsdp", "seq", None),
            P("fsdp", "seq", None),
            P("fsdp"),
            P("fsdp"),
            P("fsdp", None),
            P("fsdp", None),
            P("seq", "fsdp", None, None),
            P("seq", None, "fsdp"),
        ),
        check_vma=False,
    )
```

```python
import jax
import jax.numpy as jnp
from jax import lax
from jax.experimental import pallas as pl
from jax.experimental.pallas import tpu as pltpu
from jax.sharding import PartitionSpec as P

D = 2048
HEADS = 16
HEAD = 128
FFE = 1024
TOP = 8

epsilon = 1e-06
f32 = jnp.float32
bf16 = jnp.bfloat16


def swap(value, axis, bit):
    size = lax.axis_size(axis)
    return lax.ppermute(value, axis, [(i, i ^ bit) for i in range(size)])


def dot(a, b, contract, batch=((), ())):
    return lax.dot_general(a, b, (contract, batch), preferred_element_type=f32)


def segment_ids(length_row, span_len):
    ends = jnp.cumsum(length_row)
    places = lax.iota(jnp.int32, span_len)
    return jnp.sum((places[:, None] >= ends[None, :]).astype(jnp.int32), axis=1)


def score_probs(keys, queries, seg_column, seg_row):
    raw = dot(keys, queries, ((1,), (1,)))
    raw = jnp.where(seg_column == seg_row, raw, -1e30)
    top = jnp.max(raw, axis=0, keepdims=True)
    part = jnp.exp((raw - top) * HEAD ** (-0.5))
    return part * (1.0 / jnp.sum(part, axis=0, keepdims=True))


def head_columns(heads_here, head):
    return [
        pl.ds(pl.multiple_of((third * heads_here + head) * HEAD, HEAD), HEAD) for third in range(3)
    ]


def attend_forward_kernel(heads_here, qkv_ref, seg_column, seg_row, out_ref):
    block = out_ref.shape[0]
    at = pl.ds(pl.multiple_of(pl.program_id(1) * block, block), block)
    q_at, k_at, v_at = head_columns(heads_here, pl.program_id(0))
    probs = score_probs(qkv_ref[:, k_at], qkv_ref[at, q_at], seg_column[...], seg_row[...])
    out_ref[...] = dot(qkv_ref[:, v_at], probs.astype(bf16), ((0,), (0,))).T.astype(bf16)


def attend_backward_kernel(
    heads_here, qkv_ref, grad_ref, seg_column, seg_row, out_ref, grad_k, grad_v
):
    block = grad_ref.shape[0]
    turn = pl.program_id(1)
    at = pl.ds(pl.multiple_of(turn * block, block), block)
    q_at, k_at, v_at = head_columns(heads_here, pl.program_id(0))
    queries, keys, grads = qkv_ref[at, q_at], qkv_ref[:, k_at], grad_ref[...]
    probs = score_probs(keys, queries, seg_column[...], seg_row[...])
    grad_probs = dot(qkv_ref[:, v_at], grads, ((1,), (1,)))
    inner = jnp.sum(probs * grad_probs, axis=0, keepdims=True)
    grad_scores = (probs * (grad_probs - inner)).astype(bf16)
    scale = HEAD ** (-0.5)

    @pl.when(turn == 0)
    def _():
        grad_k[...] = jnp.zeros_like(grad_k)
        grad_v[...] = jnp.zeros_like(grad_v)

    grad_v[...] += dot(probs.astype(bf16), grads, ((1,), (0,)))
    grad_k[...] += dot(grad_scores, queries, ((1,), (0,)))
    out_ref[at, q_at] = (dot(keys, grad_scores, ((0,), (0,))).T * scale).astype(bf16)

    @pl.when(turn == pl.num_programs(1) - 1)
    def _():
        out_ref[:, k_at] = (grad_k[...] * scale).astype(bf16)
        out_ref[:, v_at] = grad_v[...].astype(bf16)


def attend(qkv, segment, grad=None):
    span_len, columns = qkv.shape
    heads_here = columns // (3 * HEAD)
    blocks = 3
    block = span_len // blocks
    whole = pl.BlockSpec((span_len, columns), lambda h, i: (0, 0), pipeline_mode=pl.Buffered(1))
    cut = pl.BlockSpec((block, HEAD), lambda h, i: (i, h))
    segments = [
        pl.BlockSpec((span_len, 1), lambda h, i: (0, 0)),
        pl.BlockSpec((1, block), lambda h, i: (0, i)),
    ]
    backward = grad is not None
    return pl.pallas_call(
        lambda *refs: (attend_backward_kernel if backward else attend_forward_kernel)(
            heads_here, *refs
        ),
        out_shape=jax.ShapeDtypeStruct((span_len, columns if backward else columns // 3), bf16),
        grid=(heads_here, blocks),
        in_specs=[whole, *[cut] * backward, *segments],
        out_specs=pl.BlockSpec((span_len, columns), lambda h, i: (0, 0)) if backward else cut,
        scratch_shapes=[pltpu.VMEM((span_len, HEAD), f32)] * (2 * backward),
        compiler_params=pltpu.CompilerParams(
            dimension_semantics=("arbitrary", "arbitrary"), vmem_limit_bytes=60 * 2**20
        ),
        cost_estimate=pl.CostEstimate(
            flops=(40 if backward else 20) * span_len * span_len * HEAD * heads_here,
            bytes_accessed=4 * span_len * columns,
            transcendentals=span_len * span_len * heads_here,
        ),
        name="attend_backward" if backward else "attend_forward",
    )(*[qkv, *[grad] * backward, segment.reshape(span_len, 1), segment.reshape(1, span_len)])


def finish_kernel(in_ref, gate_ref, down_ref):
    ffe = down_ref.shape[1]
    whole = in_ref[0].astype(f32)
    gate_ref[0, :, 0, :] = whole[:, :ffe]
    gate_ref[0, :, 1, :] = whole[:, ffe : 2 * ffe]
    down_ref[0] = whole[:, 2 * ffe :].T


def finish_grads(packed):
    count, rows, columns = packed.shape
    ffe = columns // 3
    return pl.pallas_call(
        finish_kernel,
        out_shape=[
            jax.ShapeDtypeStruct((count, rows, 2, ffe), f32),
            jax.ShapeDtypeStruct((count, ffe, rows), f32),
        ],
        grid=(count,),
        in_specs=[pl.BlockSpec((1, rows, columns), lambda e: (e, 0, 0))],
        out_specs=[
            pl.BlockSpec((1, rows, 2, ffe), lambda e: (e, 0, 0, 0)),
            pl.BlockSpec((1, ffe, rows), lambda e: (e, 0, 0)),
        ],
        compiler_params=pltpu.CompilerParams(vmem_limit_bytes=60 * 2**20),
        name="finish",
    )(packed)


def unpack_kernel(in_ref, out_ref):
    out_ref[...] = in_ref[0].astype(f32)


def unpack_columns(gathered, width, thirds):
    n_seq, rows, _ = gathered.shape
    return pl.pallas_call(
        unpack_kernel,
        out_shape=jax.ShapeDtypeStruct((rows, thirds * n_seq * width), f32),
        grid=(n_seq, thirds),
        in_specs=[pl.BlockSpec((1, rows, width), lambda s, p: (s, 0, p))],
        out_specs=pl.BlockSpec((rows, width), lambda s, p: (0, p * n_seq + s)),
        name="unpack",
    )(gathered)


def after(value, *others):
    if not others:
        return value
    return lax.optimization_barrier((value, *others))[0]


def reversed_bits(index, size):
    count, total = size.bit_length() - 1, 0
    for bit in range(count):
        total = total + (((index >> bit) & 1) << (count - 1 - bit))
    return total


def start_expert(mine, sent, *start, later=()):
    size = lax.axis_size("fsdp")
    mine, sent = after(mine, *start, *later), after(sent, *start)
    pieces = {size // 2: swap(sent, "fsdp", size // 2)}
    bit = size // 4
    while bit > 1:
        pieces[bit] = swap(mine, "fsdp", bit)
        bit //= 2
    return pieces


def finish_expert(pieces, *start):
    size = lax.axis_size("fsdp")
    pieces, brought = dict(pieces), {}
    for j in sorted(range(2, size, 2), key=lambda j: j.bit_count()):
        if j not in pieces:
            low = j & -j
            pieces[j] = brought[j] = swap(after(pieces[j ^ low], *start), "fsdp", low)
    return brought


def both_cores(pieces, *start):
    size = lax.axis_size("fsdp")
    return lax.all_gather(
        jnp.concatenate([after(piece, *start) for piece in pieces]),
        "fsdp",
        axis=0,
        tiled=True,
        axis_index_groups=[[i, i + 1] for i in range(0, size, 2)],
    )


def send_rows(piece, axis, *start):
    sent = after(piece, *start)
    return [piece, *[swap(sent, axis, k) for k in range(1, lax.axis_size(axis))]]


def join_rows(pieces, axis, *others):
    place, rows = lax.axis_index(axis), pieces[0].shape[0]
    whole = jnp.zeros((len(pieces) * rows, *pieces[0].shape[1:]), pieces[0].dtype)
    for k, piece in enumerate(pieces):
        piece = piece if k else after(piece, *others)
        whole = lax.dynamic_update_slice_in_dim(whole, piece, (place ^ k) * rows, 0)
    return whole


def scatter_rows(sums, axis):
    place, rows = lax.axis_index(axis), sums.shape[0] // lax.axis_size(axis)
    parts = [
        lax.dynamic_slice_in_dim(sums, (place ^ k) * rows, rows, 0)
        for k in range(lax.axis_size(axis))
    ]
    return sum((swap(part, axis, k) if k else part).astype(f32) for k, part in enumerate(parts))


def expert_kernel(size, tiles, parts, place_ref, share_ref, *rest):
    arrays = 1 + max(part[0] for part in parts)
    slots, pieces, rest = rest[:4], rest[4 : 4 + arrays], rest[4 + arrays :]
    made_refs, back_refs, rest = rest[:2], rest[2:4], rest[4:]
    grad_ref, weights, x_ref, g_ref, act, grad_proj, sems = rest
    step = pl.program_id(0)
    place = place_ref[0]
    rows = weights.shape[0] // size
    ffe = act.shape[1]
    wide = ffe // tiles
    nn, nt, tn = ((1,), (0,)), ((1,), (1,)), ((0,), (0,))

    @pl.when(step == 0)
    def _():
        copies = [
            pltpu.make_async_copy(
                pieces[parts[j][0]].at[parts[j][1] + parts[j][2] * (1 - (place & 1))],
                weights.at[pl.ds(pl.multiple_of((place ^ j) * rows, rows), rows)],
                sems.at[j],
            )
            for j in range(size)
        ]
        count = slots[0].shape[0]
        for k, slot in enumerate(slots):
            copies.append(
                pltpu.make_async_copy(
                    slot,
                    (x_ref, g_ref)[k // 2].at[pl.ds(k % 2 * count, count)],
                    sems.at[size + k],
                )
            )
        for copy in copies:
            copy.start()
        for copy in copies:
            copy.wait()

    @pl.when(step < tiles)
    def _():
        first = pl.multiple_of(step * wide, wide)
        gate = dot(x_ref[...], weights[:, pl.ds(first, wide)], nn)
        up = dot(x_ref[...], weights[:, pl.ds(pl.multiple_of(ffe + first, wide), wide)], nn)
        grad_act = dot(
            g_ref[...], weights[:, pl.ds(pl.multiple_of(2 * ffe + first, wide), wide)], nn
        )
        sigma = 1.0 / (1.0 + jnp.exp(-gate))
        silu = gate * sigma
        act[:, pl.ds(first, wide)] = (silu * up).astype(bf16)
        grad_proj[:, pl.ds(first, wide)] = (
            grad_act * up * (sigma * (1.0 + gate * (1.0 - sigma)))
        ).astype(bf16)
        grad_proj[:, pl.ds(pl.multiple_of(ffe + first, wide), wide)] = (grad_act * silu).astype(
            bf16
        )

    @pl.when(step >= tiles)
    def _():
        turn = step - tiles
        whose = place ^ reversed_bits((turn + size // 2) % size, size)
        at = pl.ds(pl.multiple_of(whose * rows, rows), rows)
        count = act.shape[0] // 2
        made = (share_ref[...] * dot(act[...], weights[at, 2 * ffe :], nt)).astype(bf16)
        back = dot(grad_proj[...], weights[at, : 2 * ffe], nt).astype(bf16)
        for g in range(2):
            made_refs[g][...] = made[g * count : (g + 1) * count]
            back_refs[g][...] = back[g * count : (g + 1) * count]

        grad_ref[0, :, : 2 * ffe] = dot(x_ref[:, at], grad_proj[...], tn).astype(bf16)
        grad_ref[0, :, 2 * ffe :] = dot(g_ref[:, at], act[...], tn).astype(bf16)


def run_expert(place, share, slots, grad_slots, pieces, parts):
    size, (_, rows, columns) = len(parts), pieces[0].shape
    count = 2 * slots[0].shape[0]
    ffe = columns // 3
    tiles = 4
    half = size // 2

    def whose(step, place):
        turn = jnp.maximum(step - tiles, 0)
        return 0, place[0] ^ reversed_bits((turn + half) % size, size)

    def stands(step, place):
        turn = jnp.maximum(step - tiles, 0)
        core = (whose(step, place)[1]) & 1
        return core * half + turn % half, 0, 0

    return pl.pallas_call(
        lambda *refs: expert_kernel(size, tiles, parts, *refs),
        out_shape=[
            *[jax.ShapeDtypeStruct((count // 2, D), bf16)] * 4,
            jax.ShapeDtypeStruct((size, rows, columns), bf16),
        ],
        grid_spec=pltpu.PrefetchScalarGridSpec(
            num_scalar_prefetch=1,
            grid=(tiles + size,),
            in_specs=[
                pl.BlockSpec((count, 1), lambda step, place: (0, 0)),
                *[pl.BlockSpec(memory_space=pl.ANY)] * (len(pieces) + 4),
            ],
            out_specs=[
                *[pl.BlockSpec((count // 2, rows), whose)] * 4,
                pl.BlockSpec((1, rows, columns), stands),
            ],
            scratch_shapes=[
                pltpu.VMEM((size * rows, columns), bf16),
                pltpu.VMEM((count, D), bf16),
                pltpu.VMEM((count, D), bf16),
                pltpu.VMEM((count, ffe), bf16),
                pltpu.VMEM((count, 2 * ffe), bf16),
                pltpu.SemaphoreType.DMA((size + 4,)),
            ],
        ),
        compiler_params=pltpu.CompilerParams(
            dimension_semantics=("arbitrary",), vmem_limit_bytes=60 * 2**20
        ),
        cost_estimate=pl.CostEstimate(
            flops=18 * count * D * ffe,
            bytes_accessed=8 * count * D + 4 * size * rows * columns,
            transcendentals=count * ffe,
        ),
        name="expert",
    )(place, share, *slots, *grad_slots, *pieces)


class GradChain:
    def __init__(self, grad):
        self.bit, self.size = 1, lax.axis_size("fsdp")
        rows, columns = grad.shape[1:]
        core_sums = lax.psum_scatter(
            grad.reshape(-1, columns),
            "fsdp",
            scatter_dimension=0,
            tiled=True,
            axis_index_groups=[[i, i + 1] for i in range(0, self.size, 2)],
        )
        self.terms = [core_sums.reshape(-1, rows, columns)]

    def arrive(self):
        if 1 < self.bit < self.size:
            self.terms.append(swap(self.send, "fsdp", self.bit))
        self.bit = min(2 * self.bit, self.size)
        return self.terms[-1]

    def add(self, *others):
        many = self.terms[0].shape[0] // 2
        if many:
            if others:
                count = len(self.terms)
                self.terms = list(lax.optimization_barrier((*self.terms, *others))[:count])
            self.send = sum(t[many:].astype(f32) for t in self.terms).astype(bf16)
            self.terms = [t[:many] for t in self.terms]
        return self.send

    def sums(self):
        self.arrive()
        return self.add()

    def ended(self):
        other = self.terms.pop()[0]
        return sum(t[0].astype(f32) for t in self.terms).astype(bf16), other


def body(
    tokens, lengths, routes, gates, gain_attn, gain_moe, w_qkv, w_out, w_gate_up, w_down, cotangent
):
    n_seq, n_fsdp = lax.axis_size("seq"), lax.axis_size("fsdp")
    at_seq, at_fsdp = lax.axis_index("seq"), lax.axis_index("fsdp")
    rows = tokens.shape[1]
    shard = D // n_fsdp
    local_count = w_gate_up.shape[0]
    per_half = local_count // 2
    half = at_fsdp // (n_fsdp // 2)
    heads_here = HEADS // n_seq
    width = heads_here * HEAD
    span_len = rows * n_seq

    packed = jnp.concatenate(
        [w_gate_up.reshape(local_count, shard, 2 * FFE), jnp.swapaxes(w_down, 1, 2)], axis=2
    )
    own_part = lax.dynamic_slice_in_dim(packed, half * per_half, per_half, 0)
    other_part = lax.dynamic_slice_in_dim(packed, (1 - half) * per_half, per_half, 0)
    cot_other = swap(cotangent[0], "fsdp", n_fsdp // 2)
    x_parts = send_rows(tokens[0], "seq")
    cot_own = join_rows(send_rows(cotangent[0], "seq", *x_parts), "seq")

    part = lax.dynamic_slice_in_dim(
        w_qkv.reshape(shard, 3, HEADS, HEAD), at_seq * heads_here, heads_here, 2
    ).reshape(shard, 3 * width)
    gains = jnp.zeros((shard, 128), bf16).at[:, 0].set(gain_attn).at[:, 1].set(gain_moe)
    gathered = lax.all_gather(
        jnp.concatenate([part, gains], axis=1), "fsdp", axis=0, tiled=True
    )
    qkv_own = gathered[:, : 3 * width]
    gain_a = gathered[:, 3 * width].astype(f32)
    gain_m = gathered[:, 3 * width + 1].astype(f32)

    routing = jnp.concatenate([routes[0].astype(f32), gates[0]], axis=1)
    routing = jnp.stack([routing, swap(routing, "fsdp", n_fsdp // 2)])
    routing = jnp.swapaxes(lax.all_gather(routing, "seq", axis=0, tiled=False), 0, 1)
    routing = routing.reshape(2 * n_seq, rows, 2 * TOP)
    capacity = rows * TOP * 4 // (3 * local_count * n_seq) + 2
    capacity = -(-capacity // 8) * 8
    named = at_seq * local_count + half * per_half + lax.iota(jnp.int32, per_half)
    hits = routing[:, :, :TOP, None].astype(jnp.int32) == named
    mask = jnp.any(hits, axis=2)
    weight = jnp.sum(jnp.where(hits, routing[:, :, TOP:, None], 0.0), axis=2)
    below = (lax.iota(jnp.int32, rows)[:, None] > lax.iota(jnp.int32, rows)[None, :]).astype(bf16)
    rank = jnp.einsum("rq,bqe->bre", below, mask.astype(bf16), preferred_element_type=f32)
    rank = jnp.where(mask, rank.astype(jnp.int32), -1)
    picks = jnp.swapaxes(rank, 1, 2)[:, :, None, :] == lax.iota(jnp.int32, capacity)[:, None]
    share = jnp.sum(
        jnp.where(picks, jnp.swapaxes(weight, 1, 2)[:, :, None, :], 0.0), axis=3
    )
    picks = picks.astype(bf16)

    def normed_rows(values, gain):
        inverse = lax.rsqrt(jnp.mean(values * values, axis=1, keepdims=True) + epsilon)
        return (values * inverse * gain).astype(bf16), inverse

    x_all = join_rows(
        x_parts, "seq", own_part, other_part, picks, share, cot_own, cot_other
    )
    begun = [start_expert(own_part[:1], other_part[:1], x_all)]
    out_full = lax.all_gather(after(w_out, x_all), "fsdp", axis=0, tiled=True)
    normed_a, _ = normed_rows(x_all.astype(f32), gain_a)
    qkv = dot(normed_a, qkv_own, ((1,), (0,))).astype(bf16)
    segment = segment_ids(lengths[0], span_len)
    attended = attend(qkv, segment)
    heads_rows = lax.all_to_all(attended, "seq", split_axis=0, concat_axis=1, tiled=True)
    cot_all = [cot_own, join_rows(send_rows(cot_other, "seq", cot_own), "seq")]
    cot_all = [rows_of.reshape(n_seq, rows, D) for rows_of in cot_all]
    experts = [finish_expert(begun[0], x_all)]
    heads_rows = after(heads_rows, *cot_all, *experts[0].values(), *begun[0].values())
    x_float = tokens[0].astype(f32)
    resid = x_float + dot(heads_rows, out_full, ((1,), (0,)))
    normed_m, inv_m = normed_rows(resid, gain_m)
    moe_own = lax.all_gather(normed_m, "seq", axis=0, tiled=False)
    moe_other = after(swap(normed_m, "fsdp", n_fsdp // 2), moe_own)
    moe_all = [moe_own, lax.all_gather(moe_other, "seq", axis=0, tiled=False), moe_other]

    place = jnp.full((1,), at_fsdp, jnp.int32)
    forward_parts, backward_parts, chains = [], [], []

    def dispatch(i, g, source, weighted):
        at = slice(g * n_seq, (g + 1) * n_seq)
        part = dot(picks[at, i], source, ((2,), (1,)), ((0,), (0,)))
        if weighted:
            part = part * share[at, i, :, None]
        return part.astype(bf16).reshape(-1, D)

    sets = [[0], [1], list(range(2, per_half))]

    def begin(k, *start):
        cut = slice(sets[k][0], sets[k][-1] + 1)
        begun.append(start_expert(own_part[cut], other_part[cut], *start))

    begin(1, moe_all[2])
    begin(2, moe_all[1])
    beside = swap(after(own_part, normed_m), "fsdp", 1)
    near, last = [both_cores(list(begun[0].values()))], {}
    for i in range(per_half):
        k = [n for n, members in enumerate(sets) if i in members][0]
        first, later, many = begun[k], experts[k], len(sets[k])
        back = backward_parts[-1] if i else []
        ready = [near[k], *later.values(), *back]
        if k not in last:
            last[k] = swap(
                jnp.concatenate([after(p, *back[:1]) for p in later.values()]), "fsdp", 1
            )
        if i == 0:
            ready.extend(begun[1].values())
        if i == 2:
            ready.extend(begun[2].values())
        cots = [after(cot_all[g], *back) for g in range(2)]
        if i >= 2:
            ready.append(chains[i - 2].sums())
        slots = [dispatch(i, g, after(moe_all[g], *ready), False) for g in range(2)]
        grad_slots = [dispatch(i, g, cots[g], True) for g in range(2)]
        if i == 0:
            experts.append(finish_expert(begun[1], slots[1]))
            near.append(both_cores(list(begun[1].values()), slots[1]))
        even = [*first, *later]
        pieces = [own_part, beside, near[k], last[k], *first.values(), *later.values()]
        at = i - sets[k][0]
        parts = {0: (0, i, 0), 1: (1, i, 0)}
        for n, j in enumerate(even):
            parts[j] = (4 + n, at, 0)
            if j in first:
                parts[j + 1] = (2, n * many + at, len(first) * many)
            else:
                parts[j + 1] = (3, (n - len(first)) * many + at, 0)
        parts = [parts[j] for j in range(n_fsdp)]
        *made, grad = run_expert(
            place, share[:, i].reshape(-1, 1), slots, grad_slots, pieces, parts
        )
        forward_parts.append([part.reshape(n_seq, capacity, D) for part in made[:2]])
        backward_parts.append([part.reshape(n_seq, capacity, D) for part in made[2:]])
        chains.append(GradChain(grad))
        if i == 1:
            experts.append(finish_expert(begun[2], made[2]))
            near.append(both_cores(list(begun[2].values()), made[2]))

    every_pick = picks.reshape(2, n_seq, per_half * capacity, rows)

    def combine(parts, g, *others):
        together = jnp.concatenate([part[g] for part in parts], axis=1)
        if others:
            together = after(together, *others)
        total = dot(every_pick[g], together, ((1,), (1,)), ((0,), (0,)))
        return total.astype(bf16).reshape(span_len, D)

    def scatter(sums, *others):
        return lax.psum_scatter(after(sums, *others), "seq", scatter_dimension=0, tiled=True)

    back_other = combine(backward_parts, 1)
    back_own = combine(backward_parts, 0, back_other)
    swapped_back = scatter(back_other)
    grad_normed_m = scatter(back_own, swapped_back)
    swapped_back = swap(swapped_back, "fsdp", n_fsdp // 2)
    for chain in chains[-2:]:
        chain.arrive()
    ready = [chain.add(back_own) for chain in chains[-2:]]
    made_other = combine(forward_parts, 1, back_own)
    made_own = combine(forward_parts, 0, made_other, *ready)
    ready = [made_own, *[chain.arrive() for chain in chains[:-2]]]
    grad_normed_m = after(grad_normed_m, *ready).astype(f32) + swapped_back.astype(f32)

    scaled_m = grad_normed_m * gain_m
    grad_resid = (
        cotangent[0].astype(f32)
        + inv_m * scaled_m
        - inv_m * inv_m * inv_m * resid * jnp.mean(scaled_m * resid, axis=1, keepdims=True)
    )
    grad_gain_m = jnp.sum(grad_normed_m * resid * inv_m, axis=0)
    grad_attn = grad_resid.astype(bf16)
    grad_heads_rows = dot(grad_attn, out_full, ((1,), (1,))).astype(bf16)
    mixed_other = scatter(made_other, grad_heads_rows)
    mixed_own = scatter(made_own, grad_heads_rows)
    grad_heads = lax.all_to_all(
        grad_heads_rows, "seq", split_axis=1, concat_axis=0, tiled=True
    )
    for chain in chains[:-2]:
        chain.add(grad_heads_rows)
    out_sum = []
    for k in range(n_seq):
        columns = lax.dynamic_slice_in_dim(grad_attn, (at_seq ^ k) * width, width, 1)
        part = dot(heads_rows, columns, ((0,), (0,))).astype(bf16)
        out_sum.append(part)
    grad_qkv = attend(qkv, segment, grad_heads)
    grad_qkv = after(grad_qkv, mixed_other, chains[0].arrive(), chains[-2].arrive())
    mixed_other = swap(mixed_other, "fsdp", n_fsdp // 2)
    mixed = (resid + mixed_own.astype(f32) + mixed_other.astype(f32)).astype(bf16)

    grad_qkv_w = dot(normed_a, grad_qkv, ((0,), (0,))).astype(bf16)
    reduced_qkv = lax.psum_scatter(grad_qkv_w, "fsdp", scatter_dimension=0, tiled=True)
    part_normed_a = dot(after(grad_qkv, grad_qkv_w), qkv_own, ((1,), (1,)))
    part_sent = part_normed_a.astype(bf16)
    chains[-2].add(grad_qkv_w)
    ready = [part_sent, *[chain.arrive() for chain in chains[1:]]]
    ready.append(chains[-1].add(grad_qkv_w))
    out_sum = [swap(after(p, grad_qkv_w), "seq", k) if k else p for k, p in enumerate(out_sum)]
    grad_normed_a = scatter_rows(after(part_sent, *out_sum), "seq")
    qkv_sum = after(reduced_qkv, mixed_other, *ready, *out_sum[1:])
    qkv_sum = lax.all_gather(qkv_sum, "seq", axis=0, tiled=False)
    out_sum[0] = after(out_sum[0], qkv_sum, grad_normed_a)
    out_sum = sum(part.astype(f32) for part in out_sum).astype(bf16)
    gain_column = jnp.zeros((D, 128), bf16).at[:, 0].set(grad_gain_m.astype(bf16))
    out_sum = jnp.concatenate([out_sum, gain_column], axis=1)
    out_sum = lax.psum_scatter(out_sum, "fsdp", scatter_dimension=0, tiled=True)
    out_sum = lax.all_gather(out_sum, "seq", axis=0, tiled=False)
    qkv_sum = unpack_columns(qkv_sum, width, 3)
    gain_m_sum = jnp.sum(out_sum[:, :, width].astype(f32), axis=0)
    out_sum = unpack_columns(out_sum, width, 1)
    gain_a_sum = jnp.sum(w_qkv.astype(f32) * qkv_sum, axis=1) / gain_attn.astype(f32)
    inv_a = lax.rsqrt(jnp.mean(x_float * x_float, axis=1, keepdims=True) + epsilon)
    scaled_a = grad_normed_a * gain_a
    grad_x = (
        grad_resid
        + inv_a * scaled_a
        - inv_a * inv_a * inv_a * x_float * jnp.mean(scaled_a * x_float, axis=1, keepdims=True)
    )

    for chain in chains:
        while chain.bit < n_fsdp:
            chain.sums()
    ended = [chain.ended() for chain in chains]
    own_grads, other_grads = jnp.stack([e[0] for e in ended]), jnp.stack([e[1] for e in ended])
    first = half == 0
    grad_all = jnp.concatenate(
        [jnp.where(first, own_grads, other_grads), jnp.where(first, other_grads, own_grads)]
    )
    grad_gate_up, grad_down = finish_grads(grad_all)
    return (
        mixed[None],
        grad_x.astype(bf16)[None],
        gain_a_sum,
        gain_m_sum,
        qkv_sum,
        out_sum,
        grad_gate_up,
        grad_down,
    )


def solution(mesh):
    placed = (
        P("fsdp", "seq", None),
        P("fsdp", None),
        P("fsdp", "seq", None),
        P("fsdp", "seq", None),
        P("fsdp"),
        P("fsdp"),
        P("fsdp", None),
        P("fsdp", None),
        P("seq", "fsdp", None, None),
        P("seq", None, "fsdp"),
        P("fsdp", "seq", None),
    )
    return jax.shard_map(
        body,
        mesh=mesh,
        in_specs=placed,
        out_specs=(
            P("fsdp", "seq", None),
            P("fsdp", "seq", None),
            P("fsdp"),
            P("fsdp"),
            P("fsdp", None),
            P("fsdp", None),
            P("seq", "fsdp", None, None),
            P("seq", None, "fsdp"),
        ),
        check_vma=False,
    )
```

```python
import jax
import jax.numpy as jnp
from jax import lax
from jax.experimental import pallas as pl
from jax.experimental.pallas import tpu as pltpu
from jax.sharding import PartitionSpec as P

D = 2048
HEADS = 16
HEAD = 128
FFE = 1024
TOP = 8

epsilon = 1e-06
f32 = jnp.float32
bf16 = jnp.bfloat16


def swap(value, axis, bit):
    size = lax.axis_size(axis)
    return lax.ppermute(value, axis, [(i, i ^ bit) for i in range(size)])


def dot(a, b, contract, batch=((), ())):
    return lax.dot_general(a, b, (contract, batch), preferred_element_type=f32)


def segment_ids(length_row, span_len):
    ends = jnp.cumsum(length_row)
    places = lax.iota(jnp.int32, span_len)
    return jnp.sum((places[:, None] >= ends[None, :]).astype(jnp.int32), axis=1)


def score_probs(keys, queries, seg_column, seg_row):
    raw = dot(keys, queries, ((1,), (1,)))
    raw = jnp.where(seg_column == seg_row, raw, -1e30)
    top = jnp.max(raw, axis=0, keepdims=True)
    part = jnp.exp((raw - top) * HEAD ** (-0.5))
    return part * (1.0 / jnp.sum(part, axis=0, keepdims=True))


def head_columns(heads_here, head):
    return [
        pl.ds(pl.multiple_of((third * heads_here + head) * HEAD, HEAD), HEAD) for third in range(3)
    ]


def attend_forward_kernel(heads_here, qkv_ref, seg_column, seg_row, out_ref):
    block = out_ref.shape[0]
    at = pl.ds(pl.multiple_of(pl.program_id(1) * block, block), block)
    q_at, k_at, v_at = head_columns(heads_here, pl.program_id(0))
    probs = score_probs(qkv_ref[:, k_at], qkv_ref[at, q_at], seg_column[...], seg_row[...])
    out_ref[...] = dot(qkv_ref[:, v_at], probs.astype(bf16), ((0,), (0,))).T.astype(bf16)


def attend_backward_kernel(
    heads_here, qkv_ref, grad_ref, seg_column, seg_row, out_ref, grad_k, grad_v
):
    block = grad_ref.shape[0]
    turn = pl.program_id(1)
    at = pl.ds(pl.multiple_of(turn * block, block), block)
    q_at, k_at, v_at = head_columns(heads_here, pl.program_id(0))
    queries, keys, grads = qkv_ref[at, q_at], qkv_ref[:, k_at], grad_ref[...]
    probs = score_probs(keys, queries, seg_column[...], seg_row[...])
    grad_probs = dot(qkv_ref[:, v_at], grads, ((1,), (1,)))
    inner = jnp.sum(probs * grad_probs, axis=0, keepdims=True)
    grad_scores = (probs * (grad_probs - inner)).astype(bf16)
    scale = HEAD ** (-0.5)

    @pl.when(turn == 0)
    def _():
        grad_k[...] = jnp.zeros_like(grad_k)
        grad_v[...] = jnp.zeros_like(grad_v)

    grad_v[...] += dot(probs.astype(bf16), grads, ((1,), (0,)))
    grad_k[...] += dot(grad_scores, queries, ((1,), (0,)))
    out_ref[at, q_at] = (dot(keys, grad_scores, ((0,), (0,))).T * scale).astype(bf16)

    @pl.when(turn == pl.num_programs(1) - 1)
    def _():
        out_ref[:, k_at] = (grad_k[...] * scale).astype(bf16)
        out_ref[:, v_at] = grad_v[...].astype(bf16)


def attend(qkv, segment, grad=None):
    span_len, columns = qkv.shape
    heads_here = columns // (3 * HEAD)
    blocks = 3
    block = span_len // blocks
    whole = pl.BlockSpec((span_len, columns), lambda h, i: (0, 0), pipeline_mode=pl.Buffered(1))
    cut = pl.BlockSpec((block, HEAD), lambda h, i: (i, h))
    segments = [
        pl.BlockSpec((span_len, 1), lambda h, i: (0, 0)),
        pl.BlockSpec((1, block), lambda h, i: (0, i)),
    ]
    backward = grad is not None
    return pl.pallas_call(
        lambda *refs: (attend_backward_kernel if backward else attend_forward_kernel)(
            heads_here, *refs
        ),
        out_shape=jax.ShapeDtypeStruct((span_len, columns if backward else columns // 3), bf16),
        grid=(heads_here, blocks),
        in_specs=[whole, *[cut] * backward, *segments],
        out_specs=pl.BlockSpec((span_len, columns), lambda h, i: (0, 0)) if backward else cut,
        scratch_shapes=[pltpu.VMEM((span_len, HEAD), f32)] * (2 * backward),
        compiler_params=pltpu.CompilerParams(
            dimension_semantics=("arbitrary", "arbitrary"), vmem_limit_bytes=60 * 2**20
        ),
        cost_estimate=pl.CostEstimate(
            flops=(40 if backward else 20) * span_len * span_len * HEAD * heads_here,
            bytes_accessed=4 * span_len * columns,
            transcendentals=span_len * span_len * heads_here,
        ),
        name="attend_backward" if backward else "attend_forward",
    )(*[qkv, *[grad] * backward, segment.reshape(span_len, 1), segment.reshape(1, span_len)])


def finish_kernel(in_ref, gate_ref, down_ref):
    ffe = down_ref.shape[1]
    whole = in_ref[0].astype(f32)
    gate_ref[0, :, 0, :] = whole[:, :ffe]
    gate_ref[0, :, 1, :] = whole[:, ffe : 2 * ffe]
    down_ref[0] = whole[:, 2 * ffe :].T


def finish_grads(packed):
    count, rows, columns = packed.shape
    ffe = columns // 3
    return pl.pallas_call(
        finish_kernel,
        out_shape=[
            jax.ShapeDtypeStruct((count, rows, 2, ffe), f32),
            jax.ShapeDtypeStruct((count, ffe, rows), f32),
        ],
        grid=(count,),
        in_specs=[pl.BlockSpec((1, rows, columns), lambda e: (e, 0, 0))],
        out_specs=[
            pl.BlockSpec((1, rows, 2, ffe), lambda e: (e, 0, 0, 0)),
            pl.BlockSpec((1, ffe, rows), lambda e: (e, 0, 0)),
        ],
        compiler_params=pltpu.CompilerParams(vmem_limit_bytes=60 * 2**20),
        name="finish",
    )(packed)


def unpack_kernel(in_ref, out_ref):
    out_ref[...] = in_ref[0].astype(f32)


def unpack_columns(gathered, width, thirds):
    n_seq, rows, _ = gathered.shape
    return pl.pallas_call(
        unpack_kernel,
        out_shape=jax.ShapeDtypeStruct((rows, thirds * n_seq * width), f32),
        grid=(n_seq, thirds),
        in_specs=[pl.BlockSpec((1, rows, width), lambda s, p: (s, 0, p))],
        out_specs=pl.BlockSpec((rows, width), lambda s, p: (0, p * n_seq + s)),
        name="unpack",
    )(gathered)


def after(value, *others):
    if not others:
        return value
    return lax.optimization_barrier((value, *others))[0]


def reversed_bits(index, size):
    count, total = size.bit_length() - 1, 0
    for bit in range(count):
        total = total + (((index >> bit) & 1) << (count - 1 - bit))
    return total


def start_expert(mine, sent, *start, later=()):
    size = lax.axis_size("fsdp")
    mine, sent = after(mine, *start, *later), after(sent, *start)
    pieces = {size // 2: swap(sent, "fsdp", size // 2)}
    bit = size // 4
    while bit > 1:
        pieces[bit] = swap(mine, "fsdp", bit)
        bit //= 2
    return pieces


def finish_expert(pieces, *start):
    size = lax.axis_size("fsdp")
    pieces, brought = dict(pieces), {}
    for j in sorted(range(2, size, 2), key=lambda j: j.bit_count()):
        if j not in pieces:
            low = j & -j
            pieces[j] = brought[j] = swap(after(pieces[j ^ low], *start), "fsdp", low)
    return brought


def both_cores(pieces, *start):
    size = lax.axis_size("fsdp")
    return lax.all_gather(
        jnp.concatenate([after(piece, *start) for piece in pieces]),
        "fsdp",
        axis=0,
        tiled=True,
        axis_index_groups=[[i, i + 1] for i in range(0, size, 2)],
    )


def send_rows(piece, axis, *start):
    sent = after(piece, *start)
    return [piece, *[swap(sent, axis, k) for k in range(1, lax.axis_size(axis))]]


def join_rows(pieces, axis, *others):
    place, rows = lax.axis_index(axis), pieces[0].shape[0]
    whole = jnp.zeros((len(pieces) * rows, *pieces[0].shape[1:]), pieces[0].dtype)
    for k, piece in enumerate(pieces):
        piece = piece if k else after(piece, *others)
        whole = lax.dynamic_update_slice_in_dim(whole, piece, (place ^ k) * rows, 0)
    return whole


def scatter_rows(sums, axis):
    place, rows = lax.axis_index(axis), sums.shape[0] // lax.axis_size(axis)
    parts = [
        lax.dynamic_slice_in_dim(sums, (place ^ k) * rows, rows, 0)
        for k in range(lax.axis_size(axis))
    ]
    return sum((swap(part, axis, k) if k else part).astype(f32) for k, part in enumerate(parts))


def expert_kernel(size, tiles, parts, place_ref, share_ref, *rest):
    arrays = 1 + max(part[0] for part in parts)
    slots, pieces, rest = rest[:4], rest[4 : 4 + arrays], rest[4 + arrays :]
    made_refs, back_refs, rest = rest[:2], rest[2:4], rest[4:]
    send_ref, keep_ref, weights, x_ref, g_ref, act, grad_proj, sems = rest
    step = pl.program_id(0)
    place = place_ref[0]
    rows = weights.shape[0] // size
    ffe = act.shape[1]
    wide = ffe // tiles
    nn, nt, tn = ((1,), (0,)), ((1,), (1,)), ((0,), (0,))

    @pl.when(step == 0)
    def _():
        copies = [
            pltpu.make_async_copy(
                pieces[parts[j][0]].at[parts[j][1] + parts[j][2] * (1 - (place & 1))],
                weights.at[pl.ds(pl.multiple_of((place ^ j) * rows, rows), rows)],
                sems.at[j],
            )
            for j in range(size)
        ]
        count = slots[0].shape[0]
        for k, slot in enumerate(slots):
            copies.append(
                pltpu.make_async_copy(
                    slot,
                    (x_ref, g_ref)[k // 2].at[pl.ds(k % 2 * count, count)],
                    sems.at[size + k],
                )
            )
        for copy in copies:
            copy.start()
        for copy in copies:
            copy.wait()

    @pl.when(step < tiles)
    def _():
        first = pl.multiple_of(step * wide, wide)
        gate = dot(x_ref[...], weights[:, pl.ds(first, wide)], nn)
        up = dot(x_ref[...], weights[:, pl.ds(pl.multiple_of(ffe + first, wide), wide)], nn)
        grad_act = dot(
            g_ref[...], weights[:, pl.ds(pl.multiple_of(2 * ffe + first, wide), wide)], nn
        )
        sigma = 1.0 / (1.0 + jnp.exp(-gate))
        silu = gate * sigma
        act[:, pl.ds(first, wide)] = (silu * up).astype(bf16)
        grad_proj[:, pl.ds(first, wide)] = (
            grad_act * up * (sigma * (1.0 + gate * (1.0 - sigma)))
        ).astype(bf16)
        grad_proj[:, pl.ds(pl.multiple_of(ffe + first, wide), wide)] = (grad_act * silu).astype(
            bf16
        )

    @pl.when(step >= tiles)
    def _():
        turn = step - tiles
        whose = place ^ reversed_bits((turn + size // 2) % size, size)
        at = pl.ds(pl.multiple_of(whose * rows, rows), rows)
        count = act.shape[0] // 2
        made = (share_ref[...] * dot(act[...], weights[at, 2 * ffe :], nt)).astype(bf16)
        back = dot(grad_proj[...], weights[at, : 2 * ffe], nt).astype(bf16)
        for g in range(2):
            made_refs[g][...] = made[g * count : (g + 1) * count]
            back_refs[g][...] = back[g * count : (g + 1) * count]

        def grads(out_ref):
            out_ref[0, :, : 2 * ffe] = dot(x_ref[:, at], grad_proj[...], tn).astype(bf16)
            out_ref[0, :, 2 * ffe :] = dot(g_ref[:, at], act[...], tn).astype(bf16)

        @pl.when(turn < size // 2)
        def _():
            grads(send_ref)

        @pl.when(turn >= size // 2)
        def _():
            grads(keep_ref)


def run_expert(place, share, slots, grad_slots, pieces, parts):
    size, (_, rows, columns) = len(parts), pieces[0].shape
    count = 2 * slots[0].shape[0]
    ffe = columns // 3
    tiles = 4
    half = size // 2

    def whose(step, place):
        turn = jnp.maximum(step - tiles, 0)
        return 0, place[0] ^ reversed_bits((turn + half) % size, size)

    return pl.pallas_call(
        lambda *refs: expert_kernel(size, tiles, parts, *refs),
        out_shape=[
            *[jax.ShapeDtypeStruct((count // 2, D), bf16)] * 4,
            jax.ShapeDtypeStruct((half, rows, columns), bf16),
            jax.ShapeDtypeStruct((half, rows, columns), bf16),
        ],
        grid_spec=pltpu.PrefetchScalarGridSpec(
            num_scalar_prefetch=1,
            grid=(tiles + size,),
            in_specs=[
                pl.BlockSpec((count, 1), lambda step, place: (0, 0)),
                *[pl.BlockSpec(memory_space=pl.ANY)] * (len(pieces) + 4),
            ],
            out_specs=[
                *[pl.BlockSpec((count // 2, rows), whose)] * 4,
                pl.BlockSpec(
                    (1, rows, columns), lambda t, place: (jnp.clip(t - tiles, 0, half - 1), 0, 0)
                ),
                pl.BlockSpec(
                    (1, rows, columns),
                    lambda t, place: (jnp.clip(t - tiles - half, 0, half - 1), 0, 0),
                ),
            ],
            scratch_shapes=[
                pltpu.VMEM((size * rows, columns), bf16),
                pltpu.VMEM((count, D), bf16),
                pltpu.VMEM((count, D), bf16),
                pltpu.VMEM((count, ffe), bf16),
                pltpu.VMEM((count, 2 * ffe), bf16),
                pltpu.SemaphoreType.DMA((size + 4,)),
            ],
        ),
        compiler_params=pltpu.CompilerParams(
            dimension_semantics=("arbitrary",), vmem_limit_bytes=60 * 2**20
        ),
        cost_estimate=pl.CostEstimate(
            flops=18 * count * D * ffe,
            bytes_accessed=8 * count * D + 4 * size * rows * columns,
            transcendentals=count * ffe,
        ),
        name="expert",
    )(place, share, *slots, *grad_slots, *pieces)


class GradChain:
    def __init__(self, send, keep):
        self.bit, self.size = 1, lax.axis_size("fsdp")
        self.terms, self.send = [keep], send

    def arrive(self):
        if self.bit < self.size:
            self.terms.append(swap(self.send, "fsdp", self.bit))
            self.bit *= 2
        return self.terms[-1]

    def add(self, *others):
        many = self.terms[0].shape[0] // 2
        if many:
            if others:
                count = len(self.terms)
                self.terms = list(lax.optimization_barrier((*self.terms, *others))[:count])
            self.send = sum(t[many:].astype(f32) for t in self.terms).astype(bf16)
            self.terms = [t[:many] for t in self.terms]
        return self.send

    def sums(self):
        self.arrive()
        return self.add()

    def ended(self):
        other = self.terms.pop()[0]
        return sum(t[0].astype(f32) for t in self.terms).astype(bf16), other


def body(
    tokens, lengths, routes, gates, gain_attn, gain_moe, w_qkv, w_out, w_gate_up, w_down, cotangent
):
    n_seq, n_fsdp = lax.axis_size("seq"), lax.axis_size("fsdp")
    at_seq, at_fsdp = lax.axis_index("seq"), lax.axis_index("fsdp")
    rows = tokens.shape[1]
    shard = D // n_fsdp
    local_count = w_gate_up.shape[0]
    per_half = local_count // 2
    half = at_fsdp // (n_fsdp // 2)
    heads_here = HEADS // n_seq
    width = heads_here * HEAD
    span_len = rows * n_seq

    packed = jnp.concatenate(
        [w_gate_up.reshape(local_count, shard, 2 * FFE), jnp.swapaxes(w_down, 1, 2)], axis=2
    )
    own_part = lax.dynamic_slice_in_dim(packed, half * per_half, per_half, 0)
    other_part = lax.dynamic_slice_in_dim(packed, (1 - half) * per_half, per_half, 0)
    cot_other = swap(cotangent[0], "fsdp", n_fsdp // 2)
    x_parts = send_rows(tokens[0], "seq")
    cot_own = join_rows(send_rows(cotangent[0], "seq", *x_parts), "seq")

    part = lax.dynamic_slice_in_dim(
        w_qkv.reshape(shard, 3, HEADS, HEAD), at_seq * heads_here, heads_here, 2
    ).reshape(shard, 3 * width)
    gains = jnp.zeros((shard, 128), bf16).at[:, 0].set(gain_attn).at[:, 1].set(gain_moe)
    gathered = lax.all_gather(
        jnp.concatenate([part, gains], axis=1), "fsdp", axis=0, tiled=True
    )
    qkv_own = gathered[:, : 3 * width]
    gain_a = gathered[:, 3 * width].astype(f32)
    gain_m = gathered[:, 3 * width + 1].astype(f32)

    routing = jnp.concatenate([routes[0].astype(f32), gates[0]], axis=1)
    routing = jnp.stack([routing, swap(routing, "fsdp", n_fsdp // 2)])
    routing = jnp.swapaxes(lax.all_gather(routing, "seq", axis=0, tiled=False), 0, 1)
    routing = routing.reshape(2 * n_seq, rows, 2 * TOP)
    capacity = rows * TOP * 4 // (3 * local_count * n_seq) + 2
    capacity = -(-capacity // 8) * 8
    named = at_seq * local_count + half * per_half + lax.iota(jnp.int32, per_half)
    hits = routing[:, :, :TOP, None].astype(jnp.int32) == named
    mask = jnp.any(hits, axis=2)
    weight = jnp.sum(jnp.where(hits, routing[:, :, TOP:, None], 0.0), axis=2)
    below = (lax.iota(jnp.int32, rows)[:, None] > lax.iota(jnp.int32, rows)[None, :]).astype(bf16)
    rank = jnp.einsum("rq,bqe->bre", below, mask.astype(bf16), preferred_element_type=f32)
    rank = jnp.where(mask, rank.astype(jnp.int32), -1)
    picks = jnp.swapaxes(rank, 1, 2)[:, :, None, :] == lax.iota(jnp.int32, capacity)[:, None]
    share = jnp.sum(
        jnp.where(picks, jnp.swapaxes(weight, 1, 2)[:, :, None, :], 0.0), axis=3
    )
    picks = picks.astype(bf16)

    def normed_rows(values, gain):
        inverse = lax.rsqrt(jnp.mean(values * values, axis=1, keepdims=True) + epsilon)
        return (values * inverse * gain).astype(bf16), inverse

    x_all = join_rows(
        x_parts, "seq", own_part, other_part, picks, share, cot_own, cot_other
    )
    out_full = lax.all_gather(after(w_out, x_all), "fsdp", axis=0, tiled=True)
    normed_a, _ = normed_rows(x_all.astype(f32), gain_a)
    qkv = dot(normed_a, qkv_own, ((1,), (0,))).astype(bf16)
    segment = segment_ids(lengths[0], span_len)
    attended = attend(qkv, segment)
    heads_rows = lax.all_to_all(attended, "seq", split_axis=0, concat_axis=1, tiled=True)
    cot_all = [cot_own, join_rows(send_rows(cot_other, "seq", cot_own), "seq")]
    cot_all = [rows_of.reshape(n_seq, rows, D) for rows_of in cot_all]
    begun = [start_expert(own_part[:1], other_part[:1], attended)]
    heads_rows = after(heads_rows, *cot_all, *begun[0].values())
    experts = [finish_expert(begun[0], heads_rows)]
    x_float = tokens[0].astype(f32)
    resid = x_float + dot(heads_rows, out_full, ((1,), (0,)))
    normed_m, inv_m = normed_rows(resid, gain_m)
    moe_own = lax.all_gather(normed_m, "seq", axis=0, tiled=False)
    moe_other = after(swap(normed_m, "fsdp", n_fsdp // 2), moe_own)
    moe_all = [moe_own, lax.all_gather(moe_other, "seq", axis=0, tiled=False), moe_other]

    place = jnp.full((1,), at_fsdp, jnp.int32)
    forward_parts, backward_parts, chains = [], [], []

    def dispatch(i, g, source, weighted):
        at = slice(g * n_seq, (g + 1) * n_seq)
        part = dot(picks[at, i], source, ((2,), (1,)), ((0,), (0,)))
        if weighted:
            part = part * share[at, i, :, None]
        return part.astype(bf16).reshape(-1, D)

    sets = [[i] for i in range(per_half)]

    def begin(k, *start):
        cut = slice(sets[k][0], sets[k][-1] + 1)
        begun.append(start_expert(own_part[cut], other_part[cut], *start))

    begin(1, moe_all[2])
    begin(2, moe_all[1])
    beside = swap(after(own_part, normed_m), "fsdp", 1)
    near, last = [both_cores(list(begun[0].values()))], {}
    for i in range(per_half):
        k = [n for n, members in enumerate(sets) if i in members][0]
        first, later, many = begun[k], experts[k], len(sets[k])
        back = backward_parts[-1] if i else []
        ready = [near[k], *later.values(), *back]
        if k not in last:
            last[k] = swap(
                jnp.concatenate([after(p, *back[:1]) for p in later.values()]), "fsdp", 1
            )
        if i + 1 < per_half:
            ready.extend(begun[i + 1].values())
        cots = [after(cot_all[g], *back) for g in range(2)]
        for chain in chains[max(i - 3, 0) : max(i - 1, 0)]:
            ready.append(chain.arrive())
        slots = [dispatch(i, g, after(moe_all[g], *ready), False) for g in range(2)]
        ready = [chain.add(back[0]) for chain in chains[max(i - 3, 0) : max(i - 1, 0)]]
        slots[1] = after(slots[1], *ready)
        grad_slots = [dispatch(i, g, cots[g], True) for g in range(2)]
        if i + 1 < per_half:
            experts.append(finish_expert(begun[i + 1], slots[1]))
            near.append(both_cores(list(begun[i + 1].values()), slots[1]))
        even = [*first, *later]
        pieces = [own_part, beside, near[k], last[k], *first.values(), *later.values()]
        at = i - sets[k][0]
        parts = {0: (0, i, 0), 1: (1, i, 0)}
        for n, j in enumerate(even):
            parts[j] = (4 + n, at, 0)
            if j in first:
                parts[j + 1] = (2, n * many + at, len(first) * many)
            else:
                parts[j + 1] = (3, (n - len(first)) * many + at, 0)
        parts = [parts[j] for j in range(n_fsdp)]
        *made, send, keep = run_expert(
            place, share[:, i].reshape(-1, 1), slots, grad_slots, pieces, parts
        )
        forward_parts.append([part.reshape(n_seq, capacity, D) for part in made[:2]])
        backward_parts.append([part.reshape(n_seq, capacity, D) for part in made[2:]])
        chains.append(GradChain(send, keep))
        if i + 3 < per_half:
            begin(i + 3, made[2])

    every_pick = picks.reshape(2, n_seq, per_half * capacity, rows)

    def combine(parts, g, *others):
        together = jnp.concatenate([part[g] for part in parts], axis=1)
        if others:
            together = after(together, *others)
        total = dot(every_pick[g], together, ((1,), (1,)), ((0,), (0,)))
        return total.astype(bf16).reshape(span_len, D)

    def scatter(sums, *others):
        return lax.psum_scatter(after(sums, *others), "seq", scatter_dimension=0, tiled=True)

    back_other = combine(backward_parts, 1, chains[-3].arrive())
    back_own = combine(backward_parts, 0, back_other)
    swapped_back = scatter(back_other)
    grad_normed_m = scatter(back_own, swapped_back)
    swapped_back = swap(swapped_back, "fsdp", n_fsdp // 2)
    ready = [chain.arrive() for chain in chains[-2:]]
    ready.extend(chain.add(back_own) for chain in chains[-3:])
    made_other = combine(forward_parts, 1, back_own)
    made_own = combine(forward_parts, 0, made_other, *ready)
    ready = [made_own, *[chain.arrive() for chain in (*chains[:-3], chains[-2])]]
    grad_normed_m = after(grad_normed_m, *ready).astype(f32) + swapped_back.astype(f32)

    scaled_m = grad_normed_m * gain_m
    grad_resid = (
        cotangent[0].astype(f32)
        + inv_m * scaled_m
        - inv_m * inv_m * inv_m * resid * jnp.mean(scaled_m * resid, axis=1, keepdims=True)
    )
    grad_gain_m = jnp.sum(grad_normed_m * resid * inv_m, axis=0)
    grad_attn = grad_resid.astype(bf16)
    grad_heads_rows = dot(grad_attn, out_full, ((1,), (1,))).astype(bf16)
    mixed_other = scatter(made_other, grad_heads_rows)
    mixed_own = scatter(made_own, grad_heads_rows)
    grad_heads = lax.all_to_all(
        grad_heads_rows, "seq", split_axis=1, concat_axis=0, tiled=True
    )
    chains[-2].add(grad_heads_rows)
    out_sum = []
    for k in range(n_seq):
        columns = lax.dynamic_slice_in_dim(grad_attn, (at_seq ^ k) * width, width, 1)
        part = dot(heads_rows, columns, ((0,), (0,))).astype(bf16)
        out_sum.append(part)
    grad_qkv = attend(qkv, segment, grad_heads)
    ready = [chain.arrive() for chain in (chains[-3], chains[-1])]
    grad_qkv = after(grad_qkv, mixed_other, *ready)
    mixed_other = swap(mixed_other, "fsdp", n_fsdp // 2)
    mixed = (resid + mixed_own.astype(f32) + mixed_other.astype(f32)).astype(bf16)

    grad_qkv_w = dot(normed_a, grad_qkv, ((0,), (0,))).astype(bf16)
    reduced_qkv = after(grad_qkv_w, mixed_own)
    reduced_qkv = lax.psum_scatter(reduced_qkv, "fsdp", scatter_dimension=0, tiled=True)
    part_normed_a = dot(after(grad_qkv, grad_qkv_w), qkv_own, ((1,), (1,)))
    part_sent = part_normed_a.astype(bf16)
    ready = [part_sent, chains[-1].add(grad_qkv_w)]
    out_sum = [swap(after(p, grad_qkv_w), "seq", k) if k else p for k, p in enumerate(out_sum)]
    grad_normed_a = scatter_rows(after(part_sent, *out_sum), "seq")
    qkv_sum = after(reduced_qkv, mixed_other, *ready)
    qkv_sum = lax.all_gather(qkv_sum, "seq", axis=0, tiled=False)
    out_sum[0] = after(out_sum[0], qkv_sum, grad_normed_a, *[c.arrive() for c in chains[-2:]])
    out_sum = sum(part.astype(f32) for part in out_sum).astype(bf16)
    gain_column = jnp.zeros((D, 128), bf16).at[:, 0].set(grad_gain_m.astype(bf16))
    out_sum = jnp.concatenate([out_sum, gain_column], axis=1)
    out_sum = lax.psum_scatter(out_sum, "fsdp", scatter_dimension=0, tiled=True)
    out_sum = lax.all_gather(out_sum, "seq", axis=0, tiled=False)
    qkv_sum = unpack_columns(qkv_sum, width, 3)
    gain_m_sum = jnp.sum(out_sum[:, :, width].astype(f32), axis=0)
    out_sum = unpack_columns(out_sum, width, 1)
    gain_a_sum = jnp.sum(w_qkv.astype(f32) * qkv_sum, axis=1) / gain_attn.astype(f32)
    inv_a = lax.rsqrt(jnp.mean(x_float * x_float, axis=1, keepdims=True) + epsilon)
    scaled_a = grad_normed_a * gain_a
    grad_x = (
        grad_resid
        + inv_a * scaled_a
        - inv_a * inv_a * inv_a * x_float * jnp.mean(scaled_a * x_float, axis=1, keepdims=True)
    )

    for chain in chains:
        while chain.bit < n_fsdp:
            chain.sums()
    ended = [chain.ended() for chain in chains]
    own_grads, other_grads = jnp.stack([e[0] for e in ended]), jnp.stack([e[1] for e in ended])
    first = half == 0
    grad_all = jnp.concatenate(
        [jnp.where(first, own_grads, other_grads), jnp.where(first, other_grads, own_grads)]
    )
    grad_gate_up, grad_down = finish_grads(grad_all)
    return (
        mixed[None],
        grad_x.astype(bf16)[None],
        gain_a_sum,
        gain_m_sum,
        qkv_sum,
        out_sum,
        grad_gate_up,
        grad_down,
    )


def solution(mesh):
    placed = (
        P("fsdp", "seq", None),
        P("fsdp", None),
        P("fsdp", "seq", None),
        P("fsdp", "seq", None),
        P("fsdp"),
        P("fsdp"),
        P("fsdp", None),
        P("fsdp", None),
        P("seq", "fsdp", None, None),
        P("seq", None, "fsdp"),
        P("fsdp", "seq", None),
    )
    return jax.shard_map(
        body,
        mesh=mesh,
        in_specs=placed,
        out_specs=(
            P("fsdp", "seq", None),
            P("fsdp", "seq", None),
            P("fsdp"),
            P("fsdp"),
            P("fsdp", None),
            P("fsdp", None),
            P("seq", "fsdp", None, None),
            P("seq", None, "fsdp"),
        ),
        check_vma=False,
    )
```

```python
import jax
import jax.numpy as jnp
from jax import lax
from jax.experimental import pallas as pl
from jax.experimental.pallas import tpu as pltpu
from jax.sharding import PartitionSpec as P

D = 2048
HEADS = 16
HEAD = 128
FFE = 1024
TOP = 8

epsilon = 1e-06
f32 = jnp.float32
bf16 = jnp.bfloat16


def swap(value, axis, bit):
    size = lax.axis_size(axis)
    return lax.ppermute(value, axis, [(i, i ^ bit) for i in range(size)])


def dot(a, b, contract, batch=((), ())):
    return lax.dot_general(a, b, (contract, batch), preferred_element_type=f32)


def segment_ids(length_row, span_len):
    ends = jnp.cumsum(length_row)
    places = lax.iota(jnp.int32, span_len)
    return jnp.sum((places[:, None] >= ends[None, :]).astype(jnp.int32), axis=1)


def score_probs(keys, queries, seg_column, seg_row):
    raw = dot(keys, queries, ((1,), (1,)))
    raw = jnp.where(seg_column == seg_row, raw, -1e30)
    top = jnp.max(raw, axis=0, keepdims=True)
    part = jnp.exp((raw - top) * HEAD ** (-0.5))
    return part * (1.0 / jnp.sum(part, axis=0, keepdims=True))


def head_columns(heads_here, head):
    return [
        pl.ds(pl.multiple_of((third * heads_here + head) * HEAD, HEAD), HEAD) for third in range(3)
    ]


def attend_forward_kernel(heads_here, qkv_ref, seg_column, seg_row, out_ref):
    block = out_ref.shape[0]
    at = pl.ds(pl.multiple_of(pl.program_id(1) * block, block), block)
    q_at, k_at, v_at = head_columns(heads_here, pl.program_id(0))
    probs = score_probs(qkv_ref[:, k_at], qkv_ref[at, q_at], seg_column[...], seg_row[...])
    out_ref[...] = dot(qkv_ref[:, v_at], probs.astype(bf16), ((0,), (0,))).T.astype(bf16)


def attend_backward_kernel(
    heads_here, qkv_ref, grad_ref, seg_column, seg_row, out_ref, grad_k, grad_v
):
    block = grad_ref.shape[0]
    turn = pl.program_id(1)
    at = pl.ds(pl.multiple_of(turn * block, block), block)
    q_at, k_at, v_at = head_columns(heads_here, pl.program_id(0))
    queries, keys, grads = qkv_ref[at, q_at], qkv_ref[:, k_at], grad_ref[...]
    probs = score_probs(keys, queries, seg_column[...], seg_row[...])
    grad_probs = dot(qkv_ref[:, v_at], grads, ((1,), (1,)))
    inner = jnp.sum(probs * grad_probs, axis=0, keepdims=True)
    grad_scores = (probs * (grad_probs - inner)).astype(bf16)
    scale = HEAD ** (-0.5)

    @pl.when(turn == 0)
    def _():
        grad_k[...] = jnp.zeros_like(grad_k)
        grad_v[...] = jnp.zeros_like(grad_v)

    grad_v[...] += dot(probs.astype(bf16), grads, ((1,), (0,)))
    grad_k[...] += dot(grad_scores, queries, ((1,), (0,)))
    out_ref[at, q_at] = (dot(keys, grad_scores, ((0,), (0,))).T * scale).astype(bf16)

    @pl.when(turn == pl.num_programs(1) - 1)
    def _():
        out_ref[:, k_at] = (grad_k[...] * scale).astype(bf16)
        out_ref[:, v_at] = grad_v[...].astype(bf16)


def attend(qkv, segment, grad=None):
    span_len, columns = qkv.shape
    heads_here = columns // (3 * HEAD)
    blocks = 3
    block = span_len // blocks
    whole = pl.BlockSpec((span_len, columns), lambda h, i: (0, 0), pipeline_mode=pl.Buffered(1))
    cut = pl.BlockSpec((block, HEAD), lambda h, i: (i, h))
    segments = [
        pl.BlockSpec((span_len, 1), lambda h, i: (0, 0)),
        pl.BlockSpec((1, block), lambda h, i: (0, i)),
    ]
    backward = grad is not None
    return pl.pallas_call(
        lambda *refs: (attend_backward_kernel if backward else attend_forward_kernel)(
            heads_here, *refs
        ),
        out_shape=jax.ShapeDtypeStruct((span_len, columns if backward else columns // 3), bf16),
        grid=(heads_here, blocks),
        in_specs=[whole, *[cut] * backward, *segments],
        out_specs=pl.BlockSpec((span_len, columns), lambda h, i: (0, 0)) if backward else cut,
        scratch_shapes=[pltpu.VMEM((span_len, HEAD), f32)] * (2 * backward),
        compiler_params=pltpu.CompilerParams(
            dimension_semantics=("arbitrary", "arbitrary"), vmem_limit_bytes=60 * 2**20
        ),
        cost_estimate=pl.CostEstimate(
            flops=(40 if backward else 20) * span_len * span_len * HEAD * heads_here,
            bytes_accessed=4 * span_len * columns,
            transcendentals=span_len * span_len * heads_here,
        ),
        name="attend_backward" if backward else "attend_forward",
    )(*[qkv, *[grad] * backward, segment.reshape(span_len, 1), segment.reshape(1, span_len)])


def finish_kernel(in_ref, gate_ref, down_ref):
    ffe = down_ref.shape[1]
    whole = in_ref[0].astype(f32)
    gate_ref[0, :, 0, :] = whole[:, :ffe]
    gate_ref[0, :, 1, :] = whole[:, ffe : 2 * ffe]
    down_ref[0] = whole[:, 2 * ffe :].T


def finish_grads(packed):
    count, rows, columns = packed.shape
    ffe = columns // 3
    return pl.pallas_call(
        finish_kernel,
        out_shape=[
            jax.ShapeDtypeStruct((count, rows, 2, ffe), f32),
            jax.ShapeDtypeStruct((count, ffe, rows), f32),
        ],
        grid=(count,),
        in_specs=[pl.BlockSpec((1, rows, columns), lambda e: (e, 0, 0))],
        out_specs=[
            pl.BlockSpec((1, rows, 2, ffe), lambda e: (e, 0, 0, 0)),
            pl.BlockSpec((1, ffe, rows), lambda e: (e, 0, 0)),
        ],
        compiler_params=pltpu.CompilerParams(vmem_limit_bytes=60 * 2**20),
        name="finish",
    )(packed)


def unpack_kernel(in_ref, out_ref):
    out_ref[...] = in_ref[0].astype(f32)


def unpack_columns(gathered, width, thirds):
    n_seq, rows, _ = gathered.shape
    return pl.pallas_call(
        unpack_kernel,
        out_shape=jax.ShapeDtypeStruct((rows, thirds * n_seq * width), f32),
        grid=(n_seq, thirds),
        in_specs=[pl.BlockSpec((1, rows, width), lambda s, p: (s, 0, p))],
        out_specs=pl.BlockSpec((rows, width), lambda s, p: (0, p * n_seq + s)),
        name="unpack",
    )(gathered)


def after(value, *others):
    if not others:
        return value
    return lax.optimization_barrier((value, *others))[0]


def reversed_bits(index, size):
    count, total = size.bit_length() - 1, 0
    for bit in range(count):
        total = total + (((index >> bit) & 1) << (count - 1 - bit))
    return total


def start_expert(mine, sent, *start, later=()):
    size = lax.axis_size("fsdp")
    mine, sent = after(mine, *start, *later), after(sent, *start)
    pieces = {size // 2: swap(sent, "fsdp", size // 2)}
    bit = size // 4
    while bit > 1:
        pieces[bit] = swap(mine, "fsdp", bit)
        bit //= 2
    return pieces


def finish_expert(pieces, *start):
    size = lax.axis_size("fsdp")
    pieces, brought = dict(pieces), {}
    for j in sorted(range(2, size, 2), key=lambda j: j.bit_count()):
        if j not in pieces:
            low = j & -j
            pieces[j] = brought[j] = swap(after(pieces[j ^ low], *start), "fsdp", low)
    return brought


def both_cores(pieces, *start):
    size = lax.axis_size("fsdp")
    return lax.all_gather(
        jnp.concatenate([after(piece, *start) for piece in pieces]),
        "fsdp",
        axis=0,
        tiled=True,
        axis_index_groups=[[i, i + 1] for i in range(0, size, 2)],
    )


def send_rows(piece, axis, *start):
    sent = after(piece, *start)
    return [piece, *[swap(sent, axis, k) for k in range(1, lax.axis_size(axis))]]


def join_rows(pieces, axis, *others):
    place, rows = lax.axis_index(axis), pieces[0].shape[0]
    whole = jnp.zeros((len(pieces) * rows, *pieces[0].shape[1:]), pieces[0].dtype)
    for k, piece in enumerate(pieces):
        piece = piece if k else after(piece, *others)
        whole = lax.dynamic_update_slice_in_dim(whole, piece, (place ^ k) * rows, 0)
    return whole


def scatter_rows(sums, axis):
    place, rows = lax.axis_index(axis), sums.shape[0] // lax.axis_size(axis)
    parts = [
        lax.dynamic_slice_in_dim(sums, (place ^ k) * rows, rows, 0)
        for k in range(lax.axis_size(axis))
    ]
    return sum((swap(part, axis, k) if k else part).astype(f32) for k, part in enumerate(parts))


def expert_kernel(size, tiles, parts, place_ref, share_ref, *rest):
    arrays = 1 + max(part[0] for part in parts)
    slots, pieces, rest = rest[:4], rest[4 : 4 + arrays], rest[4 + arrays :]
    made_refs, back_refs, rest = rest[:2], rest[2:4], rest[4:]
    send_ref, keep_ref, weights, x_ref, g_ref, act, grad_proj, sems = rest
    step = pl.program_id(0)
    place = place_ref[0]
    rows = weights.shape[0] // size
    ffe = act.shape[1]
    wide = ffe // tiles
    nn, nt, tn = ((1,), (0,)), ((1,), (1,)), ((0,), (0,))

    @pl.when(step == 0)
    def _():
        copies = [
            pltpu.make_async_copy(
                pieces[parts[j][0]].at[parts[j][1] + parts[j][2] * (1 - (place & 1))],
                weights.at[pl.ds(pl.multiple_of((place ^ j) * rows, rows), rows)],
                sems.at[j],
            )
            for j in range(size)
        ]
        count = slots[0].shape[0]
        for k, slot in enumerate(slots):
            copies.append(
                pltpu.make_async_copy(
                    slot,
                    (x_ref, g_ref)[k // 2].at[pl.ds(k % 2 * count, count)],
                    sems.at[size + k],
                )
            )
        for copy in copies:
            copy.start()
        for copy in copies:
            copy.wait()

    @pl.when(step < tiles)
    def _():
        first = pl.multiple_of(step * wide, wide)
        gate = dot(x_ref[...], weights[:, pl.ds(first, wide)], nn)
        up = dot(x_ref[...], weights[:, pl.ds(pl.multiple_of(ffe + first, wide), wide)], nn)
        grad_act = dot(
            g_ref[...], weights[:, pl.ds(pl.multiple_of(2 * ffe + first, wide), wide)], nn
        )
        sigma = 1.0 / (1.0 + jnp.exp(-gate))
        silu = gate * sigma
        act[:, pl.ds(first, wide)] = (silu * up).astype(bf16)
        grad_proj[:, pl.ds(first, wide)] = (
            grad_act * up * (sigma * (1.0 + gate * (1.0 - sigma)))
        ).astype(bf16)
        grad_proj[:, pl.ds(pl.multiple_of(ffe + first, wide), wide)] = (grad_act * silu).astype(
            bf16
        )

    @pl.when(step >= tiles)
    def _():
        turn = step - tiles
        whose = place ^ reversed_bits((turn + size // 2) % size, size)
        at = pl.ds(pl.multiple_of(whose * rows, rows), rows)
        count = act.shape[0] // 2
        made = (share_ref[...] * dot(act[...], weights[at, 2 * ffe :], nt)).astype(bf16)
        back = dot(grad_proj[...], weights[at, : 2 * ffe], nt).astype(bf16)
        for g in range(2):
            made_refs[g][...] = made[g * count : (g + 1) * count]
            back_refs[g][...] = back[g * count : (g + 1) * count]

        def grads(out_ref):
            out_ref[0, :, : 2 * ffe] = dot(x_ref[:, at], grad_proj[...], tn).astype(bf16)
            out_ref[0, :, 2 * ffe :] = dot(g_ref[:, at], act[...], tn).astype(bf16)

        @pl.when(turn < size // 2)
        def _():
            grads(send_ref)

        @pl.when(turn >= size // 2)
        def _():
            grads(keep_ref)


def run_expert(place, share, slots, grad_slots, pieces, parts):
    size, (_, rows, columns) = len(parts), pieces[0].shape
    count = 2 * slots[0].shape[0]
    ffe = columns // 3
    tiles = 4
    half = size // 2

    def whose(step, place):
        turn = jnp.maximum(step - tiles, 0)
        return 0, place[0] ^ reversed_bits((turn + half) % size, size)

    return pl.pallas_call(
        lambda *refs: expert_kernel(size, tiles, parts, *refs),
        out_shape=[
            *[jax.ShapeDtypeStruct((count // 2, D), bf16)] * 4,
            jax.ShapeDtypeStruct((half, rows, columns), bf16),
            jax.ShapeDtypeStruct((half, rows, columns), bf16),
        ],
        grid_spec=pltpu.PrefetchScalarGridSpec(
            num_scalar_prefetch=1,
            grid=(tiles + size,),
            in_specs=[
                pl.BlockSpec((count, 1), lambda step, place: (0, 0)),
                *[pl.BlockSpec(memory_space=pl.ANY)] * (len(pieces) + 4),
            ],
            out_specs=[
                *[pl.BlockSpec((count // 2, rows), whose)] * 4,
                pl.BlockSpec(
                    (1, rows, columns), lambda t, place: (jnp.clip(t - tiles, 0, half - 1), 0, 0)
                ),
                pl.BlockSpec(
                    (1, rows, columns),
                    lambda t, place: (jnp.clip(t - tiles - half, 0, half - 1), 0, 0),
                ),
            ],
            scratch_shapes=[
                pltpu.VMEM((size * rows, columns), bf16),
                pltpu.VMEM((count, D), bf16),
                pltpu.VMEM((count, D), bf16),
                pltpu.VMEM((count, ffe), bf16),
                pltpu.VMEM((count, 2 * ffe), bf16),
                pltpu.SemaphoreType.DMA((size + 4,)),
            ],
        ),
        compiler_params=pltpu.CompilerParams(
            dimension_semantics=("arbitrary",), vmem_limit_bytes=60 * 2**20
        ),
        cost_estimate=pl.CostEstimate(
            flops=18 * count * D * ffe,
            bytes_accessed=8 * count * D + 4 * size * rows * columns,
            transcendentals=count * ffe,
        ),
        name="expert",
    )(place, share, *slots, *grad_slots, *pieces)


class GradChain:
    def __init__(self, send, keep):
        self.bit, self.size = 1, lax.axis_size("fsdp")
        self.terms, self.send = [keep], send

    def arrive(self):
        if self.bit < self.size:
            self.terms.append(swap(self.send, "fsdp", self.bit))
            self.bit *= 2
        return self.terms[-1]

    def add(self, *others):
        many = self.terms[0].shape[0] // 2
        if many:
            if others:
                count = len(self.terms)
                self.terms = list(lax.optimization_barrier((*self.terms, *others))[:count])
            self.send = sum(t[many:].astype(f32) for t in self.terms).astype(bf16)
            self.terms = [t[:many] for t in self.terms]
        return self.send

    def sums(self):
        self.arrive()
        return self.add()

    def ended(self):
        other = self.terms.pop()[0]
        return sum(t[0].astype(f32) for t in self.terms).astype(bf16), other


def body(
    tokens, lengths, routes, gates, gain_attn, gain_moe, w_qkv, w_out, w_gate_up, w_down, cotangent
):
    n_seq, n_fsdp = lax.axis_size("seq"), lax.axis_size("fsdp")
    at_seq, at_fsdp = lax.axis_index("seq"), lax.axis_index("fsdp")
    rows = tokens.shape[1]
    shard = D // n_fsdp
    local_count = w_gate_up.shape[0]
    per_half = local_count // 2
    half = at_fsdp // (n_fsdp // 2)
    heads_here = HEADS // n_seq
    width = heads_here * HEAD
    span_len = rows * n_seq

    packed = jnp.concatenate(
        [w_gate_up.reshape(local_count, shard, 2 * FFE), jnp.swapaxes(w_down, 1, 2)], axis=2
    )
    own_part = lax.dynamic_slice_in_dim(packed, half * per_half, per_half, 0)
    other_part = lax.dynamic_slice_in_dim(packed, (1 - half) * per_half, per_half, 0)
    cot_other = swap(cotangent[0], "fsdp", n_fsdp // 2)
    x_parts = send_rows(tokens[0], "seq")
    cot_own = join_rows(send_rows(cotangent[0], "seq", *x_parts), "seq")

    part = lax.dynamic_slice_in_dim(
        w_qkv.reshape(shard, 3, HEADS, HEAD), at_seq * heads_here, heads_here, 2
    ).reshape(shard, 3 * width)
    gains = jnp.zeros((shard, 128), bf16).at[:, 0].set(gain_attn).at[:, 1].set(gain_moe)
    gathered = lax.all_gather(
        jnp.concatenate([part, gains], axis=1), "fsdp", axis=0, tiled=True
    )
    qkv_own = gathered[:, : 3 * width]
    gain_a = gathered[:, 3 * width].astype(f32)
    gain_m = gathered[:, 3 * width + 1].astype(f32)

    routing = jnp.concatenate([routes[0].astype(f32), gates[0]], axis=1)
    routing = jnp.stack([routing, swap(routing, "fsdp", n_fsdp // 2)])
    routing = jnp.swapaxes(lax.all_gather(routing, "seq", axis=0, tiled=False), 0, 1)
    routing = routing.reshape(2 * n_seq, rows, 2 * TOP)
    capacity = rows * TOP * 4 // (3 * local_count * n_seq) + 2
    capacity = -(-capacity // 8) * 8
    named = at_seq * local_count + half * per_half + lax.iota(jnp.int32, per_half)
    hits = routing[:, :, :TOP, None].astype(jnp.int32) == named
    mask = jnp.any(hits, axis=2)
    weight = jnp.sum(jnp.where(hits, routing[:, :, TOP:, None], 0.0), axis=2)
    below = (lax.iota(jnp.int32, rows)[:, None] > lax.iota(jnp.int32, rows)[None, :]).astype(bf16)
    rank = jnp.einsum("rq,bqe->bre", below, mask.astype(bf16), preferred_element_type=f32)
    rank = jnp.where(mask, rank.astype(jnp.int32), -1)
    picks = jnp.swapaxes(rank, 1, 2)[:, :, None, :] == lax.iota(jnp.int32, capacity)[:, None]
    share = jnp.sum(
        jnp.where(picks, jnp.swapaxes(weight, 1, 2)[:, :, None, :], 0.0), axis=3
    )
    picks = picks.astype(bf16)

    def normed_rows(values, gain):
        inverse = lax.rsqrt(jnp.mean(values * values, axis=1, keepdims=True) + epsilon)
        return (values * inverse * gain).astype(bf16), inverse

    x_all = join_rows(
        x_parts, "seq", own_part, other_part, picks, share, cot_own, cot_other
    )
    out_full = lax.all_gather(after(w_out, x_all), "fsdp", axis=0, tiled=True)
    normed_a, _ = normed_rows(x_all.astype(f32), gain_a)
    qkv = dot(normed_a, qkv_own, ((1,), (0,))).astype(bf16)
    segment = segment_ids(lengths[0], span_len)
    attended = attend(qkv, segment)
    heads_rows = lax.all_to_all(attended, "seq", split_axis=0, concat_axis=1, tiled=True)
    cot_all = [cot_own, join_rows(send_rows(cot_other, "seq", cot_own), "seq")]
    cot_all = [rows_of.reshape(n_seq, rows, D) for rows_of in cot_all]
    begun = [start_expert(own_part[:1], other_part[:1], attended)]
    heads_rows = after(heads_rows, *cot_all, *begun[0].values())
    experts = [finish_expert(begun[0], heads_rows)]
    x_float = tokens[0].astype(f32)
    resid = x_float + dot(heads_rows, out_full, ((1,), (0,)))
    normed_m, inv_m = normed_rows(resid, gain_m)
    moe_own = lax.all_gather(normed_m, "seq", axis=0, tiled=False)
    moe_other = after(swap(normed_m, "fsdp", n_fsdp // 2), moe_own)
    moe_all = [moe_own, lax.all_gather(moe_other, "seq", axis=0, tiled=False), moe_other]

    place = jnp.full((1,), at_fsdp, jnp.int32)
    forward_parts, backward_parts, chains = [], [], []

    def dispatch(i, g, source, weighted):
        at = slice(g * n_seq, (g + 1) * n_seq)
        part = dot(picks[at, i], source, ((2,), (1,)), ((0,), (0,)))
        if weighted:
            part = part * share[at, i, :, None]
        return part.astype(bf16).reshape(-1, D)

    sets = [[i] for i in range(per_half)]

    def begin(k, *start):
        cut = slice(sets[k][0], sets[k][-1] + 1)
        begun.append(start_expert(own_part[cut], other_part[cut], *start))

    begin(1, moe_all[2])
    begin(2, moe_all[1])
    beside = swap(after(own_part, normed_m), "fsdp", 1)
    near, last = [both_cores(list(begun[0].values()))], {}
    for i in range(per_half):
        k = [n for n, members in enumerate(sets) if i in members][0]
        first, later, many = begun[k], experts[k], len(sets[k])
        back = backward_parts[-1] if i else []
        ready = [near[k], *later.values(), *back]
        if k not in last:
            last[k] = swap(
                jnp.concatenate([after(p, *back[:1]) for p in later.values()]), "fsdp", 1
            )
        if i + 1 < per_half:
            ready.extend(begun[i + 1].values())
        cots = [after(cot_all[g], *back) for g in range(2)]
        for chain in chains[max(i - 3, 0) : max(i - 1, 0)]:
            ready.append(chain.arrive())
        if i == 0:
            ready = [dispatch(i, g, cots[g], True) for g in range(2)]
        slots = [dispatch(i, g, after(moe_all[g], *ready), False) for g in range(2)]
        ready = [chain.add(back[0]) for chain in chains[max(i - 3, 0) : max(i - 1, 0)]]
        slots[1] = after(slots[1], *ready)
        grad_slots = [dispatch(i, g, cots[g], True) for g in range(2)]
        if i + 1 < per_half:
            experts.append(finish_expert(begun[i + 1], slots[1]))
            near.append(both_cores(list(begun[i + 1].values()), slots[1]))
        even = [*first, *later]
        pieces = [own_part, beside, near[k], last[k], *first.values(), *later.values()]
        at = i - sets[k][0]
        parts = {0: (0, i, 0), 1: (1, i, 0)}
        for n, j in enumerate(even):
            parts[j] = (4 + n, at, 0)
            if j in first:
                parts[j + 1] = (2, n * many + at, len(first) * many)
            else:
                parts[j + 1] = (3, (n - len(first)) * many + at, 0)
        parts = [parts[j] for j in range(n_fsdp)]
        *made, send, keep = run_expert(
            place, share[:, i].reshape(-1, 1), slots, grad_slots, pieces, parts
        )
        forward_parts.append([part.reshape(n_seq, capacity, D) for part in made[:2]])
        backward_parts.append([part.reshape(n_seq, capacity, D) for part in made[2:]])
        chains.append(GradChain(send, keep))
        if i + 3 < per_half:
            begin(i + 3, made[2])

    every_pick = picks.reshape(2, n_seq, per_half * capacity, rows)

    def combine(parts, g, *others):
        together = jnp.concatenate([part[g] for part in parts], axis=1)
        if others:
            together = after(together, *others)
        total = dot(every_pick[g], together, ((1,), (1,)), ((0,), (0,)))
        return total.astype(bf16).reshape(span_len, D)

    def scatter(sums, *others):
        return lax.psum_scatter(after(sums, *others), "seq", scatter_dimension=0, tiled=True)

    back_other = combine(backward_parts, 1, *[chain.arrive() for chain in chains[:-2]])
    back_own = combine(backward_parts, 0, back_other)
    swapped_back = scatter(back_other)
    ready = [chain.arrive() for chain in chains[-2:]]
    ready.extend(chain.add(back_own) for chain in chains[-3:])
    ready.append(chains[-3].arrive())
    grad_normed_m = scatter(back_own, swapped_back, *ready)
    swapped_back = swap(swapped_back, "fsdp", n_fsdp // 2)
    ready = [swapped_back, chains[-2].arrive()]
    made_other = combine(forward_parts, 1, back_own)
    made_own = combine(forward_parts, 0, made_other, *ready)
    mixed_other, mixed_own = scatter(made_other, grad_normed_m), scatter(made_own, grad_normed_m)
    ready = [made_own]
    grad_normed_m = after(grad_normed_m, *ready).astype(f32) + swapped_back.astype(f32)

    scaled_m = grad_normed_m * gain_m
    grad_resid = (
        cotangent[0].astype(f32)
        + inv_m * scaled_m
        - inv_m * inv_m * inv_m * resid * jnp.mean(scaled_m * resid, axis=1, keepdims=True)
    )
    grad_gain_m = jnp.sum(grad_normed_m * resid * inv_m, axis=0)
    grad_attn = grad_resid.astype(bf16)
    grad_heads_rows = dot(grad_attn, out_full, ((1,), (1,))).astype(bf16)
    grad_heads = lax.all_to_all(
        grad_heads_rows, "seq", split_axis=1, concat_axis=0, tiled=True
    )
    chains[-2].add(grad_heads_rows)
    out_sum = []
    for k in range(n_seq):
        columns = lax.dynamic_slice_in_dim(grad_attn, (at_seq ^ k) * width, width, 1)
        part = dot(heads_rows, columns, ((0,), (0,))).astype(bf16)
        out_sum.append(part)
    grad_qkv = attend(qkv, segment, grad_heads)
    ready = [chain.arrive() for chain in chains[-2:]]
    grad_qkv = after(grad_qkv, mixed_own, *ready)
    mixed_other = swap(after(mixed_other, grad_qkv), "fsdp", n_fsdp // 2)
    mixed = (resid + mixed_own.astype(f32) + mixed_other.astype(f32)).astype(bf16)

    grad_qkv_w = dot(normed_a, grad_qkv, ((0,), (0,))).astype(bf16)
    reduced_qkv = lax.psum_scatter(grad_qkv_w, "fsdp", scatter_dimension=0, tiled=True)
    part_normed_a = dot(after(grad_qkv, grad_qkv_w), qkv_own, ((1,), (1,)))
    part_sent = part_normed_a.astype(bf16)
    ready = [part_sent, chains[-1].add(grad_qkv_w)]
    out_sum = [swap(after(p, grad_qkv_w), "seq", k) if k else p for k, p in enumerate(out_sum)]
    grad_normed_a = scatter_rows(after(part_sent, *out_sum), "seq")
    qkv_sum = after(reduced_qkv, mixed_other, *ready, *out_sum[1:])
    qkv_sum = lax.all_gather(qkv_sum, "seq", axis=0, tiled=False)
    out_sum[0] = after(out_sum[0], qkv_sum, grad_normed_a, chains[-1].arrive())
    out_sum = sum(part.astype(f32) for part in out_sum).astype(bf16)
    gain_column = jnp.zeros((D, 128), bf16).at[:, 0].set(grad_gain_m.astype(bf16))
    out_sum = jnp.concatenate([out_sum, gain_column], axis=1)
    out_sum = lax.psum_scatter(out_sum, "fsdp", scatter_dimension=0, tiled=True)
    out_sum = lax.all_gather(out_sum, "seq", axis=0, tiled=False)
    qkv_sum = unpack_columns(qkv_sum, width, 3)
    gain_m_sum = jnp.sum(out_sum[:, :, width].astype(f32), axis=0)
    out_sum = unpack_columns(out_sum, width, 1)
    gain_a_sum = jnp.sum(w_qkv.astype(f32) * qkv_sum, axis=1) / gain_attn.astype(f32)
    inv_a = lax.rsqrt(jnp.mean(x_float * x_float, axis=1, keepdims=True) + epsilon)
    scaled_a = grad_normed_a * gain_a
    grad_x = (
        grad_resid
        + inv_a * scaled_a
        - inv_a * inv_a * inv_a * x_float * jnp.mean(scaled_a * x_float, axis=1, keepdims=True)
    )

    for chain in chains:
        while chain.bit < n_fsdp:
            chain.sums()
    ended = [chain.ended() for chain in chains]
    own_grads, other_grads = jnp.stack([e[0] for e in ended]), jnp.stack([e[1] for e in ended])
    first = half == 0
    grad_all = jnp.concatenate(
        [jnp.where(first, own_grads, other_grads), jnp.where(first, other_grads, own_grads)]
    )
    grad_gate_up, grad_down = finish_grads(grad_all)
    return (
        mixed[None],
        grad_x.astype(bf16)[None],
        gain_a_sum,
        gain_m_sum,
        qkv_sum,
        out_sum,
        grad_gate_up,
        grad_down,
    )


def solution(mesh):
    placed = (
        P("fsdp", "seq", None),
        P("fsdp", None),
        P("fsdp", "seq", None),
        P("fsdp", "seq", None),
        P("fsdp"),
        P("fsdp"),
        P("fsdp", None),
        P("fsdp", None),
        P("seq", "fsdp", None, None),
        P("seq", None, "fsdp"),
        P("fsdp", "seq", None),
    )
    return jax.shard_map(
        body,
        mesh=mesh,
        in_specs=placed,
        out_specs=(
            P("fsdp", "seq", None),
            P("fsdp", "seq", None),
            P("fsdp"),
            P("fsdp"),
            P("fsdp", None),
            P("fsdp", None),
            P("seq", "fsdp", None, None),
            P("seq", None, "fsdp"),
        ),
        check_vma=False,
    )
```

```python
import jax
import jax.numpy as jnp
from jax import lax
from jax.experimental import pallas as pl
from jax.experimental.pallas import tpu as pltpu
from jax.sharding import PartitionSpec as P

D = 2048
HEADS = 16
HEAD = 128
FFE = 1024
TOP = 8

epsilon = 1e-06
f32 = jnp.float32
bf16 = jnp.bfloat16


def swap(value, axis, bit):
    size = lax.axis_size(axis)
    return lax.ppermute(value, axis, [(i, i ^ bit) for i in range(size)])


def dot(a, b, contract, batch=((), ())):
    return lax.dot_general(a, b, (contract, batch), preferred_element_type=f32)


def segment_ids(length_row, span_len):
    ends = jnp.cumsum(length_row)
    places = lax.iota(jnp.int32, span_len)
    return jnp.sum((places[:, None] >= ends[None, :]).astype(jnp.int32), axis=1)


def score_probs(keys, queries, seg_column, seg_row):
    raw = dot(keys, queries, ((1,), (1,)))
    raw = jnp.where(seg_column == seg_row, raw, -1e30)
    top = jnp.max(raw, axis=0, keepdims=True)
    part = jnp.exp((raw - top) * HEAD ** (-0.5))
    return part * (1.0 / jnp.sum(part, axis=0, keepdims=True))


def head_columns(heads_here, head):
    return [
        pl.ds(pl.multiple_of((third * heads_here + head) * HEAD, HEAD), HEAD) for third in range(3)
    ]


def attend_forward_kernel(heads_here, qkv_ref, seg_column, seg_row, out_ref):
    block = out_ref.shape[0]
    at = pl.ds(pl.multiple_of(pl.program_id(1) * block, block), block)
    q_at, k_at, v_at = head_columns(heads_here, pl.program_id(0))
    probs = score_probs(qkv_ref[:, k_at], qkv_ref[at, q_at], seg_column[...], seg_row[...])
    out_ref[...] = dot(qkv_ref[:, v_at], probs.astype(bf16), ((0,), (0,))).T.astype(bf16)


def attend_backward_kernel(
    heads_here, qkv_ref, grad_ref, seg_column, seg_row, out_ref, grad_k, grad_v
):
    block = grad_ref.shape[0]
    turn = pl.program_id(1)
    at = pl.ds(pl.multiple_of(turn * block, block), block)
    q_at, k_at, v_at = head_columns(heads_here, pl.program_id(0))
    queries, keys, grads = qkv_ref[at, q_at], qkv_ref[:, k_at], grad_ref[...]
    probs = score_probs(keys, queries, seg_column[...], seg_row[...])
    grad_probs = dot(qkv_ref[:, v_at], grads, ((1,), (1,)))
    inner = jnp.sum(probs * grad_probs, axis=0, keepdims=True)
    grad_scores = (probs * (grad_probs - inner)).astype(bf16)
    scale = HEAD ** (-0.5)

    @pl.when(turn == 0)
    def _():
        grad_k[...] = jnp.zeros_like(grad_k)
        grad_v[...] = jnp.zeros_like(grad_v)

    grad_v[...] += dot(probs.astype(bf16), grads, ((1,), (0,)))
    grad_k[...] += dot(grad_scores, queries, ((1,), (0,)))
    out_ref[at, q_at] = (dot(keys, grad_scores, ((0,), (0,))).T * scale).astype(bf16)

    @pl.when(turn == pl.num_programs(1) - 1)
    def _():
        out_ref[:, k_at] = (grad_k[...] * scale).astype(bf16)
        out_ref[:, v_at] = grad_v[...].astype(bf16)


def attend(qkv, segment, grad=None):
    span_len, columns = qkv.shape
    heads_here = columns // (3 * HEAD)
    blocks = 3
    block = span_len // blocks
    whole = pl.BlockSpec((span_len, columns), lambda h, i: (0, 0), pipeline_mode=pl.Buffered(1))
    cut = pl.BlockSpec((block, HEAD), lambda h, i: (i, h))
    segments = [
        pl.BlockSpec((span_len, 1), lambda h, i: (0, 0)),
        pl.BlockSpec((1, block), lambda h, i: (0, i)),
    ]
    backward = grad is not None
    return pl.pallas_call(
        lambda *refs: (attend_backward_kernel if backward else attend_forward_kernel)(
            heads_here, *refs
        ),
        out_shape=jax.ShapeDtypeStruct((span_len, columns if backward else columns // 3), bf16),
        grid=(heads_here, blocks),
        in_specs=[whole, *[cut] * backward, *segments],
        out_specs=pl.BlockSpec((span_len, columns), lambda h, i: (0, 0)) if backward else cut,
        scratch_shapes=[pltpu.VMEM((span_len, HEAD), f32)] * (2 * backward),
        compiler_params=pltpu.CompilerParams(
            dimension_semantics=("arbitrary", "arbitrary"), vmem_limit_bytes=60 * 2**20
        ),
        cost_estimate=pl.CostEstimate(
            flops=(40 if backward else 20) * span_len * span_len * HEAD * heads_here,
            bytes_accessed=4 * span_len * columns,
            transcendentals=span_len * span_len * heads_here,
        ),
        name="attend_backward" if backward else "attend_forward",
    )(*[qkv, *[grad] * backward, segment.reshape(span_len, 1), segment.reshape(1, span_len)])


def finish_kernel(in_ref, gate_ref, down_ref):
    ffe = down_ref.shape[1]
    whole = in_ref[0].astype(f32)
    gate_ref[0, :, 0, :] = whole[:, :ffe]
    gate_ref[0, :, 1, :] = whole[:, ffe : 2 * ffe]
    down_ref[0] = whole[:, 2 * ffe :].T


def finish_grads(packed):
    count, rows, columns = packed.shape
    ffe = columns // 3
    return pl.pallas_call(
        finish_kernel,
        out_shape=[
            jax.ShapeDtypeStruct((count, rows, 2, ffe), f32),
            jax.ShapeDtypeStruct((count, ffe, rows), f32),
        ],
        grid=(count,),
        in_specs=[pl.BlockSpec((1, rows, columns), lambda e: (e, 0, 0))],
        out_specs=[
            pl.BlockSpec((1, rows, 2, ffe), lambda e: (e, 0, 0, 0)),
            pl.BlockSpec((1, ffe, rows), lambda e: (e, 0, 0)),
        ],
        compiler_params=pltpu.CompilerParams(vmem_limit_bytes=60 * 2**20),
        name="finish",
    )(packed)


def unpack_kernel(in_ref, out_ref):
    out_ref[...] = in_ref[0].astype(f32)


def unpack_columns(gathered, width, thirds):
    n_seq, rows, _ = gathered.shape
    return pl.pallas_call(
        unpack_kernel,
        out_shape=jax.ShapeDtypeStruct((rows, thirds * n_seq * width), f32),
        grid=(n_seq, thirds),
        in_specs=[pl.BlockSpec((1, rows, width), lambda s, p: (s, 0, p))],
        out_specs=pl.BlockSpec((rows, width), lambda s, p: (0, p * n_seq + s)),
        name="unpack",
    )(gathered)


def after(value, *others):
    if not others:
        return value
    return lax.optimization_barrier((value, *others))[0]


def reversed_bits(index, size):
    count, total = size.bit_length() - 1, 0
    for bit in range(count):
        total = total + (((index >> bit) & 1) << (count - 1 - bit))
    return total


def start_expert(mine, sent, *start, later=()):
    size = lax.axis_size("fsdp")
    mine, sent = after(mine, *start, *later), after(sent, *start)
    pieces = {size // 2: swap(sent, "fsdp", size // 2)}
    bit = size // 4
    while bit > 1:
        pieces[bit] = swap(mine, "fsdp", bit)
        bit //= 2
    return pieces


def finish_expert(pieces, *start):
    size = lax.axis_size("fsdp")
    pieces, brought = dict(pieces), {}
    for j in sorted(range(2, size, 2), key=lambda j: j.bit_count()):
        if j not in pieces:
            low = j & -j
            pieces[j] = brought[j] = swap(after(pieces[j ^ low], *start), "fsdp", low)
    return brought


def both_cores(pieces, *start):
    size = lax.axis_size("fsdp")
    return lax.all_gather(
        jnp.concatenate([after(piece, *start) for piece in pieces]),
        "fsdp",
        axis=0,
        tiled=True,
        axis_index_groups=[[i, i + 1] for i in range(0, size, 2)],
    )


def send_rows(piece, axis, *start):
    sent = after(piece, *start)
    return [piece, *[swap(sent, axis, k) for k in range(1, lax.axis_size(axis))]]


def join_rows(pieces, axis, *others):
    place, rows = lax.axis_index(axis), pieces[0].shape[0]
    whole = jnp.zeros((len(pieces) * rows, *pieces[0].shape[1:]), pieces[0].dtype)
    for k, piece in enumerate(pieces):
        piece = piece if k else after(piece, *others)
        whole = lax.dynamic_update_slice_in_dim(whole, piece, (place ^ k) * rows, 0)
    return whole


def scatter_rows(sums, axis):
    place, rows = lax.axis_index(axis), sums.shape[0] // lax.axis_size(axis)
    parts = [
        lax.dynamic_slice_in_dim(sums, (place ^ k) * rows, rows, 0)
        for k in range(lax.axis_size(axis))
    ]
    return sum((swap(part, axis, k) if k else part).astype(f32) for k, part in enumerate(parts))


def expert_kernel(size, tiles, parts, place_ref, share_ref, *rest):
    arrays = 1 + max(part[0] for part in parts)
    slots, pieces, rest = rest[:4], rest[4 : 4 + arrays], rest[4 + arrays :]
    made_refs, back_refs, rest = rest[:2], rest[2:4], rest[4:]
    send_ref, keep_ref, weights, x_ref, g_ref, act, grad_proj, sems = rest
    step = pl.program_id(0)
    place = place_ref[0]
    rows = weights.shape[0] // size
    ffe = act.shape[1]
    wide = ffe // tiles
    nn, nt, tn = ((1,), (0,)), ((1,), (1,)), ((0,), (0,))

    @pl.when(step == 0)
    def _():
        copies = [
            pltpu.make_async_copy(
                pieces[parts[j][0]].at[parts[j][1] + parts[j][2] * (1 - (place & 1))],
                weights.at[pl.ds(pl.multiple_of((place ^ j) * rows, rows), rows)],
                sems.at[j],
            )
            for j in range(size)
        ]
        count = slots[0].shape[0]
        for k, slot in enumerate(slots):
            copies.append(
                pltpu.make_async_copy(
                    slot,
                    (x_ref, g_ref)[k // 2].at[pl.ds(k % 2 * count, count)],
                    sems.at[size + k],
                )
            )
        for copy in copies:
            copy.start()
        for copy in copies:
            copy.wait()

    @pl.when(step < tiles)
    def _():
        first = pl.multiple_of(step * wide, wide)
        gate = dot(x_ref[...], weights[:, pl.ds(first, wide)], nn)
        up = dot(x_ref[...], weights[:, pl.ds(pl.multiple_of(ffe + first, wide), wide)], nn)
        grad_act = dot(
            g_ref[...], weights[:, pl.ds(pl.multiple_of(2 * ffe + first, wide), wide)], nn
        )
        sigma = 1.0 / (1.0 + jnp.exp(-gate))
        silu = gate * sigma
        act[:, pl.ds(first, wide)] = (silu * up).astype(bf16)
        grad_proj[:, pl.ds(first, wide)] = (
            grad_act * up * (sigma * (1.0 + gate * (1.0 - sigma)))
        ).astype(bf16)
        grad_proj[:, pl.ds(pl.multiple_of(ffe + first, wide), wide)] = (grad_act * silu).astype(
            bf16
        )

    @pl.when(step >= tiles)
    def _():
        turn = step - tiles
        whose = place ^ reversed_bits((turn + size // 2) % size, size)
        at = pl.ds(pl.multiple_of(whose * rows, rows), rows)
        count = act.shape[0] // 2
        made = (share_ref[...] * dot(act[...], weights[at, 2 * ffe :], nt)).astype(bf16)
        back = dot(grad_proj[...], weights[at, : 2 * ffe], nt).astype(bf16)
        for g in range(2):
            made_refs[g][...] = made[g * count : (g + 1) * count]
            back_refs[g][...] = back[g * count : (g + 1) * count]

        def grads(out_ref):
            out_ref[0, :, : 2 * ffe] = dot(x_ref[:, at], grad_proj[...], tn).astype(bf16)
            out_ref[0, :, 2 * ffe :] = dot(g_ref[:, at], act[...], tn).astype(bf16)

        @pl.when(turn < size // 2)
        def _():
            grads(send_ref)

        @pl.when(turn >= size // 2)
        def _():
            grads(keep_ref)


def run_expert(place, share, slots, grad_slots, pieces, parts):
    size, (_, rows, columns) = len(parts), pieces[0].shape
    count = 2 * slots[0].shape[0]
    ffe = columns // 3
    tiles = 4
    half = size // 2

    def whose(step, place):
        turn = jnp.maximum(step - tiles, 0)
        return 0, place[0] ^ reversed_bits((turn + half) % size, size)

    return pl.pallas_call(
        lambda *refs: expert_kernel(size, tiles, parts, *refs),
        out_shape=[
            *[jax.ShapeDtypeStruct((count // 2, D), bf16)] * 4,
            jax.ShapeDtypeStruct((half, rows, columns), bf16),
            jax.ShapeDtypeStruct((half, rows, columns), bf16),
        ],
        grid_spec=pltpu.PrefetchScalarGridSpec(
            num_scalar_prefetch=1,
            grid=(tiles + size,),
            in_specs=[
                pl.BlockSpec((count, 1), lambda step, place: (0, 0)),
                *[pl.BlockSpec(memory_space=pl.ANY)] * (len(pieces) + 4),
            ],
            out_specs=[
                *[pl.BlockSpec((count // 2, rows), whose)] * 4,
                pl.BlockSpec(
                    (1, rows, columns), lambda t, place: (jnp.clip(t - tiles, 0, half - 1), 0, 0)
                ),
                pl.BlockSpec(
                    (1, rows, columns),
                    lambda t, place: (jnp.clip(t - tiles - half, 0, half - 1), 0, 0),
                ),
            ],
            scratch_shapes=[
                pltpu.VMEM((size * rows, columns), bf16),
                pltpu.VMEM((count, D), bf16),
                pltpu.VMEM((count, D), bf16),
                pltpu.VMEM((count, ffe), bf16),
                pltpu.VMEM((count, 2 * ffe), bf16),
                pltpu.SemaphoreType.DMA((size + 4,)),
            ],
        ),
        compiler_params=pltpu.CompilerParams(
            dimension_semantics=("arbitrary",), vmem_limit_bytes=60 * 2**20
        ),
        cost_estimate=pl.CostEstimate(
            flops=18 * count * D * ffe,
            bytes_accessed=8 * count * D + 4 * size * rows * columns,
            transcendentals=count * ffe,
        ),
        name="expert",
    )(place, share, *slots, *grad_slots, *pieces)


class GradChain:
    def __init__(self, send, keep):
        self.bit, self.size = 1, lax.axis_size("fsdp")
        self.terms, self.send = [keep], send

    def arrive(self):
        if self.bit < self.size:
            self.terms.append(swap(self.send, "fsdp", self.bit))
            self.bit *= 2
        return self.terms[-1]

    def add(self, *others):
        many = self.terms[0].shape[0] // 2
        if many:
            if others:
                count = len(self.terms)
                self.terms = list(lax.optimization_barrier((*self.terms, *others))[:count])
            self.send = sum(t[many:].astype(f32) for t in self.terms).astype(bf16)
            self.terms = [t[:many] for t in self.terms]
        return self.send

    def sums(self):
        self.arrive()
        return self.add()

    def ended(self):
        other = self.terms.pop()[0]
        return sum(t[0].astype(f32) for t in self.terms).astype(bf16), other


def body(
    tokens, lengths, routes, gates, gain_attn, gain_moe, w_qkv, w_out, w_gate_up, w_down, cotangent
):
    n_seq, n_fsdp = lax.axis_size("seq"), lax.axis_size("fsdp")
    at_seq, at_fsdp = lax.axis_index("seq"), lax.axis_index("fsdp")
    rows = tokens.shape[1]
    shard = D // n_fsdp
    local_count = w_gate_up.shape[0]
    per_half = local_count // 2
    half = at_fsdp // (n_fsdp // 2)
    heads_here = HEADS // n_seq
    width = heads_here * HEAD
    span_len = rows * n_seq

    packed = jnp.concatenate(
        [w_gate_up.reshape(local_count, shard, 2 * FFE), jnp.swapaxes(w_down, 1, 2)], axis=2
    )
    own_part = lax.dynamic_slice_in_dim(packed, half * per_half, per_half, 0)
    other_part = lax.dynamic_slice_in_dim(packed, (1 - half) * per_half, per_half, 0)
    cot_other = swap(cotangent[0], "fsdp", n_fsdp // 2)
    x_parts = send_rows(tokens[0], "seq")
    cot_own = join_rows(send_rows(cotangent[0], "seq", *x_parts), "seq")

    part = lax.dynamic_slice_in_dim(
        w_qkv.reshape(shard, 3, HEADS, HEAD), at_seq * heads_here, heads_here, 2
    ).reshape(shard, 3 * width)
    gains = jnp.zeros((shard, 128), bf16).at[:, 0].set(gain_attn).at[:, 1].set(gain_moe)
    part = jnp.concatenate([part, gains], axis=1)
    gathered = lax.all_gather(part, "fsdp", axis=0, tiled=True)
    qkv_own = gathered[:, : 3 * width]
    gain_a = gathered[:, 3 * width].astype(f32)
    gain_m = gathered[:, 3 * width + 1].astype(f32)

    routing = jnp.concatenate([routes[0].astype(f32), gates[0]], axis=1)
    routing = jnp.stack([routing, swap(routing, "fsdp", n_fsdp // 2)])
    routing = jnp.swapaxes(lax.all_gather(routing, "seq", axis=0, tiled=False), 0, 1)
    routing = routing.reshape(2 * n_seq, rows, 2 * TOP)
    capacity = rows * TOP * 4 // (3 * local_count * n_seq) + 2
    capacity = -(-capacity // 8) * 8
    named = at_seq * local_count + half * per_half + lax.iota(jnp.int32, per_half)
    hits = routing[:, :, :TOP, None].astype(jnp.int32) == named
    mask = jnp.any(hits, axis=2)
    weight = jnp.sum(jnp.where(hits, routing[:, :, TOP:, None], 0.0), axis=2)
    below = (lax.iota(jnp.int32, rows)[:, None] > lax.iota(jnp.int32, rows)[None, :]).astype(bf16)
    rank = jnp.einsum("rq,bqe->bre", below, mask.astype(bf16), preferred_element_type=f32)
    rank = jnp.where(mask, rank.astype(jnp.int32), -1)
    picks = jnp.swapaxes(rank, 1, 2)[:, :, None, :] == lax.iota(jnp.int32, capacity)[:, None]
    share = jnp.sum(
        jnp.where(picks, jnp.swapaxes(weight, 1, 2)[:, :, None, :], 0.0), axis=3
    )
    picks = picks.astype(bf16)

    def normed_rows(values, gain):
        inverse = lax.rsqrt(jnp.mean(values * values, axis=1, keepdims=True) + epsilon)
        return (values * inverse * gain).astype(bf16), inverse

    x_all = join_rows(
        x_parts, "seq", own_part, other_part
    )
    out_full = lax.all_gather(after(w_out, part, *x_parts[1:]), "fsdp", axis=0, tiled=True)
    normed_a, _ = normed_rows(x_all.astype(f32), gain_a)
    qkv = dot(normed_a, qkv_own, ((1,), (0,))).astype(bf16)
    segment = segment_ids(lengths[0], span_len)
    attended = attend(qkv, segment)
    heads_rows = lax.all_to_all(attended, "seq", split_axis=0, concat_axis=1, tiled=True)
    cot_all = [cot_own, join_rows(send_rows(cot_other, "seq", cot_own), "seq")]
    cot_all = [rows_of.reshape(n_seq, rows, D) for rows_of in cot_all]
    begun = [start_expert(own_part[:1], other_part[:1], attended)]
    heads_rows = after(heads_rows, picks, share, *cot_all, *begun[0].values())
    experts = [finish_expert(begun[0], heads_rows)]
    x_float = tokens[0].astype(f32)
    resid = x_float + dot(heads_rows, out_full, ((1,), (0,)))
    normed_m, inv_m = normed_rows(resid, gain_m)
    moe_own = lax.all_gather(normed_m, "seq", axis=0, tiled=False)
    moe_other = after(swap(normed_m, "fsdp", n_fsdp // 2), moe_own)
    moe_all = [moe_own, lax.all_gather(moe_other, "seq", axis=0, tiled=False), moe_other]

    place = jnp.full((1,), at_fsdp, jnp.int32)
    forward_parts, backward_parts, chains = [], [], []

    def dispatch(i, g, source, weighted):
        at = slice(g * n_seq, (g + 1) * n_seq)
        part = dot(picks[at, i], source, ((2,), (1,)), ((0,), (0,)))
        if weighted:
            part = part * share[at, i, :, None]
        return part.astype(bf16).reshape(-1, D)

    sets = [[i] for i in range(per_half)]

    def begin(k, *start):
        cut = slice(sets[k][0], sets[k][-1] + 1)
        begun.append(start_expert(own_part[cut], other_part[cut], *start))

    begin(1, moe_all[2])
    begin(2, moe_all[1])
    beside = swap(after(own_part, normed_m), "fsdp", 1)
    near, last = [both_cores(list(begun[0].values()))], {}
    for i in range(per_half):
        k = [n for n, members in enumerate(sets) if i in members][0]
        first, later, many = begun[k], experts[k], len(sets[k])
        back = backward_parts[-1] if i else []
        ready = [near[k], *later.values(), *back]
        if k not in last:
            last[k] = swap(
                jnp.concatenate([after(p, *back[:1]) for p in later.values()]), "fsdp", 1
            )
        if i + 1 < per_half:
            ready.extend(begun[i + 1].values())
        cots = [after(cot_all[g], *back) for g in range(2)]
        for chain in chains[max(i - 3, 0) : max(i - 1, 0)]:
            ready.append(chain.arrive())
        if i == 0:
            ready = [dispatch(i, g, cots[g], True) for g in range(2)]
        slots = [dispatch(i, g, after(moe_all[g], *ready), False) for g in range(2)]
        ready = [chain.add(back[0]) for chain in chains[max(i - 3, 0) : max(i - 1, 0)]]
        slots[1] = after(slots[1], *ready)
        grad_slots = [dispatch(i, g, cots[g], True) for g in range(2)]
        if i + 1 < per_half:
            experts.append(finish_expert(begun[i + 1], slots[1]))
            near.append(both_cores(list(begun[i + 1].values()), slots[1]))
        even = [*first, *later]
        pieces = [own_part, beside, near[k], last[k], *first.values(), *later.values()]
        at = i - sets[k][0]
        parts = {0: (0, i, 0), 1: (1, i, 0)}
        for n, j in enumerate(even):
            parts[j] = (4 + n, at, 0)
            if j in first:
                parts[j + 1] = (2, n * many + at, len(first) * many)
            else:
                parts[j + 1] = (3, (n - len(first)) * many + at, 0)
        parts = [parts[j] for j in range(n_fsdp)]
        *made, send, keep = run_expert(
            place, share[:, i].reshape(-1, 1), slots, grad_slots, pieces, parts
        )
        forward_parts.append([part.reshape(n_seq, capacity, D) for part in made[:2]])
        backward_parts.append([part.reshape(n_seq, capacity, D) for part in made[2:]])
        chains.append(GradChain(send, keep))
        if i + 3 < per_half:
            begin(i + 3, made[2])

    every_pick = picks.reshape(2, n_seq, per_half * capacity, rows)

    def combine(parts, g, *others):
        together = jnp.concatenate([part[g] for part in parts], axis=1)
        if others:
            together = after(together, *others)
        total = dot(every_pick[g], together, ((1,), (1,)), ((0,), (0,)))
        return total.astype(bf16).reshape(span_len, D)

    def scatter(sums, *others):
        return lax.psum_scatter(after(sums, *others), "seq", scatter_dimension=0, tiled=True)

    back_other = combine(backward_parts, 1, *[chain.arrive() for chain in chains[:-2]])
    back_own = combine(backward_parts, 0, back_other)
    swapped_back = scatter(back_other)
    ready = [chain.arrive() for chain in chains[-2:]]
    ready.extend(chain.add(back_own) for chain in chains[-3:])
    ready.append(chains[-3].arrive())
    grad_normed_m = scatter(back_own, swapped_back, *ready)
    swapped_back = swap(swapped_back, "fsdp", n_fsdp // 2)
    ready = [swapped_back, chains[-2].arrive()]
    made_other = combine(forward_parts, 1, back_own)
    made_own = combine(forward_parts, 0, made_other, *ready)
    mixed_other = scatter(made_other, grad_normed_m, made_own)
    ready = [made_own]
    grad_normed_m = after(grad_normed_m, *ready).astype(f32) + swapped_back.astype(f32)

    scaled_m = grad_normed_m * gain_m
    grad_resid = (
        cotangent[0].astype(f32)
        + inv_m * scaled_m
        - inv_m * inv_m * inv_m * resid * jnp.mean(scaled_m * resid, axis=1, keepdims=True)
    )
    grad_gain_m = jnp.sum(grad_normed_m * resid * inv_m, axis=0)
    grad_attn = grad_resid.astype(bf16)
    grad_heads_rows = dot(grad_attn, out_full, ((1,), (1,))).astype(bf16)
    mixed_own = scatter(made_own, grad_heads_rows)
    grad_heads = lax.all_to_all(
        grad_heads_rows, "seq", split_axis=1, concat_axis=0, tiled=True
    )
    chains[-2].add(grad_heads_rows)
    out_sum = []
    for k in range(n_seq):
        columns = lax.dynamic_slice_in_dim(grad_attn, (at_seq ^ k) * width, width, 1)
        part = dot(heads_rows, columns, ((0,), (0,))).astype(bf16)
        out_sum.append(part)
    grad_qkv = attend(qkv, segment, grad_heads)
    ready = [chain.arrive() for chain in chains[-2:]]
    grad_qkv = after(grad_qkv, mixed_other, *ready)
    mixed_other = swap(after(mixed_other, grad_qkv), "fsdp", n_fsdp // 2)
    mixed = (resid + mixed_own.astype(f32) + mixed_other.astype(f32)).astype(bf16)

    grad_qkv_w = dot(normed_a, grad_qkv, ((0,), (0,))).astype(bf16)
    reduced_qkv = after(grad_qkv_w, mixed_own)
    reduced_qkv = lax.psum_scatter(reduced_qkv, "fsdp", scatter_dimension=0, tiled=True)
    part_normed_a = dot(after(grad_qkv, grad_qkv_w), qkv_own, ((1,), (1,)))
    part_sent = part_normed_a.astype(bf16)
    ready = [part_sent, chains[-1].add(grad_qkv_w)]
    out_sum = [swap(after(p, grad_qkv_w), "seq", k) if k else p for k, p in enumerate(out_sum)]
    qkv_sum = after(reduced_qkv, mixed_other, *ready, *out_sum[1:])
    qkv_sum = lax.all_gather(qkv_sum, "seq", axis=0, tiled=False)
    grad_normed_a = scatter_rows(after(part_sent, qkv_sum), "seq")
    out_sum[0] = after(out_sum[0], qkv_sum, chains[-1].arrive())
    out_sum = sum(part.astype(f32) for part in out_sum).astype(bf16)
    gain_column = jnp.zeros((D, 128), bf16).at[:, 0].set(grad_gain_m.astype(bf16))
    out_sum = jnp.concatenate([out_sum, gain_column], axis=1)
    out_sum = lax.psum_scatter(out_sum, "fsdp", scatter_dimension=0, tiled=True)
    out_sum = lax.all_gather(out_sum, "seq", axis=0, tiled=False)
    qkv_sum = unpack_columns(qkv_sum, width, 3)
    gain_m_sum = jnp.sum(out_sum[:, :, width].astype(f32), axis=0)
    out_sum = unpack_columns(out_sum, width, 1)
    gain_a_sum = jnp.sum(w_qkv.astype(f32) * qkv_sum, axis=1) / gain_attn.astype(f32)
    inv_a = lax.rsqrt(jnp.mean(x_float * x_float, axis=1, keepdims=True) + epsilon)
    scaled_a = grad_normed_a * gain_a
    grad_x = (
        grad_resid
        + inv_a * scaled_a
        - inv_a * inv_a * inv_a * x_float * jnp.mean(scaled_a * x_float, axis=1, keepdims=True)
    )

    for chain in chains:
        while chain.bit < n_fsdp:
            chain.sums()
    ended = [chain.ended() for chain in chains]
    own_grads, other_grads = jnp.stack([e[0] for e in ended]), jnp.stack([e[1] for e in ended])
    first = half == 0
    grad_all = jnp.concatenate(
        [jnp.where(first, own_grads, other_grads), jnp.where(first, other_grads, own_grads)]
    )
    grad_gate_up, grad_down = finish_grads(grad_all)
    return (
        mixed[None],
        grad_x.astype(bf16)[None],
        gain_a_sum,
        gain_m_sum,
        qkv_sum,
        out_sum,
        grad_gate_up,
        grad_down,
    )


def solution(mesh):
    placed = (
        P("fsdp", "seq", None),
        P("fsdp", None),
        P("fsdp", "seq", None),
        P("fsdp", "seq", None),
        P("fsdp"),
        P("fsdp"),
        P("fsdp", None),
        P("fsdp", None),
        P("seq", "fsdp", None, None),
        P("seq", None, "fsdp"),
        P("fsdp", "seq", None),
    )
    return jax.shard_map(
        body,
        mesh=mesh,
        in_specs=placed,
        out_specs=(
            P("fsdp", "seq", None),
            P("fsdp", "seq", None),
            P("fsdp"),
            P("fsdp"),
            P("fsdp", None),
            P("fsdp", None),
            P("seq", "fsdp", None, None),
            P("seq", None, "fsdp"),
        ),
        check_vma=False,
    )
```

```python
import jax
import jax.numpy as jnp
from jax import lax
from jax.experimental import pallas as pl
from jax.experimental.pallas import tpu as pltpu
from jax.sharding import PartitionSpec as P

D = 2048
HEADS = 16
HEAD = 128
FFE = 1024
TOP = 8

epsilon = 1e-06
f32 = jnp.float32
bf16 = jnp.bfloat16


def swap(value, axis, bit):
    size = lax.axis_size(axis)
    return lax.ppermute(value, axis, [(i, i ^ bit) for i in range(size)])


def dot(a, b, contract, batch=((), ())):
    return lax.dot_general(a, b, (contract, batch), preferred_element_type=f32)


def segment_ids(length_row, span_len):
    ends = jnp.cumsum(length_row)
    places = lax.iota(jnp.int32, span_len)
    return jnp.sum((places[:, None] >= ends[None, :]).astype(jnp.int32), axis=1)


def score_probs(keys, queries, seg_column, seg_row):
    raw = dot(keys, queries, ((1,), (1,)))
    raw = jnp.where(seg_column == seg_row, raw, -1e30)
    top = jnp.max(raw, axis=0, keepdims=True)
    part = jnp.exp((raw - top) * HEAD ** (-0.5))
    return part * (1.0 / jnp.sum(part, axis=0, keepdims=True))


def head_columns(heads_here, head):
    return [
        pl.ds(pl.multiple_of((third * heads_here + head) * HEAD, HEAD), HEAD) for third in range(3)
    ]


def attend_forward_kernel(heads_here, qkv_ref, seg_column, seg_row, out_ref):
    block = out_ref.shape[0]
    at = pl.ds(pl.multiple_of(pl.program_id(1) * block, block), block)
    q_at, k_at, v_at = head_columns(heads_here, pl.program_id(0))
    probs = score_probs(qkv_ref[:, k_at], qkv_ref[at, q_at], seg_column[...], seg_row[...])
    out_ref[...] = dot(qkv_ref[:, v_at], probs.astype(bf16), ((0,), (0,))).T.astype(bf16)


def attend_backward_kernel(
    heads_here, qkv_ref, grad_ref, seg_column, seg_row, out_ref, grad_k, grad_v
):
    block = grad_ref.shape[0]
    turn = pl.program_id(1)
    at = pl.ds(pl.multiple_of(turn * block, block), block)
    q_at, k_at, v_at = head_columns(heads_here, pl.program_id(0))
    queries, keys, grads = qkv_ref[at, q_at], qkv_ref[:, k_at], grad_ref[...]
    probs = score_probs(keys, queries, seg_column[...], seg_row[...])
    grad_probs = dot(qkv_ref[:, v_at], grads, ((1,), (1,)))
    inner = jnp.sum(probs * grad_probs, axis=0, keepdims=True)
    grad_scores = (probs * (grad_probs - inner)).astype(bf16)
    scale = HEAD ** (-0.5)

    @pl.when(turn == 0)
    def _():
        grad_k[...] = jnp.zeros_like(grad_k)
        grad_v[...] = jnp.zeros_like(grad_v)

    grad_v[...] += dot(probs.astype(bf16), grads, ((1,), (0,)))
    grad_k[...] += dot(grad_scores, queries, ((1,), (0,)))
    out_ref[at, q_at] = (dot(keys, grad_scores, ((0,), (0,))).T * scale).astype(bf16)

    @pl.when(turn == pl.num_programs(1) - 1)
    def _():
        out_ref[:, k_at] = (grad_k[...] * scale).astype(bf16)
        out_ref[:, v_at] = grad_v[...].astype(bf16)


def attend(qkv, segment, grad=None):
    span_len, columns = qkv.shape
    heads_here = columns // (3 * HEAD)
    blocks = 3
    block = span_len // blocks
    whole = pl.BlockSpec((span_len, columns), lambda h, i: (0, 0), pipeline_mode=pl.Buffered(1))
    cut = pl.BlockSpec((block, HEAD), lambda h, i: (i, h))
    segments = [
        pl.BlockSpec((span_len, 1), lambda h, i: (0, 0)),
        pl.BlockSpec((1, block), lambda h, i: (0, i)),
    ]
    backward = grad is not None
    return pl.pallas_call(
        lambda *refs: (attend_backward_kernel if backward else attend_forward_kernel)(
            heads_here, *refs
        ),
        out_shape=jax.ShapeDtypeStruct((span_len, columns if backward else columns // 3), bf16),
        grid=(heads_here, blocks),
        in_specs=[whole, *[cut] * backward, *segments],
        out_specs=pl.BlockSpec((span_len, columns), lambda h, i: (0, 0)) if backward else cut,
        scratch_shapes=[pltpu.VMEM((span_len, HEAD), f32)] * (2 * backward),
        compiler_params=pltpu.CompilerParams(
            dimension_semantics=("arbitrary", "arbitrary"), vmem_limit_bytes=60 * 2**20
        ),
        cost_estimate=pl.CostEstimate(
            flops=(40 if backward else 20) * span_len * span_len * HEAD * heads_here,
            bytes_accessed=4 * span_len * columns,
            transcendentals=span_len * span_len * heads_here,
        ),
        name="attend_backward" if backward else "attend_forward",
    )(*[qkv, *[grad] * backward, segment.reshape(span_len, 1), segment.reshape(1, span_len)])


def finish_kernel(in_ref, gate_ref, down_ref):
    ffe = down_ref.shape[1]
    whole = in_ref[0].astype(f32)
    gate_ref[0, :, 0, :] = whole[:, :ffe]
    gate_ref[0, :, 1, :] = whole[:, ffe : 2 * ffe]
    down_ref[0] = whole[:, 2 * ffe :].T


def finish_grads(packed):
    count, rows, columns = packed.shape
    ffe = columns // 3
    return pl.pallas_call(
        finish_kernel,
        out_shape=[
            jax.ShapeDtypeStruct((count, rows, 2, ffe), f32),
            jax.ShapeDtypeStruct((count, ffe, rows), f32),
        ],
        grid=(count,),
        in_specs=[pl.BlockSpec((1, rows, columns), lambda e: (e, 0, 0))],
        out_specs=[
            pl.BlockSpec((1, rows, 2, ffe), lambda e: (e, 0, 0, 0)),
            pl.BlockSpec((1, ffe, rows), lambda e: (e, 0, 0)),
        ],
        compiler_params=pltpu.CompilerParams(vmem_limit_bytes=60 * 2**20),
        name="finish",
    )(packed)


def unpack_kernel(in_ref, out_ref):
    out_ref[...] = in_ref[0].astype(f32)


def unpack_columns(gathered, width, thirds):
    n_seq, rows, _ = gathered.shape
    return pl.pallas_call(
        unpack_kernel,
        out_shape=jax.ShapeDtypeStruct((rows, thirds * n_seq * width), f32),
        grid=(n_seq, thirds),
        in_specs=[pl.BlockSpec((1, rows, width), lambda s, p: (s, 0, p))],
        out_specs=pl.BlockSpec((rows, width), lambda s, p: (0, p * n_seq + s)),
        name="unpack",
    )(gathered)


def after(value, *others):
    if not others:
        return value
    return lax.optimization_barrier((value, *others))[0]


def reversed_bits(index, size):
    count, total = size.bit_length() - 1, 0
    for bit in range(count):
        total = total + (((index >> bit) & 1) << (count - 1 - bit))
    return total


def start_expert(mine, sent, *start, later=()):
    size = lax.axis_size("fsdp")
    mine, sent = after(mine, *start, *later), after(sent, *start)
    pieces = {size // 2: swap(sent, "fsdp", size // 2)}
    bit = size // 4
    while bit > 1:
        pieces[bit] = swap(mine, "fsdp", bit)
        bit //= 2
    return pieces


def finish_expert(pieces, *start):
    size = lax.axis_size("fsdp")
    pieces, brought = dict(pieces), {}
    for j in sorted(range(2, size, 2), key=lambda j: j.bit_count()):
        if j not in pieces:
            low = j & -j
            pieces[j] = brought[j] = swap(after(pieces[j ^ low], *start), "fsdp", low)
    return brought


def both_cores(pieces, *start):
    size = lax.axis_size("fsdp")
    return lax.all_gather(
        jnp.concatenate([after(piece, *start) for piece in pieces]),
        "fsdp",
        axis=0,
        tiled=True,
        axis_index_groups=[[i, i + 1] for i in range(0, size, 2)],
    )


def send_rows(piece, axis, *start):
    sent = after(piece, *start)
    return [piece, *[swap(sent, axis, k) for k in range(1, lax.axis_size(axis))]]


def join_rows(pieces, axis, *others):
    place, rows = lax.axis_index(axis), pieces[0].shape[0]
    whole = jnp.zeros((len(pieces) * rows, *pieces[0].shape[1:]), pieces[0].dtype)
    for k, piece in enumerate(pieces):
        piece = piece if k else after(piece, *others)
        whole = lax.dynamic_update_slice_in_dim(whole, piece, (place ^ k) * rows, 0)
    return whole


def scatter_rows(sums, axis):
    place, rows = lax.axis_index(axis), sums.shape[0] // lax.axis_size(axis)
    parts = [
        lax.dynamic_slice_in_dim(sums, (place ^ k) * rows, rows, 0)
        for k in range(lax.axis_size(axis))
    ]
    return sum((swap(part, axis, k) if k else part).astype(f32) for k, part in enumerate(parts))


def expert_kernel(size, tiles, parts, place_ref, share_ref, *rest):
    arrays = 1 + max(part[0] for part in parts)
    slots, pieces, rest = rest[:4], rest[4 : 4 + arrays], rest[4 + arrays :]
    made_refs, back_refs, rest = rest[:2], rest[2:4], rest[4:]
    send_ref, keep_ref, weights, x_ref, g_ref, act, grad_proj, sems = rest
    step = pl.program_id(0)
    place = place_ref[0]
    rows = weights.shape[0] // size
    ffe = act.shape[1]
    wide = ffe // tiles
    nn, nt, tn = ((1,), (0,)), ((1,), (1,)), ((0,), (0,))

    @pl.when(step == 0)
    def _():
        copies = [
            pltpu.make_async_copy(
                pieces[parts[j][0]].at[parts[j][1] + parts[j][2] * (1 - (place & 1))],
                weights.at[pl.ds(pl.multiple_of((place ^ j) * rows, rows), rows)],
                sems.at[j],
            )
            for j in range(size)
        ]
        count = slots[0].shape[0]
        for k, slot in enumerate(slots):
            copies.append(
                pltpu.make_async_copy(
                    slot,
                    (x_ref, g_ref)[k // 2].at[pl.ds(k % 2 * count, count)],
                    sems.at[size + k],
                )
            )
        for copy in copies:
            copy.start()
        for copy in copies:
            copy.wait()

    @pl.when(step < tiles)
    def _():
        first = pl.multiple_of(step * wide, wide)
        gate = dot(x_ref[...], weights[:, pl.ds(first, wide)], nn)
        up = dot(x_ref[...], weights[:, pl.ds(pl.multiple_of(ffe + first, wide), wide)], nn)
        grad_act = dot(
            g_ref[...], weights[:, pl.ds(pl.multiple_of(2 * ffe + first, wide), wide)], nn
        )
        sigma = 1.0 / (1.0 + jnp.exp(-gate))
        silu = gate * sigma
        act[:, pl.ds(first, wide)] = (silu * up).astype(bf16)
        grad_proj[:, pl.ds(first, wide)] = (
            grad_act * up * (sigma * (1.0 + gate * (1.0 - sigma)))
        ).astype(bf16)
        grad_proj[:, pl.ds(pl.multiple_of(ffe + first, wide), wide)] = (grad_act * silu).astype(
            bf16
        )

    @pl.when(step >= tiles)
    def _():
        turn = step - tiles
        whose = place ^ reversed_bits((turn + size // 2) % size, size)
        at = pl.ds(pl.multiple_of(whose * rows, rows), rows)
        count = act.shape[0] // 2
        made = (share_ref[...] * dot(act[...], weights[at, 2 * ffe :], nt)).astype(bf16)
        back = dot(grad_proj[...], weights[at, : 2 * ffe], nt).astype(bf16)
        for g in range(2):
            made_refs[g][...] = made[g * count : (g + 1) * count]
            back_refs[g][...] = back[g * count : (g + 1) * count]

        def grads(out_ref):
            out_ref[0, :, : 2 * ffe] = dot(x_ref[:, at], grad_proj[...], tn).astype(bf16)
            out_ref[0, :, 2 * ffe :] = dot(g_ref[:, at], act[...], tn).astype(bf16)

        @pl.when(turn < size // 2)
        def _():
            grads(send_ref)

        @pl.when(turn >= size // 2)
        def _():
            grads(keep_ref)


def run_expert(place, share, slots, grad_slots, pieces, parts):
    size, (_, rows, columns) = len(parts), pieces[0].shape
    count = 2 * slots[0].shape[0]
    ffe = columns // 3
    tiles = 4
    half = size // 2

    def whose(step, place):
        turn = jnp.maximum(step - tiles, 0)
        return 0, place[0] ^ reversed_bits((turn + half) % size, size)

    return pl.pallas_call(
        lambda *refs: expert_kernel(size, tiles, parts, *refs),
        out_shape=[
            *[jax.ShapeDtypeStruct((count // 2, D), bf16)] * 4,
            jax.ShapeDtypeStruct((half, rows, columns), bf16),
            jax.ShapeDtypeStruct((half, rows, columns), bf16),
        ],
        grid_spec=pltpu.PrefetchScalarGridSpec(
            num_scalar_prefetch=1,
            grid=(tiles + size,),
            in_specs=[
                pl.BlockSpec((count, 1), lambda step, place: (0, 0)),
                *[pl.BlockSpec(memory_space=pl.ANY)] * (len(pieces) + 4),
            ],
            out_specs=[
                *[pl.BlockSpec((count // 2, rows), whose)] * 4,
                pl.BlockSpec(
                    (1, rows, columns), lambda t, place: (jnp.clip(t - tiles, 0, half - 1), 0, 0)
                ),
                pl.BlockSpec(
                    (1, rows, columns),
                    lambda t, place: (jnp.clip(t - tiles - half, 0, half - 1), 0, 0),
                ),
            ],
            scratch_shapes=[
                pltpu.VMEM((size * rows, columns), bf16),
                pltpu.VMEM((count, D), bf16),
                pltpu.VMEM((count, D), bf16),
                pltpu.VMEM((count, ffe), bf16),
                pltpu.VMEM((count, 2 * ffe), bf16),
                pltpu.SemaphoreType.DMA((size + 4,)),
            ],
        ),
        compiler_params=pltpu.CompilerParams(
            dimension_semantics=("arbitrary",), vmem_limit_bytes=60 * 2**20
        ),
        cost_estimate=pl.CostEstimate(
            flops=18 * count * D * ffe,
            bytes_accessed=8 * count * D + 4 * size * rows * columns,
            transcendentals=count * ffe,
        ),
        name="expert",
    )(place, share, *slots, *grad_slots, *pieces)


class GradChain:
    def __init__(self, send, keep):
        self.bit, self.size = 1, lax.axis_size("fsdp")
        self.terms, self.send = [keep], send

    def arrive(self):
        if self.bit < self.size:
            self.terms.append(swap(self.send, "fsdp", self.bit))
            self.bit *= 2
        return self.terms[-1]

    def add(self, *others):
        many = self.terms[0].shape[0] // 2
        if many:
            if others:
                count = len(self.terms)
                self.terms = list(lax.optimization_barrier((*self.terms, *others))[:count])
            self.send = sum(t[many:].astype(f32) for t in self.terms).astype(bf16)
            self.terms = [t[:many] for t in self.terms]
        return self.send

    def sums(self):
        self.arrive()
        return self.add()

    def ended(self):
        other = self.terms.pop()[0]
        return sum(t[0].astype(f32) for t in self.terms).astype(bf16), other


def body(
    tokens, lengths, routes, gates, gain_attn, gain_moe, w_qkv, w_out, w_gate_up, w_down, cotangent
):
    n_seq, n_fsdp = lax.axis_size("seq"), lax.axis_size("fsdp")
    at_seq, at_fsdp = lax.axis_index("seq"), lax.axis_index("fsdp")
    rows = tokens.shape[1]
    shard = D // n_fsdp
    local_count = w_gate_up.shape[0]
    per_half = local_count // 2
    half = at_fsdp // (n_fsdp // 2)
    heads_here = HEADS // n_seq
    width = heads_here * HEAD
    span_len = rows * n_seq

    packed = jnp.concatenate(
        [w_gate_up.reshape(local_count, shard, 2 * FFE), jnp.swapaxes(w_down, 1, 2)], axis=2
    )
    own_part = lax.dynamic_slice_in_dim(packed, half * per_half, per_half, 0)
    other_part = lax.dynamic_slice_in_dim(packed, (1 - half) * per_half, per_half, 0)
    cot_other = swap(cotangent[0], "fsdp", n_fsdp // 2)
    x_parts = send_rows(tokens[0], "seq")
    cot_own = join_rows(send_rows(cotangent[0], "seq", *x_parts), "seq")

    part = lax.dynamic_slice_in_dim(
        w_qkv.reshape(shard, 3, HEADS, HEAD), at_seq * heads_here, heads_here, 2
    ).reshape(shard, 3 * width)
    gains = jnp.zeros((shard, 128), bf16).at[:, 0].set(gain_attn).at[:, 1].set(gain_moe)
    gathered = lax.all_gather(
        jnp.concatenate([part, gains], axis=1), "fsdp", axis=0, tiled=True
    )
    qkv_own = gathered[:, : 3 * width]
    gain_a = gathered[:, 3 * width].astype(f32)
    gain_m = gathered[:, 3 * width + 1].astype(f32)

    routing = jnp.concatenate([routes[0].astype(f32), gates[0]], axis=1)
    routing = jnp.stack([routing, swap(routing, "fsdp", n_fsdp // 2)])
    routing = jnp.swapaxes(lax.all_gather(routing, "seq", axis=0, tiled=False), 0, 1)
    routing = routing.reshape(2 * n_seq, rows, 2 * TOP)
    capacity = rows * TOP * 4 // (3 * local_count * n_seq) + 2
    capacity = -(-capacity // 8) * 8
    named = at_seq * local_count + half * per_half + lax.iota(jnp.int32, per_half)
    hits = routing[:, :, :TOP, None].astype(jnp.int32) == named
    mask = jnp.any(hits, axis=2)
    weight = jnp.sum(jnp.where(hits, routing[:, :, TOP:, None], 0.0), axis=2)
    below = (lax.iota(jnp.int32, rows)[:, None] > lax.iota(jnp.int32, rows)[None, :]).astype(bf16)
    rank = jnp.einsum("rq,bqe->bre", below, mask.astype(bf16), preferred_element_type=f32)
    rank = jnp.where(mask, rank.astype(jnp.int32), -1)
    picks = jnp.swapaxes(rank, 1, 2)[:, :, None, :] == lax.iota(jnp.int32, capacity)[:, None]
    share = jnp.sum(
        jnp.where(picks, jnp.swapaxes(weight, 1, 2)[:, :, None, :], 0.0), axis=3
    )
    picks = picks.astype(bf16)

    def normed_rows(values, gain):
        inverse = lax.rsqrt(jnp.mean(values * values, axis=1, keepdims=True) + epsilon)
        return (values * inverse * gain).astype(bf16), inverse

    x_all = join_rows(
        x_parts, "seq", own_part, other_part, picks, share, cot_own, cot_other
    )
    out_full = lax.all_gather(after(w_out, x_all), "fsdp", axis=0, tiled=True)
    normed_a, _ = normed_rows(x_all.astype(f32), gain_a)
    qkv = dot(normed_a, qkv_own, ((1,), (0,))).astype(bf16)
    segment = segment_ids(lengths[0], span_len)
    attended = attend(qkv, segment)
    heads_rows = lax.all_to_all(attended, "seq", split_axis=0, concat_axis=1, tiled=True)
    cot_all = [cot_own, join_rows(send_rows(cot_other, "seq", cot_own), "seq")]
    cot_all = [rows_of.reshape(n_seq, rows, D) for rows_of in cot_all]
    begun = [start_expert(own_part[:1], other_part[:1], attended)]
    heads_rows = after(heads_rows, *cot_all, *begun[0].values())
    experts = [finish_expert(begun[0], heads_rows)]
    x_float = tokens[0].astype(f32)
    resid = x_float + dot(heads_rows, out_full, ((1,), (0,)))
    normed_m, inv_m = normed_rows(resid, gain_m)
    moe_own = lax.all_gather(normed_m, "seq", axis=0, tiled=False)
    moe_other = after(swap(normed_m, "fsdp", n_fsdp // 2), moe_own)
    moe_all = [moe_own, lax.all_gather(moe_other, "seq", axis=0, tiled=False), moe_other]

    place = jnp.full((1,), at_fsdp, jnp.int32)
    forward_parts, backward_parts, chains = [], [], []

    def dispatch(i, g, source, weighted):
        at = slice(g * n_seq, (g + 1) * n_seq)
        part = dot(picks[at, i], source, ((2,), (1,)), ((0,), (0,)))
        if weighted:
            part = part * share[at, i, :, None]
        return part.astype(bf16).reshape(-1, D)

    sets = [[i] for i in range(per_half)]

    def begin(k, *start):
        cut = slice(sets[k][0], sets[k][-1] + 1)
        begun.append(start_expert(own_part[cut], other_part[cut], *start))

    begin(1, moe_all[2])
    begin(2, moe_all[1])
    beside = swap(after(own_part, normed_m), "fsdp", 1)
    near, last = [both_cores(list(begun[0].values()))], {}
    every_grad_slots = []
    for i in range(per_half):
        k = [n for n, members in enumerate(sets) if i in members][0]
        first, later, many = begun[k], experts[k], len(sets[k])
        back = backward_parts[-1] if i else []
        ready = [near[k], *later.values(), *back]
        if k not in last:
            last[k] = swap(
                jnp.concatenate([after(p, *back[:1]) for p in later.values()]), "fsdp", 1
            )
        if i + 1 < per_half:
            ready.extend(begun[i + 1].values())
        if i < 2:
            cots = [after(cot_all[g], *back) for g in range(2)]
            every_grad_slots.extend(
                [dispatch(j, g, cots[g], True) for g in range(2)]
                for j in (range(1, per_half) if i else (0,))
            )
        for chain in chains[max(i - 3, 0) : max(i - 1, 0)]:
            ready.append(chain.arrive())
        if i == 0:
            ready = every_grad_slots[0]
        slots = [dispatch(i, g, after(moe_all[g], *ready), False) for g in range(2)]
        ready = [chain.add(back[0]) for chain in chains[max(i - 3, 0) : max(i - 1, 0)]]
        slots[1] = after(slots[1], *ready)
        grad_slots = every_grad_slots[i]
        if i == 1:
            slots[1] = after(slots[1], *[part for parts in every_grad_slots[1:] for part in parts])
        if i + 1 < per_half:
            experts.append(finish_expert(begun[i + 1], slots[1]))
            near.append(both_cores(list(begun[i + 1].values()), slots[1]))
        even = [*first, *later]
        pieces = [own_part, beside, near[k], last[k], *first.values(), *later.values()]
        at = i - sets[k][0]
        parts = {0: (0, i, 0), 1: (1, i, 0)}
        for n, j in enumerate(even):
            parts[j] = (4 + n, at, 0)
            if j in first:
                parts[j + 1] = (2, n * many + at, len(first) * many)
            else:
                parts[j + 1] = (3, (n - len(first)) * many + at, 0)
        parts = [parts[j] for j in range(n_fsdp)]
        *made, send, keep = run_expert(
            place, share[:, i].reshape(-1, 1), slots, grad_slots, pieces, parts
        )
        forward_parts.append([part.reshape(n_seq, capacity, D) for part in made[:2]])
        backward_parts.append([part.reshape(n_seq, capacity, D) for part in made[2:]])
        chains.append(GradChain(send, keep))
        if i + 3 < per_half:
            begin(i + 3, made[2])

    every_pick = picks.reshape(2, n_seq, per_half * capacity, rows)

    def combine(parts, g, *others):
        together = jnp.concatenate([part[g] for part in parts], axis=1)
        if others:
            together = after(together, *others)
        total = dot(every_pick[g], together, ((1,), (1,)), ((0,), (0,)))
        return total.astype(bf16).reshape(span_len, D)

    def scatter(sums, *others):
        return lax.psum_scatter(after(sums, *others), "seq", scatter_dimension=0, tiled=True)

    back_other = combine(backward_parts, 1, *[chain.arrive() for chain in chains[:-2]])
    back_own = combine(backward_parts, 0, back_other)
    swapped_back = scatter(back_other)
    ready = [chain.arrive() for chain in chains[-2:]]
    ready.extend(chain.add(back_own) for chain in chains[-3:])
    ready.append(chains[-3].arrive())
    grad_normed_m = scatter(back_own, swapped_back, *ready)
    swapped_back = swap(swapped_back, "fsdp", n_fsdp // 2)
    ready = [swapped_back, chains[-2].arrive()]
    made_other = combine(forward_parts, 1, back_own)
    made_own = combine(forward_parts, 0, made_other, *ready)
    mixed_other, mixed_own = scatter(made_other, grad_normed_m), scatter(made_own, grad_normed_m)
    ready = [made_own]
    grad_normed_m = after(grad_normed_m, *ready).astype(f32) + swapped_back.astype(f32)

    scaled_m = grad_normed_m * gain_m
    grad_resid = (
        cotangent[0].astype(f32)
        + inv_m * scaled_m
        - inv_m * inv_m * inv_m * resid * jnp.mean(scaled_m * resid, axis=1, keepdims=True)
    )
    grad_gain_m = jnp.sum(grad_normed_m * resid * inv_m, axis=0)
    grad_attn = grad_resid.astype(bf16)
    grad_heads_rows = dot(grad_attn, out_full, ((1,), (1,))).astype(bf16)
    grad_heads = lax.all_to_all(
        grad_heads_rows, "seq", split_axis=1, concat_axis=0, tiled=True
    )
    chains[-2].add(grad_heads_rows)
    out_sum = []
    for k in range(n_seq):
        columns = lax.dynamic_slice_in_dim(grad_attn, (at_seq ^ k) * width, width, 1)
        part = dot(heads_rows, columns, ((0,), (0,))).astype(bf16)
        out_sum.append(part)
    grad_qkv = attend(qkv, segment, grad_heads)
    ready = [chain.arrive() for chain in chains[-2:]]
    grad_qkv = after(grad_qkv, mixed_own, *ready)
    mixed_other = swap(after(mixed_other, grad_qkv), "fsdp", n_fsdp // 2)
    mixed = (resid + mixed_own.astype(f32) + mixed_other.astype(f32)).astype(bf16)

    grad_qkv_w = dot(normed_a, grad_qkv, ((0,), (0,))).astype(bf16)
    reduced_qkv = lax.psum_scatter(grad_qkv_w, "fsdp", scatter_dimension=0, tiled=True)
    part_normed_a = dot(after(grad_qkv, grad_qkv_w), qkv_own, ((1,), (1,)))
    part_sent = part_normed_a.astype(bf16)
    ready = [part_sent, chains[-1].add(grad_qkv_w)]
    out_sum = [swap(after(p, grad_qkv_w), "seq", k) if k else p for k, p in enumerate(out_sum)]
    grad_normed_a = scatter_rows(after(part_sent, *out_sum), "seq")
    qkv_sum = after(reduced_qkv, mixed_other, *ready, *out_sum[1:])
    qkv_sum = lax.all_gather(qkv_sum, "seq", axis=0, tiled=False)
    out_sum[0] = after(out_sum[0], qkv_sum, grad_normed_a, chains[-1].arrive())
    out_sum = sum(part.astype(f32) for part in out_sum).astype(bf16)
    gain_column = jnp.zeros((D, 128), bf16).at[:, 0].set(grad_gain_m.astype(bf16))
    out_sum = jnp.concatenate([out_sum, gain_column], axis=1)
    out_sum = lax.psum_scatter(out_sum, "fsdp", scatter_dimension=0, tiled=True)
    out_sum = lax.all_gather(out_sum, "seq", axis=0, tiled=False)
    qkv_sum = unpack_columns(qkv_sum, width, 3)
    gain_m_sum = jnp.sum(out_sum[:, :, width].astype(f32), axis=0)
    out_sum = unpack_columns(out_sum, width, 1)
    gain_a_sum = jnp.sum(w_qkv.astype(f32) * qkv_sum, axis=1) / gain_attn.astype(f32)
    inv_a = lax.rsqrt(jnp.mean(x_float * x_float, axis=1, keepdims=True) + epsilon)
    scaled_a = grad_normed_a * gain_a
    grad_x = (
        grad_resid
        + inv_a * scaled_a
        - inv_a * inv_a * inv_a * x_float * jnp.mean(scaled_a * x_float, axis=1, keepdims=True)
    )

    for chain in chains:
        while chain.bit < n_fsdp:
            chain.sums()
    ended = [chain.ended() for chain in chains]
    own_grads, other_grads = jnp.stack([e[0] for e in ended]), jnp.stack([e[1] for e in ended])
    first = half == 0
    grad_all = jnp.concatenate(
        [jnp.where(first, own_grads, other_grads), jnp.where(first, other_grads, own_grads)]
    )
    grad_gate_up, grad_down = finish_grads(grad_all)
    return (
        mixed[None],
        grad_x.astype(bf16)[None],
        gain_a_sum,
        gain_m_sum,
        qkv_sum,
        out_sum,
        grad_gate_up,
        grad_down,
    )


def solution(mesh):
    placed = (
        P("fsdp", "seq", None),
        P("fsdp", None),
        P("fsdp", "seq", None),
        P("fsdp", "seq", None),
        P("fsdp"),
        P("fsdp"),
        P("fsdp", None),
        P("fsdp", None),
        P("seq", "fsdp", None, None),
        P("seq", None, "fsdp"),
        P("fsdp", "seq", None),
    )
    return jax.shard_map(
        body,
        mesh=mesh,
        in_specs=placed,
        out_specs=(
            P("fsdp", "seq", None),
            P("fsdp", "seq", None),
            P("fsdp"),
            P("fsdp"),
            P("fsdp", None),
            P("fsdp", None),
            P("seq", "fsdp", None, None),
            P("seq", None, "fsdp"),
        ),
        check_vma=False,
    )
```

```python
import jax
import jax.numpy as jnp
from jax import lax
from jax.experimental import pallas as pl
from jax.experimental.pallas import tpu as pltpu
from jax.sharding import PartitionSpec as P

D = 2048
HEADS = 16
HEAD = 128
FFE = 1024
TOP = 8

epsilon = 1e-06
f32 = jnp.float32
bf16 = jnp.bfloat16


def swap(value, axis, bit):
    size = lax.axis_size(axis)
    return lax.ppermute(value, axis, [(i, i ^ bit) for i in range(size)])


def dot(a, b, contract, batch=((), ())):
    return lax.dot_general(a, b, (contract, batch), preferred_element_type=f32)


def segment_ids(length_row, span_len):
    ends = jnp.cumsum(length_row)
    places = lax.iota(jnp.int32, span_len)
    return jnp.sum((places[:, None] >= ends[None, :]).astype(jnp.int32), axis=1)


def score_probs(keys, queries, seg_column, seg_row):
    raw = dot(keys, queries, ((1,), (1,)))
    raw = jnp.where(seg_column == seg_row, raw, -1e30)
    top = jnp.max(raw, axis=0, keepdims=True)
    part = jnp.exp((raw - top) * HEAD ** (-0.5))
    return part * (1.0 / jnp.sum(part, axis=0, keepdims=True))


def head_columns(heads_here, head):
    return [
        pl.ds(pl.multiple_of((third * heads_here + head) * HEAD, HEAD), HEAD) for third in range(3)
    ]


def attend_forward_kernel(heads_here, qkv_ref, seg_column, seg_row, out_ref):
    block = out_ref.shape[0]
    at = pl.ds(pl.multiple_of(pl.program_id(1) * block, block), block)
    q_at, k_at, v_at = head_columns(heads_here, pl.program_id(0))
    probs = score_probs(qkv_ref[:, k_at], qkv_ref[at, q_at], seg_column[...], seg_row[...])
    out_ref[...] = dot(qkv_ref[:, v_at], probs.astype(bf16), ((0,), (0,))).T.astype(bf16)


def attend_backward_kernel(
    heads_here, qkv_ref, grad_ref, seg_column, seg_row, out_ref, grad_k, grad_v
):
    block = grad_ref.shape[0]
    turn = pl.program_id(1)
    at = pl.ds(pl.multiple_of(turn * block, block), block)
    q_at, k_at, v_at = head_columns(heads_here, pl.program_id(0))
    queries, keys, grads = qkv_ref[at, q_at], qkv_ref[:, k_at], grad_ref[...]
    probs = score_probs(keys, queries, seg_column[...], seg_row[...])
    grad_probs = dot(qkv_ref[:, v_at], grads, ((1,), (1,)))
    inner = jnp.sum(probs * grad_probs, axis=0, keepdims=True)
    grad_scores = (probs * (grad_probs - inner)).astype(bf16)
    scale = HEAD ** (-0.5)

    @pl.when(turn == 0)
    def _():
        grad_k[...] = jnp.zeros_like(grad_k)
        grad_v[...] = jnp.zeros_like(grad_v)

    grad_v[...] += dot(probs.astype(bf16), grads, ((1,), (0,)))
    grad_k[...] += dot(grad_scores, queries, ((1,), (0,)))
    out_ref[at, q_at] = (dot(keys, grad_scores, ((0,), (0,))).T * scale).astype(bf16)

    @pl.when(turn == pl.num_programs(1) - 1)
    def _():
        out_ref[:, k_at] = (grad_k[...] * scale).astype(bf16)
        out_ref[:, v_at] = grad_v[...].astype(bf16)


def attend(qkv, segment, grad=None):
    span_len, columns = qkv.shape
    heads_here = columns // (3 * HEAD)
    blocks = 3
    block = span_len // blocks
    whole = pl.BlockSpec((span_len, columns), lambda h, i: (0, 0), pipeline_mode=pl.Buffered(1))
    cut = pl.BlockSpec((block, HEAD), lambda h, i: (i, h))
    segments = [
        pl.BlockSpec((span_len, 1), lambda h, i: (0, 0)),
        pl.BlockSpec((1, block), lambda h, i: (0, i)),
    ]
    backward = grad is not None
    return pl.pallas_call(
        lambda *refs: (attend_backward_kernel if backward else attend_forward_kernel)(
            heads_here, *refs
        ),
        out_shape=jax.ShapeDtypeStruct((span_len, columns if backward else columns // 3), bf16),
        grid=(heads_here, blocks),
        in_specs=[whole, *[cut] * backward, *segments],
        out_specs=pl.BlockSpec((span_len, columns), lambda h, i: (0, 0)) if backward else cut,
        scratch_shapes=[pltpu.VMEM((span_len, HEAD), f32)] * (2 * backward),
        compiler_params=pltpu.CompilerParams(
            dimension_semantics=("arbitrary", "arbitrary"), vmem_limit_bytes=60 * 2**20
        ),
        cost_estimate=pl.CostEstimate(
            flops=(40 if backward else 20) * span_len * span_len * HEAD * heads_here,
            bytes_accessed=4 * span_len * columns,
            transcendentals=span_len * span_len * heads_here,
        ),
        name="attend_backward" if backward else "attend_forward",
    )(*[qkv, *[grad] * backward, segment.reshape(span_len, 1), segment.reshape(1, span_len)])


def finish_kernel(in_ref, gate_ref, down_ref):
    ffe = down_ref.shape[1]
    whole = in_ref[0].astype(f32)
    gate_ref[0, :, 0, :] = whole[:, :ffe]
    gate_ref[0, :, 1, :] = whole[:, ffe : 2 * ffe]
    down_ref[0] = whole[:, 2 * ffe :].T


def finish_grads(packed):
    count, rows, columns = packed.shape
    ffe = columns // 3
    return pl.pallas_call(
        finish_kernel,
        out_shape=[
            jax.ShapeDtypeStruct((count, rows, 2, ffe), f32),
            jax.ShapeDtypeStruct((count, ffe, rows), f32),
        ],
        grid=(count,),
        in_specs=[pl.BlockSpec((1, rows, columns), lambda e: (e, 0, 0))],
        out_specs=[
            pl.BlockSpec((1, rows, 2, ffe), lambda e: (e, 0, 0, 0)),
            pl.BlockSpec((1, ffe, rows), lambda e: (e, 0, 0)),
        ],
        compiler_params=pltpu.CompilerParams(vmem_limit_bytes=60 * 2**20),
        name="finish",
    )(packed)


def unpack_kernel(in_ref, out_ref):
    out_ref[...] = in_ref[0].astype(f32)


def unpack_columns(gathered, width, thirds):
    n_seq, rows, _ = gathered.shape
    return pl.pallas_call(
        unpack_kernel,
        out_shape=jax.ShapeDtypeStruct((rows, thirds * n_seq * width), f32),
        grid=(n_seq, thirds),
        in_specs=[pl.BlockSpec((1, rows, width), lambda s, p: (s, 0, p))],
        out_specs=pl.BlockSpec((rows, width), lambda s, p: (0, p * n_seq + s)),
        name="unpack",
    )(gathered)


def after(value, *others):
    if not others:
        return value
    return lax.optimization_barrier((value, *others))[0]


def reversed_bits(index, size):
    count, total = size.bit_length() - 1, 0
    for bit in range(count):
        total = total + (((index >> bit) & 1) << (count - 1 - bit))
    return total


def start_expert(mine, sent, *start, later=()):
    size = lax.axis_size("fsdp")
    mine, sent = after(mine, *start, *later), after(sent, *start)
    pieces = {size // 2: swap(sent, "fsdp", size // 2)}
    bit = size // 4
    while bit > 1:
        pieces[bit] = swap(mine, "fsdp", bit)
        bit //= 2
    return pieces


def finish_expert(pieces, *start):
    size = lax.axis_size("fsdp")
    pieces, brought = dict(pieces), {}
    for j in sorted(range(2, size, 2), key=lambda j: j.bit_count()):
        if j not in pieces:
            low = j & -j
            pieces[j] = brought[j] = swap(after(pieces[j ^ low], *start), "fsdp", low)
    return brought


def both_cores(pieces, *start):
    size = lax.axis_size("fsdp")
    return lax.all_gather(
        jnp.concatenate([after(piece, *start) for piece in pieces]),
        "fsdp",
        axis=0,
        tiled=True,
        axis_index_groups=[[i, i + 1] for i in range(0, size, 2)],
    )


def send_rows(piece, axis, *start):
    sent = after(piece, *start)
    return [piece, *[swap(sent, axis, k) for k in range(1, lax.axis_size(axis))]]


def join_rows(pieces, axis, *others):
    place, rows = lax.axis_index(axis), pieces[0].shape[0]
    whole = jnp.zeros((len(pieces) * rows, *pieces[0].shape[1:]), pieces[0].dtype)
    for k, piece in enumerate(pieces):
        piece = piece if k else after(piece, *others)
        whole = lax.dynamic_update_slice_in_dim(whole, piece, (place ^ k) * rows, 0)
    return whole


def scatter_rows(sums, axis):
    place, rows = lax.axis_index(axis), sums.shape[0] // lax.axis_size(axis)
    parts = [
        lax.dynamic_slice_in_dim(sums, (place ^ k) * rows, rows, 0)
        for k in range(lax.axis_size(axis))
    ]
    return sum((swap(part, axis, k) if k else part).astype(f32) for k, part in enumerate(parts))


def expert_kernel(size, tiles, parts, place_ref, share_ref, *rest):
    arrays = 1 + max(part[0] for part in parts)
    slots, pieces, rest = rest[:4], rest[4 : 4 + arrays], rest[4 + arrays :]
    made_refs, back_refs, rest = rest[:2], rest[2:4], rest[4:]
    send_ref, keep_ref, weights, x_ref, g_ref, act, grad_proj, sems = rest
    step = pl.program_id(0)
    place = place_ref[0]
    rows = weights.shape[0] // size
    ffe = act.shape[1]
    wide = ffe // tiles
    nn, nt, tn = ((1,), (0,)), ((1,), (1,)), ((0,), (0,))

    @pl.when(step == 0)
    def _():
        copies = [
            pltpu.make_async_copy(
                pieces[parts[j][0]].at[parts[j][1] + parts[j][2] * (1 - (place & 1))],
                weights.at[pl.ds(pl.multiple_of((place ^ j) * rows, rows), rows)],
                sems.at[j],
            )
            for j in range(size)
        ]
        count = slots[0].shape[0]
        for k, slot in enumerate(slots):
            copies.append(
                pltpu.make_async_copy(
                    slot,
                    (x_ref, g_ref)[k // 2].at[pl.ds(k % 2 * count, count)],
                    sems.at[size + k],
                )
            )
        for copy in copies:
            copy.start()
        for copy in copies:
            copy.wait()

    @pl.when(step < tiles)
    def _():
        first = pl.multiple_of(step * wide, wide)
        gate = dot(x_ref[...], weights[:, pl.ds(first, wide)], nn)
        up = dot(x_ref[...], weights[:, pl.ds(pl.multiple_of(ffe + first, wide), wide)], nn)
        grad_act = dot(
            g_ref[...], weights[:, pl.ds(pl.multiple_of(2 * ffe + first, wide), wide)], nn
        )
        sigma = 1.0 / (1.0 + jnp.exp(-gate))
        silu = gate * sigma
        act[:, pl.ds(first, wide)] = (silu * up).astype(bf16)
        grad_proj[:, pl.ds(first, wide)] = (
            grad_act * up * (sigma * (1.0 + gate * (1.0 - sigma)))
        ).astype(bf16)
        grad_proj[:, pl.ds(pl.multiple_of(ffe + first, wide), wide)] = (grad_act * silu).astype(
            bf16
        )

    @pl.when(step >= tiles)
    def _():
        turn = step - tiles
        whose = place ^ reversed_bits((turn + size // 2) % size, size)
        at = pl.ds(pl.multiple_of(whose * rows, rows), rows)
        count = act.shape[0] // 2
        made = (share_ref[...] * dot(act[...], weights[at, 2 * ffe :], nt)).astype(bf16)
        back = dot(grad_proj[...], weights[at, : 2 * ffe], nt).astype(bf16)
        for g in range(2):
            made_refs[g][...] = made[g * count : (g + 1) * count]
            back_refs[g][...] = back[g * count : (g + 1) * count]

        def grads(out_ref):
            out_ref[0, :, : 2 * ffe] = dot(x_ref[:, at], grad_proj[...], tn).astype(bf16)
            out_ref[0, :, 2 * ffe :] = dot(g_ref[:, at], act[...], tn).astype(bf16)

        @pl.when(turn < size // 2)
        def _():
            grads(send_ref)

        @pl.when(turn >= size // 2)
        def _():
            grads(keep_ref)


def run_expert(place, share, slots, grad_slots, pieces, parts):
    size, (_, rows, columns) = len(parts), pieces[0].shape
    count = 2 * slots[0].shape[0]
    ffe = columns // 3
    tiles = 4
    half = size // 2

    def whose(step, place):
        turn = jnp.maximum(step - tiles, 0)
        return 0, place[0] ^ reversed_bits((turn + half) % size, size)

    return pl.pallas_call(
        lambda *refs: expert_kernel(size, tiles, parts, *refs),
        out_shape=[
            *[jax.ShapeDtypeStruct((count // 2, D), bf16)] * 4,
            jax.ShapeDtypeStruct((half, rows, columns), bf16),
            jax.ShapeDtypeStruct((half, rows, columns), bf16),
        ],
        grid_spec=pltpu.PrefetchScalarGridSpec(
            num_scalar_prefetch=1,
            grid=(tiles + size,),
            in_specs=[
                pl.BlockSpec((count, 1), lambda step, place: (0, 0)),
                *[pl.BlockSpec(memory_space=pl.ANY)] * (len(pieces) + 4),
            ],
            out_specs=[
                *[pl.BlockSpec((count // 2, rows), whose)] * 4,
                pl.BlockSpec(
                    (1, rows, columns), lambda t, place: (jnp.clip(t - tiles, 0, half - 1), 0, 0)
                ),
                pl.BlockSpec(
                    (1, rows, columns),
                    lambda t, place: (jnp.clip(t - tiles - half, 0, half - 1), 0, 0),
                ),
            ],
            scratch_shapes=[
                pltpu.VMEM((size * rows, columns), bf16),
                pltpu.VMEM((count, D), bf16),
                pltpu.VMEM((count, D), bf16),
                pltpu.VMEM((count, ffe), bf16),
                pltpu.VMEM((count, 2 * ffe), bf16),
                pltpu.SemaphoreType.DMA((size + 4,)),
            ],
        ),
        compiler_params=pltpu.CompilerParams(
            dimension_semantics=("arbitrary",), vmem_limit_bytes=60 * 2**20
        ),
        cost_estimate=pl.CostEstimate(
            flops=18 * count * D * ffe,
            bytes_accessed=8 * count * D + 4 * size * rows * columns,
            transcendentals=count * ffe,
        ),
        name="expert",
    )(place, share, *slots, *grad_slots, *pieces)


class GradChain:
    def __init__(self, send, keep):
        self.bit, self.size = 1, lax.axis_size("fsdp")
        self.terms, self.send = [keep], send

    def arrive(self):
        if self.bit < self.size:
            self.terms.append(swap(self.send, "fsdp", self.bit))
            self.bit *= 2
        return self.terms[-1]

    def add(self, *others):
        many = self.terms[0].shape[0] // 2
        if many:
            if others:
                count = len(self.terms)
                self.terms = list(lax.optimization_barrier((*self.terms, *others))[:count])
            self.send = sum(t[many:].astype(f32) for t in self.terms).astype(bf16)
            self.terms = [t[:many] for t in self.terms]
        return self.send

    def sums(self):
        self.arrive()
        return self.add()

    def ended(self):
        other = self.terms.pop()[0]
        return sum(t[0].astype(f32) for t in self.terms).astype(bf16), other


def body(
    tokens, lengths, routes, gates, gain_attn, gain_moe, w_qkv, w_out, w_gate_up, w_down, cotangent
):
    n_seq, n_fsdp = lax.axis_size("seq"), lax.axis_size("fsdp")
    at_seq, at_fsdp = lax.axis_index("seq"), lax.axis_index("fsdp")
    rows = tokens.shape[1]
    shard = D // n_fsdp
    local_count = w_gate_up.shape[0]
    per_half = local_count // 2
    half = at_fsdp // (n_fsdp // 2)
    heads_here = HEADS // n_seq
    width = heads_here * HEAD
    span_len = rows * n_seq

    packed = jnp.concatenate(
        [w_gate_up.reshape(local_count, shard, 2 * FFE), jnp.swapaxes(w_down, 1, 2)], axis=2
    )
    own_part = lax.dynamic_slice_in_dim(packed, half * per_half, per_half, 0)
    other_part = lax.dynamic_slice_in_dim(packed, (1 - half) * per_half, per_half, 0)
    cot_other = swap(cotangent[0], "fsdp", n_fsdp // 2)
    x_parts = send_rows(tokens[0], "seq")
    cot_own = join_rows(send_rows(cotangent[0], "seq", *x_parts), "seq")

    part = lax.dynamic_slice_in_dim(
        w_qkv.reshape(shard, 3, HEADS, HEAD), at_seq * heads_here, heads_here, 2
    ).reshape(shard, 3 * width)
    gains = jnp.zeros((shard, 128), bf16).at[:, 0].set(gain_attn).at[:, 1].set(gain_moe)
    gathered = lax.all_gather(
        jnp.concatenate([part, gains], axis=1), "fsdp", axis=0, tiled=True
    )
    qkv_own = gathered[:, : 3 * width]
    gain_a = gathered[:, 3 * width].astype(f32)
    gain_m = gathered[:, 3 * width + 1].astype(f32)

    routing = jnp.concatenate([routes[0].astype(f32), gates[0]], axis=1)
    routing = jnp.stack([routing, swap(routing, "fsdp", n_fsdp // 2)])
    routing = jnp.swapaxes(lax.all_gather(routing, "seq", axis=0, tiled=False), 0, 1)
    routing = routing.reshape(2 * n_seq, rows, 2 * TOP)
    capacity = rows * TOP * 4 // (3 * local_count * n_seq) + 2
    capacity = -(-capacity // 8) * 8
    named = at_seq * local_count + half * per_half + lax.iota(jnp.int32, per_half)
    hits = routing[:, :, :TOP, None].astype(jnp.int32) == named
    mask = jnp.any(hits, axis=2)
    weight = jnp.sum(jnp.where(hits, routing[:, :, TOP:, None], 0.0), axis=2)
    below = (lax.iota(jnp.int32, rows)[:, None] > lax.iota(jnp.int32, rows)[None, :]).astype(bf16)
    rank = jnp.einsum("rq,bqe->bre", below, mask.astype(bf16), preferred_element_type=f32)
    rank = jnp.where(mask, rank.astype(jnp.int32), -1)
    picks = jnp.swapaxes(rank, 1, 2)[:, :, None, :] == lax.iota(jnp.int32, capacity)[:, None]
    share = jnp.sum(
        jnp.where(picks, jnp.swapaxes(weight, 1, 2)[:, :, None, :], 0.0), axis=3
    )
    picks = picks.astype(bf16)

    def normed_rows(values, gain):
        inverse = lax.rsqrt(jnp.mean(values * values, axis=1, keepdims=True) + epsilon)
        return (values * inverse * gain).astype(bf16), inverse

    x_all = join_rows(
        x_parts, "seq", own_part, other_part, picks, share, cot_own, cot_other
    )
    out_full = lax.all_gather(after(w_out, x_all), "fsdp", axis=0, tiled=True)
    normed_a, _ = normed_rows(x_all.astype(f32), gain_a)
    qkv = dot(normed_a, qkv_own, ((1,), (0,))).astype(bf16)
    segment = segment_ids(lengths[0], span_len)
    attended = attend(qkv, segment)
    heads_rows = lax.all_to_all(attended, "seq", split_axis=0, concat_axis=1, tiled=True)
    cot_all = [cot_own, join_rows(send_rows(cot_other, "seq", cot_own), "seq")]
    cot_all = [rows_of.reshape(n_seq, rows, D) for rows_of in cot_all]
    begun = [start_expert(own_part[:1], other_part[:1], attended)]
    heads_rows = after(heads_rows, *cot_all, *begun[0].values())
    experts = [finish_expert(begun[0], heads_rows)]
    x_float = tokens[0].astype(f32)
    resid = x_float + dot(heads_rows, out_full, ((1,), (0,)))
    normed_m, inv_m = normed_rows(resid, gain_m)
    moe_own = lax.all_gather(normed_m, "seq", axis=0, tiled=False)
    moe_other = after(swap(normed_m, "fsdp", n_fsdp // 2), moe_own)
    moe_all = [moe_own, lax.all_gather(moe_other, "seq", axis=0, tiled=False), moe_other]

    place = jnp.full((1,), at_fsdp, jnp.int32)
    forward_parts, backward_parts, chains = [], [], []

    def dispatch(i, g, source, weighted):
        at = slice(g * n_seq, (g + 1) * n_seq)
        part = dot(picks[at, i], source, ((2,), (1,)), ((0,), (0,)))
        if weighted:
            part = part * share[at, i, :, None]
        return part.astype(bf16).reshape(-1, D)

    sets = [[i] for i in range(per_half)]

    def begin(k, *start):
        cut = slice(sets[k][0], sets[k][-1] + 1)
        begun.append(start_expert(own_part[cut], other_part[cut], *start))

    begin(1, moe_all[2])
    begin(2, moe_all[1])
    beside = swap(after(own_part, normed_m), "fsdp", 1)
    near, last = [both_cores(list(begun[0].values()))], {}
    for i in range(per_half):
        k = [n for n, members in enumerate(sets) if i in members][0]
        first, later, many = begun[k], experts[k], len(sets[k])
        back = backward_parts[-1] if i else []
        ready = [near[k], *later.values(), *back]
        if k not in last:
            last[k] = swap(
                jnp.concatenate([after(p, *back[:1]) for p in later.values()]), "fsdp", 1
            )
        if i + 1 < per_half:
            ready.extend(begun[i + 1].values())
        cots = [after(cot_all[g], *back) for g in range(2)]
        for chain in chains[max(i - 3, 0) : max(i - 1, 0)]:
            ready.append(chain.arrive())
        if i == 0:
            ready = [dispatch(i, g, cots[g], True) for g in range(2)]
        slots = [dispatch(i, g, after(moe_all[g], *ready), False) for g in range(2)]
        ready = [chain.add(back[0]) for chain in chains[max(i - 3, 0) : max(i - 1, 0)]]
        slots[1] = after(slots[1], *ready)
        grad_slots = [dispatch(i, g, cots[g], True) for g in range(2)]
        if i + 1 < per_half:
            experts.append(finish_expert(begun[i + 1], slots[1]))
            near.append(both_cores(list(begun[i + 1].values()), slots[1]))
        even = [*first, *later]
        pieces = [own_part, beside, near[k], last[k], *first.values(), *later.values()]
        at = i - sets[k][0]
        parts = {0: (0, i, 0), 1: (1, i, 0)}
        for n, j in enumerate(even):
            parts[j] = (4 + n, at, 0)
            if j in first:
                parts[j + 1] = (2, n * many + at, len(first) * many)
            else:
                parts[j + 1] = (3, (n - len(first)) * many + at, 0)
        parts = [parts[j] for j in range(n_fsdp)]
        *made, send, keep = run_expert(
            place, share[:, i].reshape(-1, 1), slots, grad_slots, pieces, parts
        )
        forward_parts.append([part.reshape(n_seq, capacity, D) for part in made[:2]])
        backward_parts.append([part.reshape(n_seq, capacity, D) for part in made[2:]])
        chains.append(GradChain(send, keep))
        if i + 3 < per_half:
            begin(i + 3, made[2])

    every_pick = picks.reshape(2, n_seq, per_half * capacity, rows)

    def combine(parts, g, *others):
        together = jnp.concatenate([part[g] for part in parts], axis=1)
        if others:
            together = after(together, *others)
        total = dot(every_pick[g], together, ((1,), (1,)), ((0,), (0,)))
        return total.astype(bf16).reshape(span_len, D)

    def scatter(sums, *others):
        return lax.psum_scatter(after(sums, *others), "seq", scatter_dimension=0, tiled=True)

    back_other = combine(backward_parts, 1, *[chain.arrive() for chain in chains[:-2]])
    back_own = combine(backward_parts, 0, back_other)
    swapped_back = scatter(back_other)
    ready = [chain.arrive() for chain in chains[-2:]]
    ready.extend(chain.add(back_own) for chain in chains[-3:])
    ready.append(chains[-3].arrive())
    grad_normed_m = scatter(back_own, swapped_back, *ready)
    swapped_back = swap(swapped_back, "fsdp", n_fsdp // 2)
    ready = [swapped_back, chains[-2].arrive()]
    made_other = combine(forward_parts, 1, back_own)
    made_own = combine(forward_parts, 0, made_other, *ready)
    mixed_other = scatter(made_other, grad_normed_m, made_own)
    ready = [made_own]
    grad_normed_m = after(grad_normed_m, *ready).astype(f32) + swapped_back.astype(f32)

    scaled_m = grad_normed_m * gain_m
    grad_resid = (
        cotangent[0].astype(f32)
        + inv_m * scaled_m
        - inv_m * inv_m * inv_m * resid * jnp.mean(scaled_m * resid, axis=1, keepdims=True)
    )
    grad_gain_m = jnp.sum(grad_normed_m * resid * inv_m, axis=0)
    grad_attn = grad_resid.astype(bf16)
    grad_heads_rows = dot(grad_attn, out_full, ((1,), (1,))).astype(bf16)
    mixed_own = scatter(made_own, grad_heads_rows)
    grad_heads = lax.all_to_all(
        grad_heads_rows, "seq", split_axis=1, concat_axis=0, tiled=True
    )
    chains[-2].add(grad_heads_rows)
    out_sum = []
    for k in range(n_seq):
        columns = lax.dynamic_slice_in_dim(grad_attn, (at_seq ^ k) * width, width, 1)
        part = dot(heads_rows, columns, ((0,), (0,))).astype(bf16)
        out_sum.append(part)
    grad_qkv = attend(qkv, segment, grad_heads)
    ready = [chain.arrive() for chain in chains[-2:]]
    grad_qkv = after(grad_qkv, mixed_other, *ready)
    mixed_other = swap(after(mixed_other, grad_qkv), "fsdp", n_fsdp // 2)
    mixed = (resid + mixed_own.astype(f32) + mixed_other.astype(f32)).astype(bf16)

    grad_qkv_w = dot(normed_a, grad_qkv, ((0,), (0,))).astype(bf16)
    reduced_qkv = after(grad_qkv_w, mixed_own)
    reduced_qkv = lax.psum_scatter(reduced_qkv, "fsdp", scatter_dimension=0, tiled=True)
    part_normed_a = dot(after(grad_qkv, grad_qkv_w), qkv_own, ((1,), (1,)))
    part_sent = part_normed_a.astype(bf16)
    ready = [part_sent, chains[-1].add(grad_qkv_w)]
    out_sum = [swap(after(p, grad_qkv_w), "seq", k) if k else p for k, p in enumerate(out_sum)]
    qkv_sum = after(reduced_qkv, mixed_other, *ready, *out_sum[1:], chains[-1].arrive())
    qkv_sum = lax.all_gather(qkv_sum, "seq", axis=0, tiled=False)
    grad_normed_a = scatter_rows(after(part_sent, qkv_sum), "seq")
    out_sum[0] = after(out_sum[0], qkv_sum)
    out_sum = sum(part.astype(f32) for part in out_sum).astype(bf16)
    gain_column = jnp.zeros((D, 128), bf16).at[:, 0].set(grad_gain_m.astype(bf16))
    out_sum = jnp.concatenate([out_sum, gain_column], axis=1)
    out_sum = lax.psum_scatter(out_sum, "fsdp", scatter_dimension=0, tiled=True)
    out_sum = lax.all_gather(out_sum, "seq", axis=0, tiled=False)
    qkv_sum = unpack_columns(qkv_sum, width, 3)
    gain_m_sum = jnp.sum(out_sum[:, :, width].astype(f32), axis=0)
    out_sum = unpack_columns(out_sum, width, 1)
    gain_a_sum = jnp.sum(w_qkv.astype(f32) * qkv_sum, axis=1) / gain_attn.astype(f32)
    inv_a = lax.rsqrt(jnp.mean(x_float * x_float, axis=1, keepdims=True) + epsilon)
    scaled_a = grad_normed_a * gain_a
    grad_x = (
        grad_resid
        + inv_a * scaled_a
        - inv_a * inv_a * inv_a * x_float * jnp.mean(scaled_a * x_float, axis=1, keepdims=True)
    )

    for chain in chains:
        while chain.bit < n_fsdp:
            chain.sums()
    ended = [chain.ended() for chain in chains]
    own_grads, other_grads = jnp.stack([e[0] for e in ended]), jnp.stack([e[1] for e in ended])
    first = half == 0
    grad_all = jnp.concatenate(
        [jnp.where(first, own_grads, other_grads), jnp.where(first, other_grads, own_grads)]
    )
    grad_gate_up, grad_down = finish_grads(grad_all)
    return (
        mixed[None],
        grad_x.astype(bf16)[None],
        gain_a_sum,
        gain_m_sum,
        qkv_sum,
        out_sum,
        grad_gate_up,
        grad_down,
    )


def solution(mesh):
    placed = (
        P("fsdp", "seq", None),
        P("fsdp", None),
        P("fsdp", "seq", None),
        P("fsdp", "seq", None),
        P("fsdp"),
        P("fsdp"),
        P("fsdp", None),
        P("fsdp", None),
        P("seq", "fsdp", None, None),
        P("seq", None, "fsdp"),
        P("fsdp", "seq", None),
    )
    return jax.shard_map(
        body,
        mesh=mesh,
        in_specs=placed,
        out_specs=(
            P("fsdp", "seq", None),
            P("fsdp", "seq", None),
            P("fsdp"),
            P("fsdp"),
            P("fsdp", None),
            P("fsdp", None),
            P("seq", "fsdp", None, None),
            P("seq", None, "fsdp"),
        ),
        check_vma=False,
    )
```
